32 devices in a mesh: band: 16 (over z, y, x), sub: 2 (over core).
Axes of the slice: x: 2, y: 2, z: 4, core: 2. Of those that a mesh axis runs over, the one named last changes fastest.
Arguments:
- node_state: bfloat16 [16384, 512], P(('band', 'sub')), may hold values from -6 to 6
- edge_state: bfloat16 [262144, 512], P(('band', 'sub')), may hold values from -6 to 6
- send_rows: int32 [32, 32, 8], P(('band', 'sub')), may hold values from 0 to 511, as said below
- edge_sender: int32 [262144], P(('band', 'sub')), may hold values from 0 to 255, as said below
- edge_receiver: int32 [262144], P(('band', 'sub')), may hold values from 0 to 511
- edge_count: int32 [32], P(('band', 'sub')), may hold values from 1 to 8192, 163840 in all
- edge_w1: bfloat16 [1536, 512], P(('band', 'sub')), may hold values from -0.15625 to 0.15625
- edge_b1: bfloat16 [512], P(('band', 'sub')), may hold values from -3 to 3
- edge_w2: bfloat16 [512, 512], P(('band', 'sub')), may hold values from -0.25 to 0.25
- edge_gain: bfloat16 [512], P(('band', 'sub')), may hold values from 0.099609375 to 1.8984375
- edge_shift: bfloat16 [512], P(('band', 'sub')), may hold values from -2 to 2
- node_w1: bfloat16 [1024, 512], P(('band', 'sub')), may hold values from -0.1875 to 0.1875
- node_b1: bfloat16 [512], P(('band', 'sub')), may hold values from -3 to 3
- node_w2: bfloat16 [512, 512], P(('band', 'sub')), may hold values from -0.25 to 0.25
- node_gain: bfloat16 [512], P(('band', 'sub')), may hold values from 0.099609375 to 1.8984375
- node_shift: bfloat16 [512], P(('band', 'sub')), may hold values from -2 to 2
- node_cot: bfloat16 [16384, 512], P(('band', 'sub')), may hold values from -6 to 6
- edge_cot: bfloat16 [262144, 512], P(('band', 'sub')), may hold values from -6 to 6
Outputs:
- node_out: bfloat16 [16384, 512], P(('band', 'sub'))
- edge_out: bfloat16 [262144, 512], P(('band', 'sub'))
- node_grad: float32 [16384, 512], P(('band', 'sub'))
- edge_grad: float32 [262144, 512], P(('band', 'sub'))
- grad_edge_w1: float32 [1536, 512], P(('band', 'sub'))
- grad_edge_b1: float32 [512], P(('band', 'sub'))
- grad_edge_w2: float32 [512, 512], P(('band', 'sub'))
- grad_edge_gain: float32 [512], P(('band', 'sub'))
- grad_edge_shift: float32 [512], P(('band', 'sub'))
- grad_node_w1: float32 [1024, 512], P(('band', 'sub'))
- grad_node_b1: float32 [512], P(('band', 'sub'))
- grad_node_w2: float32 [512, 512], P(('band', 'sub'))
- grad_node_gain: float32 [512], P(('band', 'sub'))
- grad_node_shift: float32 [512], P(('band', 'sub'))
The draws below stay inside these ranges and needn't reach their ends.
Inputs may be any that keep to these rules, and one draw needn't show every extreme that they name: `send_rows`: each pair of devices (q, r) has a count of live slots, at most 8, exactly 8 where q and r lie in the same or adjacent bands, often none for distant bands; slots at or past the count are padding and hold 0. `edge_sender`: every edge reads a live slot of its pair. `edge_count`: edge slots of a device at or past its count are padding.
All inputs are finite; a program needn't handle non-finite values.
Results may differ from the reference program's by a relative error of at most 0.0076.
Values may be sent and summed in bfloat16 or wider, within the bound.
A program may use at most 192 MiB of HBM per device.

```python
import math
import jax
import jax.numpy as jnp
import numpy as np
from jax import lax

D = 512
NODE_DEV = 512
EDGE_CAP = 8192
SLOT = 8
NODES = 16384
EDGES = 262144
N_SUB = 2
DEVICES = 32


def pair_counts(key):
    key = jax.random.fold_in(key, 11)
    device_ids = jnp.arange(DEVICES, dtype=jnp.int32)
    band_ids = device_ids // N_SUB
    distance = jnp.abs(band_ids[:, None] - band_ids[None, :])
    middle = SLOT // 2 + jax.random.randint(jax.random.fold_in(key, 1), (DEVICES, DEVICES), 0, SLOT - SLOT // 2 + 1)
    far_part = jnp.minimum(jax.random.randint(jax.random.fold_in(key, 2), (DEVICES, DEVICES), 0, 3), SLOT)
    counts = jnp.where(distance <= 1, SLOT, jnp.where(distance == 2, middle, far_part))
    return counts.astype(jnp.int32)


def draw_send_rows(key, part):
    counts = pair_counts(key)
    key = jax.random.fold_in(key, 3)
    picked = jax.random.randint(key, (DEVICES, DEVICES, SLOT), 0, NODE_DEV)
    slots = jnp.arange(SLOT, dtype=jnp.int32)
    alive = slots[None, None, :] < counts[:, :, None]
    return jnp.where(alive, picked, 0).astype(jnp.int32)


def draw_edge_sender(key, part):
    counts = pair_counts(key)
    key = jax.random.fold_in(key, 5)
    incoming = counts.T
    totals = jnp.sum(incoming, axis=1)
    picks = jax.random.randint(key, (DEVICES, EDGE_CAP), 0, totals[:, None])
    picks = picks.at[0, 0].set(0)
    picks = picks.at[DEVICES - 1, 0].set(totals[DEVICES - 1] - 1)
    running = jnp.cumsum(incoming, axis=1)
    source = jax.vmap(lambda row, values: jnp.searchsorted(row, values, side='right'))(running, picks).astype(jnp.int32)
    before = jnp.take_along_axis(running, source, axis=1) - jnp.take_along_axis(incoming, source, axis=1)
    slot_index = picks - before
    return (source * SLOT + slot_index).reshape(EDGES).astype(jnp.int32)


def plant(drawn, key, low, high):
    spot = [jax.random.randint(jax.random.fold_in(key, axis), (), 0, length) for axis, length in enumerate(drawn.shape)]
    longest = drawn.shape.index(max(drawn.shape))
    next_to = spot[:longest] + [(spot[longest] + 1) % drawn.shape[longest]] + spot[longest + 1:]
    return drawn.at[tuple(spot)].set(low).at[tuple(next_to)].set(high)


def block_scale(stream_key, extent, cuts, least, top_value):
    loudness = 1.0
    for dim, parts in cuts:
        draws = jax.random.uniform(jax.random.fold_in(jax.random.fold_in(stream_key, 6), dim), (parts,), jnp.float32, least / len(cuts), top_value / len(cuts))
        loudness = loudness * jnp.repeat(jnp.exp(draws), extent[dim] // parts).reshape((-1,) + (1,) * (len(extent) - 1 - dim))
    return loudness


def length_profile(number_of, total, most, skew):
    loads = [(1 << 20) // math.isqrt(grade ** skew) + 1 for grade in range(2, number_of + 1)]
    rest, given = total - most - (number_of - 1), [1] * (number_of - 1)
    while rest > 0:
        candidates = [i for i in range(number_of - 1) if given[i] < most]
        mass, left = sum([loads[i] for i in candidates]), rest
        for i in candidates:
            more = min(most - given[i], max(1, left * loads[i] // mass), rest)
            given[i] = given[i] + more
            rest = rest - more
    return np.array([most] + given)


def uneven(stream_key, count, total, limit, skew):
    if count == 2:
        one = jax.random.randint(stream_key, (), max(1, total - limit), min(limit, total - 1) + 1)
        return jnp.stack([one, total - one])
    lengths = jnp.asarray(length_profile(count, total, limit, skew), jnp.int32)
    couples = (count - 1) // 2
    donor, sink = lengths[1:1 + 2 * couples:2], lengths[2:2 + 2 * couples:2]
    margin = jnp.minimum(donor - 1, limit - sink)
    shifted = jax.random.randint(jax.random.fold_in(stream_key, 1), (couples,), 0, 1 << 20) % (margin + 1)
    lengths = lengths.at[1:1 + 2 * couples:2].set(donor - shifted).at[2:2 + 2 * couples:2].set(sink + shifted)
    return lengths[jax.random.permutation(jax.random.fold_in(stream_key, 2), count)]


def bell_draw(key, shape, deviation, bound, cuts=(), kind=jnp.bfloat16):
    result = deviation * jax.random.normal(key, shape, jnp.float32)
    if cuts:
        result = result * block_scale(key, shape, cuts, -0.22, 0.18)
    return jnp.clip(result, -bound, bound).astype(kind)


def setup_inputs(seed: int = 0) -> dict:
    seeds = jax.random.split(jax.random.key(seed), 19)
    node_state = bell_draw(seeds[0], (NODES, D), 1.0, 6.0, ((0, 32),))
    edge_state = bell_draw(seeds[1], (EDGES, D), 1.0, 6.0, ((0, 32),))
    send_rows = draw_send_rows(jax.random.fold_in(seeds[18], 71), 0)
    edge_sender = draw_edge_sender(jax.random.fold_in(seeds[18], 71), 0)
    edge_receiver = plant(jax.random.randint(seeds[4], (EDGES,), 0, NODE_DEV), jax.random.fold_in(seeds[4], 1), 0, NODE_DEV - 1).astype(jnp.int32)
    edge_count = uneven(seeds[5], DEVICES, EDGES * 5 // 8, EDGE_CAP, 2).astype(jnp.int32)
    edge_w1 = bell_draw(seeds[6], (3 * D, D), (3 * D) ** -0.5, 0.15625, ((0, 32),))
    edge_b1 = bell_draw(seeds[7], (D,), 0.5, 3.0, ((0, 32),))
    edge_w2 = bell_draw(seeds[8], (D, D), D ** -0.5, 0.25, ((0, 32),))
    edge_gain = jnp.clip(1.0 + 0.18 * jax.random.normal(seeds[9], (D,), jnp.float32), 0.099609375, 1.8984375).astype(jnp.bfloat16)
    edge_shift = bell_draw(seeds[10], (D,), 0.3, 2.0, ((0, 32),))
    node_w1 = bell_draw(seeds[11], (2 * D, D), (2 * D) ** -0.5, 0.1875, ((0, 32),))
    node_b1 = bell_draw(seeds[12], (D,), 0.5, 3.0, ((0, 32),))
    node_w2 = bell_draw(seeds[13], (D, D), D ** -0.5, 0.25, ((0, 32),))
    node_gain = jnp.clip(1.0 + 0.18 * jax.random.normal(seeds[14], (D,), jnp.float32), 0.099609375, 1.8984375).astype(jnp.bfloat16)
    node_shift = bell_draw(seeds[15], (D,), 0.3, 2.0, ((0, 32),))
    node_cot = bell_draw(seeds[16], (NODES, D), 1.0, 6.0, ((0, 32),))
    edge_cot = bell_draw(seeds[17], (EDGES, D), 1.0, 6.0, ((0, 32),))
    return {"node_state": node_state, "edge_state": edge_state, "send_rows": send_rows, "edge_sender": edge_sender, "edge_receiver": edge_receiver, "edge_count": edge_count, "edge_w1": edge_w1, "edge_b1": edge_b1, "edge_w2": edge_w2, "edge_gain": edge_gain, "edge_shift": edge_shift, "node_w1": node_w1, "node_b1": node_b1, "node_w2": node_w2, "node_gain": node_gain, "node_shift": node_shift, "node_cot": node_cot, "edge_cot": edge_cot}


@jax.custom_vjp
def low(v):
    return lax.optimization_barrier(v.astype(jnp.bfloat16)).astype(jnp.float32)

@jax.custom_vjp
def low_back(v):
    return v

def low_keep(v):
    return (low(v), None)

def low_pass(kept, grad):
    return (grad,)

def back_keep(v):
    return (v, None)

def back_low(kept, grad):
    return (low(grad),)
low.defvjp(low_keep, low_pass)
low_back.defvjp(back_keep, back_low)
EPSILON = 1e-05

def layer_norm(values):
    center = values - lax.optimization_barrier(jnp.mean(values, axis=1, keepdims=True))
    variance = lax.optimization_barrier(jnp.mean(center * center, axis=1, keepdims=True))
    return center * lax.rsqrt(variance + EPSILON)

def matmul(left, right):
    return jnp.dot(left, right, precision=lax.Precision.HIGHEST)

def reference(node_state, edge_state, send_rows, edge_sender, edge_receiver, edge_count, edge_w1, edge_b1, edge_w2, edge_gain, edge_shift, node_w1, node_b1, node_w2, node_gain, node_shift, node_cot, edge_cot):
    flt = jnp.float32
    positions = jnp.arange(EDGES, dtype=jnp.int32)
    owner = positions // EDGE_CAP
    local_slot = positions - owner * EDGE_CAP
    live = (local_slot < edge_count[owner]).astype(flt)
    source = edge_sender // SLOT
    slot_index = edge_sender - source * SLOT
    sender_node = (source * NODE_DEV + send_rows[source, owner, slot_index]).astype(jnp.int32)

    def forward(nodes_f, edges_f, ew1, eb1, ew2, egain, eshift, nw1, nb1, nw2, ngain, nshift):

        def per_device(items):
            own, senders, receivers, alive, local_nodes = items
            joined = jnp.concatenate([own, nodes_f[senders], local_nodes[receivers]], axis=1)
            preact = low_back(matmul(joined, ew1) + eb1)
            hidden = low(jax.nn.silu(preact))
            projected = low_back(matmul(hidden, ew2))
            message = alive[:, None] * (layer_norm(projected) * egain + eshift)
            gathered_dev = jax.ops.segment_sum(message, receivers, num_segments=NODE_DEV)
            return (own + message, gathered_dev)
        edge_new, gathered = lax.map(jax.checkpoint(per_device), (edges_f.reshape(DEVICES, EDGE_CAP, D), sender_node.reshape(DEVICES, EDGE_CAP), edge_receiver.reshape(DEVICES, EDGE_CAP), live.reshape(DEVICES, EDGE_CAP), nodes_f.reshape(DEVICES, NODE_DEV, D)))
        gathered = gathered.reshape(NODES, D)
        node_joined = jnp.concatenate([nodes_f, low(gathered)], axis=1)
        node_pre = low_back(matmul(node_joined, nw1) + nb1)
        node_hidden = low(jax.nn.silu(node_pre))
        node_proj = low_back(matmul(node_hidden, nw2))
        node_new = nodes_f + layer_norm(node_proj) * ngain + nshift
        return (node_new, edge_new.reshape(EDGES, D))
    primals = [arr.astype(flt) for arr in (node_state, edge_state, edge_w1, edge_b1, edge_w2, edge_gain, edge_shift, node_w1, node_b1, node_w2, node_gain, node_shift)]
    (node_new, edge_new), pullback = jax.vjp(forward, *primals)
    grads = pullback((node_cot.astype(flt), edge_cot.astype(flt)))
    return (node_new.astype(jnp.bfloat16), edge_new.astype(jnp.bfloat16), grads[0], grads[1], grads[2], grads[3], grads[4], grads[5], grads[6], grads[7], grads[8], grads[9], grads[10], grads[11])
```

```python
import functools
import jax, jax.numpy as jnp
from jax import lax
from jax.experimental import pallas as pl
from jax.experimental.pallas import tpu as pltpu
from jax.sharding import PartitionSpec as P

EPS = 1e-5
F32 = jnp.float32
BF = jnp.bfloat16

def dot(a, b):
    return jnp.dot(a, b, preferred_element_type=F32)

def dot_t(a, b):
    return lax.dot_general(a, b, (((1,), (1,)), ((), ())), preferred_element_type=F32)

def t_dot(a, b):
    return lax.dot_general(a, b, (((0,), (0,)), ((), ())), preferred_element_type=F32)

def rowmean(v):
    return jnp.sum(v, axis=1, keepdims=True) * (1.0 / v.shape[1])

def norm(v):
    c = v - rowmean(v)
    s = lax.rsqrt(rowmean(c * c) + EPS)
    return c * s, s

def kernel(nb, R, count_ref, sid_ref, rid_ref, e_ref, cot_ref, snd_ref, node_ref, ncot_ref,
           w1_ref, w2_ref, nw1_ref, nw2_ref, vec_ref,
           nout_ref, eout_ref, ngrad_ref, egrad_ref, gw1_ref, gw2_ref, gnw1_ref, gnw2_ref, gvec_ref, sgrad_ref,
           wcat, w2h, hid_s, slope_s, nrm_s, scale_s, gath, dg, gacc, gain_acc, shift_acc):
    i = pl.program_id(0)
    D = e_ref.shape[1]
    S = snd_ref.shape[0]
    N = node_ref.shape[0]
    count = count_ref[0]
    b1 = vec_ref[0:1, :].astype(F32)
    gain = vec_ref[1:2, :].astype(F32)
    shift = vec_ref[2:3, :].astype(F32)

    @pl.when(i == 0)
    def _():
        wcat[0:D, :] = w1_ref[0:D, :] * 0.5
        wcat[D:D + S, :] = (dot(snd_ref[...], w1_ref[D:2 * D, :]) * 0.5).astype(BF)
        wcat[D + S:, :] = ((dot(node_ref[...], w1_ref[2 * D:, :]) + b1) * 0.5).astype(BF)
        w2h[...] = w2_ref[...] * 0.5
        gath[...] = jnp.zeros_like(gath)
        gacc[...] = jnp.zeros_like(gacc)
        gw2_ref[...] = jnp.zeros_like(gw2_ref)
        gain_acc[...] = jnp.zeros_like(gain_acc)
        shift_acc[...] = jnp.zeros_like(shift_acc)

    blk = lax.rem(i, nb)
    first = blk * R
    rows = pl.ds(pl.multiple_of(first, R), R)
    live_blk = first < count

    def onehot_cols(ids_row, width):
        ids = jnp.broadcast_to(ids_row, (128, R)).T
        lane = lax.broadcasted_iota(jnp.int32, (R, 128), 1)
        d = ids - lane
        parts = [jnp.where(d == 128 * j, 1.0, 0.0).astype(BF) for j in range(width // 128)]
        return jnp.concatenate(parts, axis=1)

    def onehot_rows(ids_row, height):
        sub = lax.broadcasted_iota(jnp.int32, (height, R), 0)
        return jnp.where(sub == ids_row, 1.0, 0.0).astype(BF)

    def ids():
        pos = first + lax.broadcasted_iota(jnp.int32, (1, R), 1)
        sid = sid_ref[pl.ds(blk, 1), :]
        rid = jnp.where(pos < count, rid_ref[pl.ds(blk, 1), :], -1)
        return sid, rid

    def live_col():
        return first + lax.broadcasted_iota(jnp.int32, (R, 1), 0) < count

    @pl.when((i < nb) & live_blk)
    def _():
        sid, rid = ids()
        x = jnp.concatenate([e_ref[...], onehot_cols(sid, S), onehot_cols(rid, N)], axis=1)
        h = dot(x, wcat[...])
        a = 1.0 + jnp.tanh(h)
        hid = h * a
        slope = a * (1.0 + 2.0 * h - hid)
        hid = hid.astype(BF)
        hid_s[rows, :] = hid
        slope_s[rows, :] = slope.astype(BF)
        proj = dot(hid, w2_ref[...])
        live = live_col()
        c = proj - rowmean(proj)
        s = lax.rsqrt(rowmean(c * c) + EPS)
        s = jnp.where(live, s, 0.0)
        scale_s[rows, :] = jnp.broadcast_to(s, (R, 128))
        nrm = c * s
        nrm_s[rows, :] = nrm.astype(BF)
        msg = nrm * gain + shift
        eout_ref[...] = (e_ref[...].astype(F32) + jnp.where(live, msg, 0.0)).astype(BF)
        gath[...] += dot(onehot_rows(rid, N), msg.astype(BF))

    @pl.when((i < nb) & jnp.logical_not(live_blk))
    def _():
        eout_ref[...] = e_ref[...]

    @pl.when(i == nb - 1)
    def _():
        nb1 = vec_ref[3:4, :].astype(F32)
        ngain = vec_ref[4:5, :].astype(F32)
        nshift = vec_ref[5:6, :].astype(F32)
        node = node_ref[...]
        g16 = gath[...].astype(BF)
        pre = dot(node, nw1_ref[0:D, :]) + dot(g16, nw1_ref[D:, :]) + nb1
        sig = 0.5 + 0.5 * jnp.tanh(0.5 * pre)
        hid = (pre * sig).astype(BF)
        proj = dot(hid, nw2_ref[...])
        nrm, s = norm(proj)
        nout_ref[...] = (node.astype(F32) + nrm * ngain + nshift).astype(BF)
        up = ncot_ref[...].astype(F32)
        gvec_ref[4:5, :] = jnp.sum(up * nrm, axis=0, keepdims=True)
        gvec_ref[5:6, :] = jnp.sum(up, axis=0, keepdims=True)
        g = up * ngain
        dproj = (s * (g - rowmean(g) - nrm * rowmean(g * nrm))).astype(BF)
        gnw2_ref[...] = t_dot(hid, dproj)
        dpre = dot_t(dproj, nw2_ref[...]) * (sig * (1.0 + pre * (1.0 - sig)))
        dpre16 = dpre.astype(BF)
        gnw1_ref[0:D, :] = t_dot(node, dpre16)
        gnw1_ref[D:, :] = t_dot(g16, dpre16)
        gvec_ref[3:4, :] = jnp.sum(dpre16.astype(F32), axis=0, keepdims=True)
        ngrad_ref[...] = up + dot_t(dpre16, nw1_ref[0:D, :])
        dg[...] = dot_t(dpre16, nw1_ref[D:, :]).astype(BF)

    @pl.when((i >= nb) & live_blk)
    def _():
        sid, rid = ids()
        live = live_col()
        cot = cot_ref[...].astype(F32)
        dm = jnp.where(live, cot, 0.0) + dot(onehot_cols(rid, N), dg[...])
        nrm = nrm_s[rows, :].astype(F32)
        p = dm * nrm
        gain_acc[...] += jnp.sum(p.reshape(R // 8, 8, D), axis=0)
        shift_acc[...] += jnp.sum(dm.reshape(R // 8, 8, D), axis=0)
        g = dm * gain
        m1 = rowmean(g)
        m2 = rowmean(p * gain)
        s = scale_s[rows, 0:1]
        dproj = (s * (g - m1 - nrm * m2)).astype(BF)
        gw2_ref[...] += t_dot(hid_s[rows, :], dproj)
        dpre = (dot_t(dproj, w2h[...]) * slope_s[rows, :].astype(F32)).astype(BF)
        gacc[0:D, :] += t_dot(e_ref[...], dpre)
        gacc[D:D + S, :] += dot(onehot_rows(sid, S), dpre)
        gacc[D + S:, :] += dot(onehot_rows(rid, N), dpre)
        egrad_ref[...] = cot + dot_t(dpre, w1_ref[0:D, :])

    @pl.when((i >= nb) & jnp.logical_not(live_blk))
    def _():
        egrad_ref[...] = cot_ref[...].astype(F32)

    @pl.when(i == 2 * nb - 1)
    def _():
        gvec_ref[1:2, :] = jnp.sum(gain_acc[...], axis=0, keepdims=True)
        gvec_ref[2:3, :] = jnp.sum(shift_acc[...], axis=0, keepdims=True)
        gvec_ref[0:1, :] = jnp.sum(gacc[D + S:, :], axis=0, keepdims=True)
        gvec_ref[6:8, :] = jnp.zeros((2, D), F32)
        us = gacc[D:D + S, :].astype(BF)
        ur = gacc[D + S:, :].astype(BF)
        gw1_ref[0:D, :] = gacc[0:D, :]
        gw1_ref[D:2 * D, :] = t_dot(snd_ref[...], us)
        gw1_ref[2 * D:, :] = t_dot(node_ref[...], ur)
        sgrad_ref[...] = dot_t(us, w1_ref[D:2 * D, :]).astype(BF)
        ngrad_ref[...] += dot_t(ur, w1_ref[2 * D:, :])


def core(count, sid, rid, e, cot, snd, node, ncot, w1, w2, nw1, nw2, vec, R=512):
    E, D = e.shape
    nb = E // R
    S, N = snd.shape[0], node.shape[0]
    V = pl.BlockSpec(memory_space=pltpu.VMEM)
    fb = pl.BlockSpec((R, D), lambda i: (jnp.minimum(i, nb - 1), 0))
    bb = pl.BlockSpec((R, D), lambda i: (jnp.maximum(i - nb, 0), 0))
    both = pl.BlockSpec((R, D), lambda i: (lax.rem(i, nb), 0))
    sds = jax.ShapeDtypeStruct
    return pl.pallas_call(
        functools.partial(kernel, nb, R),
        grid=(2 * nb,),
        in_specs=[pl.BlockSpec(memory_space=pltpu.SMEM), V, V, both, bb, V, V, V, V, V, V, V, V],
        out_specs=[V, fb, V, bb, V, V, V, V, V, V],
        out_shape=[sds((N, D), BF), sds((E, D), BF), sds((N, D), F32), sds((E, D), F32),
                   sds((3 * D, D), F32), sds((D, D), F32), sds((2 * D, D), F32), sds((D, D), F32),
                   sds((8, D), F32), sds((S, D), BF)],
        scratch_shapes=[pltpu.VMEM((D + S + N, D), BF), pltpu.VMEM((D, D), BF),
                        pltpu.VMEM((E, D), BF), pltpu.VMEM((E, D), BF), pltpu.VMEM((E, D), BF),
                        pltpu.VMEM((E, 128), F32), pltpu.VMEM((N, D), F32), pltpu.VMEM((N, D), BF),
                        pltpu.VMEM((D + S + N, D), F32), pltpu.VMEM((8, D), F32), pltpu.VMEM((8, D), F32)],
        compiler_params=pltpu.CompilerParams(vmem_limit_bytes=63 * 1024 * 1024, dimension_semantics=("arbitrary",)),
        name="edge_node_core",
    )(count, sid.reshape(nb, R), rid.reshape(nb, R), e, cot, snd, node, ncot, w1, w2, nw1, nw2, vec)


AXES = ("band", "sub")


def local(node_state, edge_state, send_rows, edge_sender, edge_receiver, edge_count, edge_w1, edge_b1, edge_w2,
          edge_gain, edge_shift, node_w1, node_b1, node_w2, node_gain, node_shift, node_cot, edge_cot):
    D = node_state.shape[1]
    N = node_state.shape[0]
    peers, slots = send_rows.shape[1:]
    mats = (edge_w1, edge_w2, node_w1, node_w2)
    vecs = (edge_b1, edge_gain, edge_shift, node_b1, node_gain, node_shift)
    part = vecs[0].shape[0]
    w1, w2, nw1, nw2 = (lax.all_gather(m, AXES, axis=0, tiled=True) for m in mats)
    vec = lax.all_gather(jnp.stack(vecs), AXES, axis=1, tiled=True)
    vec = jnp.concatenate([vec, jnp.zeros((2, D), BF)], axis=0)
    selected = send_rows[0].reshape(peers * slots)
    outgoing = jnp.take(node_state, selected, axis=0).reshape(peers, slots, D)
    senders = lax.all_to_all(outgoing, AXES, split_axis=0, concat_axis=0, tiled=True).reshape(peers * slots, D)
    node_out, edge_out, node_grad, edge_grad, gw1, gw2, gnw1, gnw2, gvec, sgrad = core(
        edge_count, edge_sender, edge_receiver, edge_state, edge_cot, senders, node_state, node_cot,
        w1, w2, nw1, nw2, vec)
    arrived = lax.all_to_all(sgrad.reshape(peers, slots, D), AXES, split_axis=0, concat_axis=0, tiled=True)
    node_grad = node_grad + jax.ops.segment_sum(
        arrived.reshape(peers * slots, D).astype(F32), selected, num_segments=N)

    def scatter(v):
        return lax.psum_scatter(v, AXES, scatter_dimension=0, tiled=True)

    gw1, gw2, gnw1, gnw2 = (scatter(v) for v in (gw1, gw2, gnw1, gnw2))
    gv = lax.psum_scatter(gvec, AXES, scatter_dimension=1, tiled=True)
    return (node_out, edge_out, node_grad, edge_grad, gw1, gv[0], gw2, gv[1], gv[2], gnw1, gv[3], gnw2, gv[4], gv[5])


def solution(mesh):
    two, one, three = P(AXES, None), P(AXES), P(AXES, None, None)
    in_specs = (two, two, three, one, one, one, two, one, two, one, one, two, one, two, one, one, two, two)
    out_specs = (two, two, two, two, two, one, two, one, one, two, one, two, one, one)
    return jax.shard_map(local, mesh=mesh, in_specs=in_specs, out_specs=out_specs, check_vma=False)
```

```python
import functools
import jax, jax.numpy as jnp
from jax import lax
from jax.experimental import pallas as pl
from jax.experimental.pallas import tpu as pltpu
from jax.sharding import PartitionSpec as P

F32 = jnp.float32
BF = jnp.bfloat16
AXES = ("band", "sub")
MESH = pl.DeviceIdType.MESH
LINE = 4


def up16(n):
    return -(-n // 16) * 16


def layout(parts):
    spots, at = [], 0
    for p in parts:
        spots.append(at)
        at += 4 * up16(p)
    return spots, at


class Place:
    def __init__(self, bands):
        self.bands = bands
        self.quads = bands // LINE
        band, self.c = lax.axis_index("band"), lax.axis_index("sub")
        self.a, self.q = band // LINE, band % LINE
        x, y = self.q % 2, self.q // 2
        self.qx = self.q + 1 - 2 * x
        self.qy = self.q + 2 - 4 * y
        self.qd = 3 - self.q
        self.me = band * 2 + self.c
        self.devices = bands * 2

    def dev(self, a, q, c):
        return (a * LINE + q, c)

    def idx(self, a, q, c):
        return (a * LINE + q) * 2 + c

    def other_a(self, k):
        return (self.a + k) % self.quads


def barrier_all(pos):
    sem = pltpu.get_barrier_semaphore()

    @pl.loop(1, pos.devices)
    def _(k):
        t = (pos.me + k) % pos.devices
        pl.semaphore_signal(sem, inc=1, device_id=(t // 2, t % 2), device_id_type=MESH)

    pl.semaphore_wait(sem, pos.devices - 1)


def gather_kernel(bands, parts, fast, w1_ref, w2_ref, nw1_ref, nw2_ref, vec_ref, sel_ref, node_ref, *refs):
    if fast:
        outs, (vec_out, snd_out, buf, outg, inc, recv, half, send, a_recv, a_send) = refs[:4], refs[4:]
    else:
        (buf, vec_out, snd_out, outg, inc, recv, half, send, a_recv, a_send) = refs
        outs = None
    pos = Place(bands)
    spots, tail = layout(parts)
    rows = buf.shape[1]
    cut = up16(rows // 2)
    me, c, a, q = pos.me, pos.c, pos.a, pos.q
    mats = (w1_ref, w2_ref, nw1_ref, nw2_ref)
    D = node_ref.shape[1]
    peers, slots = sel_ref.shape
    S = peers * slots
    for m, p, o in zip(mats, parts, spots):
        for j in range(4):
            buf[me, o + j * up16(p):o + j * up16(p) + p, :] = m[:, 128 * j:128 * j + 128]
    group = 128 // vec_ref.shape[1]
    lanes = lax.broadcasted_iota(jnp.int32, (8, 128), 1)
    vals = jnp.concatenate([vec_ref[...]] * group, axis=1).astype(F32)
    vals = jnp.where(lanes // vec_ref.shape[1] == me % group, vals, 0.0)
    buf[me, tail:tail + 16, :] = jnp.concatenate([vals, jnp.zeros((8, 128), F32)], axis=0).astype(BF)
    barrier_all(pos)
    count = [0]

    def push(src, part, sem, target):
        ref = buf.at[src] if part is None else buf.at[src, part]
        cp = pltpu.make_async_remote_copy(src_ref=ref, dst_ref=ref, send_sem=send.at[count[0]], recv_sem=sem,
                                          device_id=target, device_id_type=MESH)
        count[0] += 1
        cp.start()
        return cp

    started = []
    A_PART, B_PART = pl.ds(0, cut), pl.ds(cut, rows - cut)

    def wait(src, part, sem):
        ref = buf.at[src] if part is None else buf.at[src, part]
        pltpu.make_async_remote_copy(src_ref=ref, dst_ref=ref, send_sem=send.at[0], recv_sem=sem,
                                     device_id=pos.dev(a, q, 1 - c), device_id_type=MESH).wait_recv()

    def unpack(src):
        if outs is None:
            return
        for o_ref, p, o in zip(outs, parts, spots):
            for j in range(4):
                o_ref[pl.ds(pl.multiple_of(src * p, 16), p), 128 * j:128 * j + 128] = \
                    buf[src, o + j * p:o + j * p + p, :]

    for k in range(1, pos.quads):
        started.append(push(me, None, recv.at[me], pos.dev(pos.other_a(k), q, c)))

    def spread(src):
        started.append(push(src, None, recv.at[src], pos.dev(a, pos.qx, c)))
        started.append(push(src, None, recv.at[src], pos.dev(a, pos.qy, c)))

    def sibling(src):
        started.append(push(src, None, recv.at[src], pos.dev(a, q, 1 - c)))

    spread(me)
    sibling(me)
    ids = sel_ref[...]
    pick = (lax.broadcasted_iota(jnp.int32, (S, peers), 0) // slots
            == lax.broadcasted_iota(jnp.int32, (S, peers), 1)).astype(BF)
    low = jnp.dot(pick, (ids % 256).astype(BF), preferred_element_type=F32)
    high = jnp.dot(pick, (ids // 256).astype(BF), preferred_element_type=F32)
    mine = lax.broadcasted_iota(jnp.int32, (S, slots), 0) % slots == lax.broadcasted_iota(jnp.int32, (S, slots), 1)
    col = jnp.sum(jnp.where(mine, low + 256.0 * high, 0.0), axis=1, keepdims=True)
    hot = (col == lax.broadcasted_iota(jnp.int32, (S, node_ref.shape[0]), 1).astype(F32)).astype(BF)
    picked = jnp.dot(hot, node_ref[...], preferred_element_type=F32)
    outg[:, 0:slots, :] = picked[:, 0:D // 2].reshape(peers, slots, D // 2).astype(BF)
    outg[:, slots:, :] = picked[:, D // 2:].reshape(peers, slots, D // 2).astype(BF)

    def exchange(t):
        return pltpu.make_async_remote_copy(src_ref=outg.at[t], dst_ref=inc.at[me], send_sem=a_send.at[t],
                                            recv_sem=a_recv.at[me], device_id=(t // 2, t % 2), device_id_type=MESH)

    @pl.loop(1, pos.devices)
    def _(k):
        exchange((me + k) % pos.devices).start()

    inc[me] = outg[me]
    unpack(me)
    line = [pos.idx(pos.other_a(k), q, c) for k in range(1, pos.quads)]
    for src in line:
        wait(src, None, recv.at[src])
        spread(src)
        sibling(src)
        unpack(src)
    for k in range(pos.quads):
        ak = pos.other_a(k)
        sx, sy = pos.idx(ak, pos.qx, c), pos.idx(ak, pos.qy, c)
        wait(sx, None, recv.at[sx])
        started.append(push(sx, A_PART, half.at[0, ak], pos.dev(a, pos.qy, c)))
        sibling(sx)
        unpack(sx)
        wait(sy, None, recv.at[sy])
        started.append(push(sy, B_PART, half.at[1, ak], pos.dev(a, pos.qx, c)))
        sibling(sy)
        unpack(sy)
    for k in range(pos.quads):
        ak = pos.other_a(k)
        sd = pos.idx(ak, pos.qd, c)
        wait(sd, A_PART, half.at[0, ak])
        wait(sd, B_PART, half.at[1, ak])
        sibling(sd)
        unpack(sd)

    @pl.loop(1, pos.devices)
    def _(k):
        t = (me + k) % pos.devices
        pltpu.make_async_remote_copy(src_ref=outg.at[t], dst_ref=inc.at[t], send_sem=a_send.at[t],
                                     recv_sem=a_recv.at[t], device_id=(t // 2, t % 2), device_id_type=MESH).wait()

    snd_out[:, 0:D // 2] = inc[:, 0:slots, :].astype(F32).reshape(S, D // 2).astype(BF)
    snd_out[:, D // 2:] = inc[:, slots:, :].astype(F32).reshape(S, D // 2).astype(BF)
    for k in range(pos.quads):
        ak = pos.other_a(k)
        for qq in (q, pos.qx, pos.qy, pos.qd):
            src = pos.idx(ak, qq, 1 - c)
            wait(src, None, recv.at[src])
            unpack(src)
    for g in range(D // 128):
        v = buf[g * group, tail:tail + 16, :].astype(F32)
        for s in range(1, group):
            v = v + buf[g * group + s, tail:tail + 16, :].astype(F32)
        vec_out[:, 128 * g:128 * g + 128] = v.astype(BF)
    for cp in started:
        cp.wait_send()


def gather_weights(bands, w1, w2, nw1, nw2, vec, sel, node):
    parts = tuple(m.shape[0] for m in (w1, w2, nw1, nw2))
    fast = all(p % 16 == 0 for p in parts)
    _, tail = layout(parts)
    rows = tail + 16
    n = bands * 2
    quads = bands // LINE
    D = node.shape[1]
    peers, slots = sel.shape
    S = peers * slots
    V = pl.BlockSpec(memory_space=pltpu.VMEM)
    sds = jax.ShapeDtypeStruct
    shards = sds((n, rows, 128), BF)
    full = [sds((n * p, D), BF) for p in parts]
    outs = (full if fast else [shards]) + [sds((16, D), BF), sds((S, D), BF)]
    sends = (quads - 1) + 2 * quads + 2 * quads + 4 * quads
    scratch = ([pltpu.VMEM(shards.shape, BF)] if fast else []) + [
        pltpu.VMEM((peers, 2 * slots, D // 2), BF), pltpu.VMEM((peers, 2 * slots, D // 2), BF),
        pltpu.SemaphoreType.DMA((n,)), pltpu.SemaphoreType.DMA((2, quads)), pltpu.SemaphoreType.DMA((sends,)),
        pltpu.SemaphoreType.DMA((n,)), pltpu.SemaphoreType.DMA((n,))]
    res = pl.pallas_call(
        functools.partial(gather_kernel, bands, parts, fast),
        out_shape=outs, in_specs=[V] * 7, out_specs=[V] * len(outs), scratch_shapes=scratch,
        compiler_params=pltpu.CompilerParams(collective_id=0, has_side_effects=True, vmem_limit_bytes=60 * 2**20),
        name="gather_weights",
    )(w1, w2, nw1, nw2, vec, sel, node)
    if fast:
        return res
    got, vec, snd = res
    spots, _ = layout(parts)
    mats = []
    for p, o in zip(parts, spots):
        cols = [got[:, o + j * up16(p):o + j * up16(p) + p, :].reshape(n * p, 128) for j in range(4)]
        mats.append(jnp.concatenate(cols, axis=1))
    return (*mats, vec, snd)


def reduce_kernel(bands, p_ref, msg_ref, red_ref, arr_ref, own, sib, xa, yb, ya, xb, zin,
                  own_sem, sib_recv, x1, y1, y2, x2, z_recv, send, a_recv, a_send):
    pos = Place(bands)
    me, c, a, q = pos.me, pos.c, pos.a, pos.q
    rows = own.shape[1]
    cut = up16(rows // 2)
    A, B = pl.ds(0, cut), pl.ds(cut, rows - cut)
    count = [0]
    started = []

    def push(src, dst, sem, target):
        cp = pltpu.make_async_remote_copy(src_ref=src, dst_ref=dst, send_sem=send.at[count[0]], recv_sem=sem,
                                          device_id=target, device_id_type=MESH)
        count[0] += 1
        cp.start()
        started.append(cp)

    def wait(dst, sem):
        pltpu.make_async_remote_copy(src_ref=dst, dst_ref=dst, send_sem=send.at[0], recv_sem=sem,
                                     device_id=pos.dev(a, q, 1 - c), device_id_type=MESH).wait_recv()

    order = [pos.other_a(k) for k in range(1, pos.quads)] + [a]
    square = [pl.ds(ak * LINE, LINE) for ak in order]
    mine = []
    for ak, sq in zip(order, square):
        cp = pltpu.make_async_copy(p_ref.at[c, sq], own.at[sq], own_sem.at[ak])
        cp.start()
        mine.append(cp)
    barrier_all(pos)
    for ak, sq in zip(order, square):
        push(p_ref.at[1 - c, sq], sib.at[sq], sib_recv.at[ak], pos.dev(a, q, 1 - c))

    def exchange(t):
        return pltpu.make_async_remote_copy(src_ref=msg_ref.at[t], dst_ref=arr_ref.at[me], send_sem=a_send.at[t],
                                            recv_sem=a_recv.at[me], device_id=(t // 2, t % 2), device_id_type=MESH)

    @pl.loop(1, pos.devices)
    def _(k):
        exchange((me + k) % pos.devices).start()

    arr_ref[me] = msg_ref[me]
    to_x, to_y = pos.dev(a, pos.qx, c), pos.dev(a, pos.qy, c)

    def add(ref, idx, other):
        ref[idx] = (ref[idx].astype(F32) + other.astype(F32)).astype(BF)

    def first(k):
        ak, sq = order[k], square[k]
        at = ak * LINE
        mine[k].wait()
        wait(sib.at[sq], sib_recv.at[ak])
        own[sq] = (own[sq].astype(F32) + sib[sq].astype(F32)).astype(BF)
        push(own.at[at + pos.qx, A], xa.at[ak, 0], x1.at[ak, 0], to_x)
        push(own.at[at + pos.qy, B], yb.at[ak, 0], y1.at[ak, 0], to_y)
        push(own.at[at + pos.qd, A], xa.at[ak, 1], x1.at[ak, 1], to_x)
        push(own.at[at + pos.qd, B], yb.at[ak, 1], y1.at[ak, 1], to_y)

    def second(k):
        ak = order[k]
        at = ak * LINE
        wait(xa.at[ak, 1], x1.at[ak, 1])
        add(own, (at + pos.qy, A), xa[ak, 1])
        push(own.at[at + pos.qy, A], ya.at[ak], y2.at[ak], to_y)
        wait(yb.at[ak, 1], y1.at[ak, 1])
        add(own, (at + pos.qx, B), yb[ak, 1])
        push(own.at[at + pos.qx, B], xb.at[ak], x2.at[ak], to_x)

    def third(k):
        ak = order[k]
        at = ak * LINE
        wait(xa.at[ak, 0], x1.at[ak, 0])
        wait(yb.at[ak, 0], y1.at[ak, 0])
        wait(ya.at[ak], y2.at[ak])
        wait(xb.at[ak], x2.at[ak])
        top = own[at + q, A].astype(F32) + xa[ak, 0].astype(F32) + ya[ak].astype(F32)
        low = own[at + q, B].astype(F32) + yb[ak, 0].astype(F32) + xb[ak].astype(F32)
        if k < pos.quads - 1:
            own[at + q, A] = top.astype(BF)
            own[at + q, B] = low.astype(BF)
            push(own.at[at + q], zin.at[a], z_recv.at[a], pos.dev(ak, q, c))
        else:
            red_ref[A, :] = top
            red_ref[B, :] = low

    n = pos.quads
    first(0)
    if n > 1:
        first(1)
    for k in range(n):
        second(k)
        if k + 2 < n:
            first(k + 2)
        if k >= 1:
            third(k - 1)
    third(n - 1)
    for k in range(n - 1):
        ak = order[k]
        wait(zin.at[ak], z_recv.at[ak])
        red_ref[...] += zin[ak].astype(F32)

    @pl.loop(1, pos.devices)
    def _(k):
        t = (me + k) % pos.devices
        pltpu.make_async_remote_copy(src_ref=msg_ref.at[t], dst_ref=arr_ref.at[t], send_sem=a_send.at[t],
                                     recv_sem=a_recv.at[t], device_id=(t // 2, t % 2), device_id_type=MESH).wait()

    for cp in started:
        cp.wait_send()


def reduce_grads(bands, packed, msgs):
    rows = packed.shape[2]
    n = bands * 2
    quads = bands // LINE
    cut = up16(rows // 2)
    V = pl.BlockSpec(memory_space=pltpu.VMEM)
    sds = jax.ShapeDtypeStruct
    sem = pltpu.SemaphoreType.DMA
    return pl.pallas_call(
        functools.partial(reduce_kernel, bands),
        out_shape=[sds((rows, 128), F32), sds(msgs.shape, BF)],
        in_specs=[pl.BlockSpec(memory_space=pl.ANY), V], out_specs=[V, V],
        scratch_shapes=[
            pltpu.VMEM((bands, rows, 128), BF), pltpu.VMEM((bands, rows, 128), BF),
            pltpu.VMEM((quads, 2, cut, 128), BF), pltpu.VMEM((quads, 2, rows - cut, 128), BF),
            pltpu.VMEM((quads, cut, 128), BF), pltpu.VMEM((quads, rows - cut, 128), BF),
            pltpu.VMEM((quads, rows, 128), BF),
            sem((quads,)), sem((quads,)), sem((quads, 2)), sem((quads, 2)), sem((quads,)), sem((quads,)), sem((quads,)),
            sem((8 * quads,)), sem((n,)), sem((n,))],
        compiler_params=pltpu.CompilerParams(collective_id=1, has_side_effects=True, vmem_limit_bytes=60 * 2**20),
        name="reduce_grads",
    )(packed, msgs)


def finish_kernel(bands, parts, red_ref, arr_ref, sel_ref, part_ref, ngrad_ref, w1_ref, w2_ref, nw1_ref, nw2_ref, *vecs):
    me = lax.axis_index("band") * 2 + lax.axis_index("sub")
    spots, tail = layout(parts)
    for o_ref, p, o in zip((w1_ref, w2_ref, nw1_ref, nw2_ref), parts, spots):
        for j in range(4):
            o_ref[:, 128 * j:128 * j + 128] = red_ref[o + j * up16(p):o + j * up16(p) + p, :]
    width = vecs[0].shape[0]
    group = 128 // width
    slab = red_ref[tail:tail + 8, :]
    got = slab[:, 0:width]
    for g in range(1, group):
        got = jnp.where(me % group == g, slab[:, g * width:(g + 1) * width], got)
    for k, v_ref in enumerate(vecs):
        v_ref[...] = got[k]
    peers, slots = sel_ref.shape
    S = peers * slots
    N, D = part_ref.shape
    hot = slot_onehot(sel_ref[...], N)
    arrived = jnp.concatenate([arr_ref[:, 0:slots, :].astype(F32).reshape(S, D // 2),
                               arr_ref[:, slots:, :].astype(F32).reshape(S, D // 2)], axis=1).astype(BF)
    ngrad_ref[...] = part_ref[...] + lax.dot_general(hot, arrived, (((0,), (0,)), ((), ())), preferred_element_type=F32)


def slot_onehot(ids, nodes):
    peers, slots = ids.shape
    S = peers * slots
    pick = (lax.broadcasted_iota(jnp.int32, (S, peers), 0) // slots
            == lax.broadcasted_iota(jnp.int32, (S, peers), 1)).astype(BF)
    low = jnp.dot(pick, (ids % 256).astype(BF), preferred_element_type=F32)
    high = jnp.dot(pick, (ids // 256).astype(BF), preferred_element_type=F32)
    mine = lax.broadcasted_iota(jnp.int32, (S, slots), 0) % slots == lax.broadcasted_iota(jnp.int32, (S, slots), 1)
    col = jnp.sum(jnp.where(mine, low + 256.0 * high, 0.0), axis=1, keepdims=True)
    return (col == lax.broadcasted_iota(jnp.int32, (S, nodes), 1).astype(F32)).astype(BF)


def finish(bands, parts, width, red, arrived, sel, part):
    V = pl.BlockSpec(memory_space=pltpu.VMEM)
    sds = jax.ShapeDtypeStruct
    D = part.shape[1]
    outs = [sds(part.shape, F32)] + [sds((p, D), F32) for p in parts] + [sds((width,), F32)] * 6
    return pl.pallas_call(
        functools.partial(finish_kernel, bands, parts),
        out_shape=outs, in_specs=[V] * 4, out_specs=[V] * len(outs),
        compiler_params=pltpu.CompilerParams(vmem_limit_bytes=60 * 2**20),
        name="finish",
    )(red, arrived, sel, part)


EPS = 1e-5

def dot(a, b):
    return jnp.dot(a, b, preferred_element_type=F32)

def dot_t(a, b):
    return lax.dot_general(a, b, (((1,), (1,)), ((), ())), preferred_element_type=F32)

def t_dot(a, b):
    return lax.dot_general(a, b, (((0,), (0,)), ((), ())), preferred_element_type=F32)

def rowmean(v):
    return jnp.sum(v, axis=1, keepdims=True) * (1.0 / v.shape[1])

def norm(v):
    c = v - rowmean(v)
    s = lax.rsqrt(rowmean(c * c) + EPS)
    return c * s, s

def core_kernel(nb, R, parts, count_ref, sid_ref, rid_ref, e_ref, cot_ref, snd_ref, node_ref, ncot_ref,
           w1_ref, w2_ref, nw1_ref, nw2_ref, vec_ref,
           nout_ref, eout_ref, ngrad_ref, egrad_ref, msg_ref, *refs):
    fast = all(p % 16 == 0 for p in parts)
    pack_ref = refs[0] if fast else None
    (gw1_ref, gw2_ref, gnw1_ref, gnw2_ref, gvec_ref, wcat, w2h, hid_s, slope_s, nrm_s, scale_s, gath, dg, gacc, gain_acc, shift_acc) = refs[fast:]
    i = pl.program_id(0)
    D = e_ref.shape[1]
    S = snd_ref.shape[0]
    N = node_ref.shape[0]
    count = count_ref[0]
    b1 = vec_ref[0:1, :].astype(F32)
    gain = vec_ref[1:2, :].astype(F32)
    shift = vec_ref[2:3, :].astype(F32)

    @pl.when(i == 0)
    def _():
        wcat[0:D, :] = w1_ref[0:D, :] * 0.5
        wcat[D:D + S, :] = (dot(snd_ref[...], w1_ref[D:2 * D, :]) * 0.5).astype(BF)
        wcat[D + S:, :] = ((dot(node_ref[...], w1_ref[2 * D:, :]) + b1) * 0.5).astype(BF)
        w2h[...] = w2_ref[...] * 0.5
        gath[...] = jnp.zeros_like(gath)
        gacc[...] = jnp.zeros_like(gacc)
        gw2_ref[...] = jnp.zeros_like(gw2_ref)
        gain_acc[...] = jnp.zeros_like(gain_acc)
        shift_acc[...] = jnp.zeros_like(shift_acc)

    blk = lax.rem(i, nb)
    first = blk * R
    rows = pl.ds(pl.multiple_of(first, R), R)
    live_blk = first < count

    def onehot_cols(ids_row, width):
        ids = jnp.broadcast_to(ids_row, (128, R)).T
        lane = lax.broadcasted_iota(jnp.int32, (R, 128), 1)
        d = ids - lane
        parts = [jnp.where(d == 128 * j, 1.0, 0.0).astype(BF) for j in range(width // 128)]
        return jnp.concatenate(parts, axis=1)

    def onehot_rows(ids_row, height):
        sub = lax.broadcasted_iota(jnp.int32, (height, R), 0)
        return jnp.where(sub == ids_row, 1.0, 0.0).astype(BF)

    def ids():
        pos = first + lax.broadcasted_iota(jnp.int32, (1, R), 1)
        sid = sid_ref[pl.ds(blk, 1), :]
        rid = jnp.where(pos < count, rid_ref[pl.ds(blk, 1), :], -1)
        return sid, rid

    def live_col():
        return first + lax.broadcasted_iota(jnp.int32, (R, 1), 0) < count

    @pl.when((i < nb) & live_blk)
    def _():
        sid, rid = ids()
        x = jnp.concatenate([e_ref[...], onehot_cols(sid, S), onehot_cols(rid, N)], axis=1)
        h = dot(x, wcat[...])
        a = 1.0 + jnp.tanh(h)
        hid = h * a
        slope = a * (1.0 + 2.0 * h - hid)
        hid = hid.astype(BF)
        hid_s[rows, :] = hid
        slope_s[rows, :] = slope.astype(BF)
        proj = dot(hid, w2_ref[...])
        live = live_col()
        c = proj - rowmean(proj)
        s = lax.rsqrt(rowmean(c * c) + EPS)
        s = jnp.where(live, s, 0.0)
        scale_s[rows, :] = jnp.broadcast_to(s, (R, 128))
        nrm = c * s
        nrm_s[rows, :] = nrm.astype(BF)
        msg = nrm * gain + shift
        eout_ref[...] = (e_ref[...].astype(F32) + jnp.where(live, msg, 0.0)).astype(BF)
        gath[...] += dot(onehot_rows(rid, N), msg.astype(BF))

    @pl.when((i < nb) & jnp.logical_not(live_blk))
    def _():
        eout_ref[...] = e_ref[...]

    @pl.when(i == nb - 1)
    def _():
        nb1 = vec_ref[3:4, :].astype(F32)
        ngain = vec_ref[4:5, :].astype(F32)
        nshift = vec_ref[5:6, :].astype(F32)
        node = node_ref[...]
        g16 = gath[...].astype(BF)
        pre = dot(node, nw1_ref[0:D, :]) + dot(g16, nw1_ref[D:, :]) + nb1
        sig = 0.5 + 0.5 * jnp.tanh(0.5 * pre)
        hid = (pre * sig).astype(BF)
        proj = dot(hid, nw2_ref[...])
        nrm, s = norm(proj)
        nout_ref[...] = (node.astype(F32) + nrm * ngain + nshift).astype(BF)
        up = ncot_ref[...].astype(F32)
        gvec_ref[4:5, :] = jnp.sum(up * nrm, axis=0, keepdims=True)
        gvec_ref[5:6, :] = jnp.sum(up, axis=0, keepdims=True)
        g = up * ngain
        dproj = (s * (g - rowmean(g) - nrm * rowmean(g * nrm))).astype(BF)
        gnw2_ref[...] = t_dot(hid, dproj)
        dpre = dot_t(dproj, nw2_ref[...]) * (sig * (1.0 + pre * (1.0 - sig)))
        dpre16 = dpre.astype(BF)
        gnw1_ref[0:D, :] = t_dot(node, dpre16)
        gnw1_ref[D:, :] = t_dot(g16, dpre16)
        gvec_ref[3:4, :] = jnp.sum(dpre16.astype(F32), axis=0, keepdims=True)
        ngrad_ref[...] = up + dot_t(dpre16, nw1_ref[0:D, :])
        dg[...] = dot_t(dpre16, nw1_ref[D:, :]).astype(BF)

    @pl.when((i >= nb) & live_blk)
    def _():
        sid, rid = ids()
        live = live_col()
        cot = cot_ref[...].astype(F32)
        dm = jnp.where(live, cot, 0.0) + dot(onehot_cols(rid, N), dg[...])
        nrm = nrm_s[rows, :].astype(F32)
        p = dm * nrm
        gain_acc[...] += jnp.sum(p.reshape(R // 8, 8, D), axis=0)
        shift_acc[...] += jnp.sum(dm.reshape(R // 8, 8, D), axis=0)
        g = dm * gain
        m1 = rowmean(g)
        m2 = rowmean(p * gain)
        s = scale_s[rows, 0:1]
        dproj = (s * (g - m1 - nrm * m2)).astype(BF)
        gw2_ref[...] += t_dot(hid_s[rows, :], dproj)
        dpre = (dot_t(dproj, w2h[...]) * slope_s[rows, :].astype(F32)).astype(BF)
        gacc[0:D, :] += t_dot(e_ref[...], dpre)
        gacc[D:D + S, :] += dot(onehot_rows(sid, S), dpre)
        gacc[D + S:, :] += dot(onehot_rows(rid, N), dpre)
        egrad_ref[...] = cot + dot_t(dpre, w1_ref[0:D, :])

    @pl.when((i >= nb) & jnp.logical_not(live_blk))
    def _():
        egrad_ref[...] = cot_ref[...].astype(F32)

    @pl.when(i == 2 * nb - 1)
    def _():
        gvec_ref[1:2, :] = jnp.sum(gain_acc[...], axis=0, keepdims=True)
        gvec_ref[2:3, :] = jnp.sum(shift_acc[...], axis=0, keepdims=True)
        gvec_ref[0:1, :] = jnp.sum(gacc[D + S:, :], axis=0, keepdims=True)
        gvec_ref[6:8, :] = jnp.zeros((2, D), F32)
        us = gacc[D:D + S, :].astype(BF)
        ur = gacc[D + S:, :].astype(BF)
        gw1_ref[0:D, :] = gacc[0:D, :]
        gw1_ref[D:2 * D, :] = t_dot(snd_ref[...], us)
        gw1_ref[2 * D:, :] = t_dot(node_ref[...], ur)
        sgrad = dot_t(us, w1_ref[D:2 * D, :])
        peers, slots = msg_ref.shape[0], msg_ref.shape[1] // 2
        msg_ref[:, 0:slots, :] = sgrad[:, 0:D // 2].reshape(peers, slots, D // 2).astype(BF)
        msg_ref[:, slots:, :] = sgrad[:, D // 2:].reshape(peers, slots, D // 2).astype(BF)
        ngrad_ref[...] += dot_t(ur, w1_ref[2 * D:, :])
        if not fast:
            return
        spots, tail = layout(parts)
        bands = pack_ref.shape[1]
        group = 2 * bands // (D // 128)

        @pl.loop(0, bands)
        def _(b):
            for c in range(2):
                d = b * 2 + c
                for g_ref, p, o in zip((gw1_ref, gw2_ref, gnw1_ref, gnw2_ref), parts, spots):
                    for j in range(D // 128):
                        at = o + j * up16(p)
                        pack_ref[c, b, at:at + p, :] = g_ref[pl.ds(pl.multiple_of(d * p, p), p),
                                                             128 * j:128 * j + 128].astype(BF)

        for d in range(2 * bands):
            g = d // group
            pack_ref[d % 2, d // 2, tail:tail + 16, :] = jnp.concatenate(
                [gvec_ref[:, 128 * g:128 * g + 128]] * 2, axis=0).astype(BF)


def core(bands, parts, count, sid, rid, e, cot, snd, node, ncot, w1, w2, nw1, nw2, vec, R=512):
    E, D = e.shape
    nb = E // R
    S, N = snd.shape[0], node.shape[0]
    V = pl.BlockSpec(memory_space=pltpu.VMEM)
    fb = pl.BlockSpec((R, D), lambda i: (jnp.minimum(i, nb - 1), 0))
    bb = pl.BlockSpec((R, D), lambda i: (jnp.maximum(i - nb, 0), 0))
    both = pl.BlockSpec((R, D), lambda i: (lax.rem(i, nb), 0))
    sds = jax.ShapeDtypeStruct
    slots = S // (2 * bands)
    fast = all(p % 16 == 0 for p in parts)
    rows = layout(parts)[1] + 16
    grads = [(3 * D, D), (D, D), (2 * D, D), (D, D), (8, D)]
    outs = [sds((N, D), BF), sds((E, D), BF), sds((N, D), F32), sds((E, D), F32),
            sds((2 * bands, 2 * slots, D // 2), BF)]
    outs += [sds((2, bands, rows, 128), BF)] if fast else [sds(g, F32) for g in grads]
    *res, packed = res = pl.pallas_call(
        functools.partial(core_kernel, nb, R, parts),
        grid=(2 * nb,),
        in_specs=[pl.BlockSpec(memory_space=pltpu.SMEM), V, V, both, bb, V, V, V, V, V, V, V, V],
        out_specs=[V, fb, V, bb] + [V] * (len(outs) - 4),
        out_shape=outs,
        scratch_shapes=([pltpu.VMEM(g, F32) for g in grads] if fast else []) + [
            pltpu.VMEM((D + S + N, D), BF), pltpu.VMEM((D, D), BF),
            pltpu.VMEM((E, D), BF), pltpu.VMEM((E, D), BF), pltpu.VMEM((E, D), BF),
            pltpu.VMEM((E, 128), F32), pltpu.VMEM((N, D), F32), pltpu.VMEM((N, D), BF),
            pltpu.VMEM((D + S + N, D), F32), pltpu.VMEM((8, D), F32), pltpu.VMEM((8, D), F32)],
        compiler_params=pltpu.CompilerParams(vmem_limit_bytes=63 * 1024 * 1024, dimension_semantics=("arbitrary",)),
        name="edge_node_core",
    )(count, sid.reshape(nb, R), rid.reshape(nb, R), e, cot, snd, node, ncot, w1, w2, nw1, nw2, vec)
    if not fast:
        packed = pack_grads(bands, parts, res[5:])
    return (*res[:4], packed, res[4])


def pack_grads(bands, parts, grads):
    *mats, vec = [g.astype(BF) for g in grads]
    n, D = 2 * bands, vec.shape[1]
    blocks = []
    for m, p in zip(mats, parts):
        for j in range(D // 128):
            block = m[:, 128 * j:128 * j + 128].reshape(n, p, 128)
            blocks.append(jnp.pad(block, ((0, 0), (0, up16(p) - p), (0, 0))))
    slabs = jnp.repeat(vec.reshape(8, D // 128, 128).transpose(1, 0, 2), n // (D // 128), axis=0)
    full = jnp.concatenate(blocks + [slabs, slabs], axis=1)
    return full.reshape(bands, 2, full.shape[1], 128).transpose(1, 0, 2, 3)


def local(bands, node_state, edge_state, send_rows, edge_sender, edge_receiver, edge_count, edge_w1, edge_b1, edge_w2,
          edge_gain, edge_shift, node_w1, node_b1, node_w2, node_gain, node_shift, node_cot, edge_cot):
    parts = tuple(m.shape[0] for m in (edge_w1, edge_w2, node_w1, node_w2))
    width = edge_b1.shape[0]
    vecs = (edge_b1, edge_gain, edge_shift, node_b1, node_gain, node_shift)
    sel = send_rows[0]
    none = jnp.zeros((width,), BF)
    w1, w2, nw1, nw2, vec, senders = gather_weights(
        bands, edge_w1, edge_w2, node_w1, node_w2, jnp.stack(vecs + (none, none)), sel, node_state)
    node_out, edge_out, node_part, edge_grad, packed, msgs = core(
        bands, parts, edge_count, edge_sender, edge_receiver, edge_state, edge_cot, senders, node_state, node_cot,
        w1, w2, nw1, nw2, vec)
    red, arrived = reduce_grads(bands, packed, msgs)
    node_grad, gw1, gw2, gnw1, gnw2, *gv = finish(bands, parts, width, red, arrived, sel, node_part)
    return (node_out, edge_out, node_grad, edge_grad, gw1, gv[0], gw2, gv[1], gv[2], gnw1, gv[3], gnw2, gv[4], gv[5])


def solution(mesh):
    two, one, three = P(AXES, None), P(AXES), P(AXES, None, None)
    in_specs = (two, two, three, one, one, one, two, one, two, one, one, two, one, two, one, one, two, two)
    out_specs = (two, two, two, two, two, one, two, one, one, two, one, two, one, one)
    return jax.shard_map(functools.partial(local, mesh.shape["band"]), mesh=mesh, in_specs=in_specs,
                         out_specs=out_specs, check_vma=False)
```

```python
import functools
import jax, jax.numpy as jnp
from jax import lax
from jax.experimental import pallas as pl
from jax.experimental.pallas import tpu as pltpu
from jax.sharding import PartitionSpec as P

F32 = jnp.float32
BF = jnp.bfloat16
AXES = ("band", "sub")
MESH = pl.DeviceIdType.MESH
LINE = 4


def up16(n):
    return -(-n // 16) * 16


def layout(parts):
    spots, at = [], 0
    for p in parts:
        spots.append(at)
        at += 4 * up16(p)
    return spots, at


class Place:
    def __init__(self, bands):
        self.bands = bands
        self.quads = bands // LINE
        band, self.c = lax.axis_index("band"), lax.axis_index("sub")
        self.a, self.q = band // LINE, band % LINE
        x, y = self.q % 2, self.q // 2
        self.qx = self.q + 1 - 2 * x
        self.qy = self.q + 2 - 4 * y
        self.qd = 3 - self.q
        self.me = band * 2 + self.c
        self.devices = bands * 2

    def dev(self, a, q, c):
        return (a * LINE + q, c)

    def idx(self, a, q, c):
        return (a * LINE + q) * 2 + c

    def other_a(self, k):
        return (self.a + k) % self.quads


def barrier_all(pos):
    sem = pltpu.get_barrier_semaphore()

    @pl.loop(1, pos.devices)
    def _(k):
        t = (pos.me + k) % pos.devices
        pl.semaphore_signal(sem, inc=1, device_id=(t // 2, t % 2), device_id_type=MESH)

    pl.semaphore_wait(sem, pos.devices - 1)


def gather_kernel(bands, parts, fast, w1_ref, w2_ref, nw1_ref, nw2_ref, sel_ref, node_ref, *refs):
    vecs, refs = refs[:6], refs[6:]
    if fast:
        outs, (vec_out, snd_out, buf, wide, outg, inc, recv, half, send, a_recv, a_send) = refs[:4], refs[4:]
    else:
        (buf, vec_out, snd_out, wide, outg, inc, recv, half, send, a_recv, a_send) = refs
        outs = None
    pos = Place(bands)
    spots, tail = layout(parts)
    rows = buf.shape[1]
    cut = up16(rows // 2)
    me, c, a, q = pos.me, pos.c, pos.a, pos.q
    mats = (w1_ref, w2_ref, nw1_ref, nw2_ref)
    D = node_ref.shape[1]
    slots, peers = sel_ref.shape
    S = peers * slots
    for m, p, o in zip(mats, parts, spots):
        for j in range(4):
            buf[me, o + j * up16(p):o + j * up16(p) + p, :] = m[:, 128 * j:128 * j + 128]
    width = vecs[0].shape[0]
    group = 128 // width
    lanes = lax.broadcasted_iota(jnp.int32, (1, 128), 1)
    for k in range(16):
        if k < 6:
            val = jnp.concatenate([vecs[k][...].astype(F32).reshape(1, width)] * group, axis=1)
            wide[k:k + 1, :] = jnp.where(lanes // width == me % group, val, 0.0)
        else:
            wide[k:k + 1, :] = jnp.zeros((1, 128), F32)
    buf[me, tail:tail + 16, :] = wide[...].astype(BF)
    barrier_all(pos)
    count = [0]

    def push(src, part, sem, target):
        ref = buf.at[src] if part is None else buf.at[src, part]
        cp = pltpu.make_async_remote_copy(src_ref=ref, dst_ref=ref, send_sem=send.at[count[0]], recv_sem=sem,
                                          device_id=target, device_id_type=MESH)
        count[0] += 1
        cp.start()
        return cp

    started = []
    A_PART, B_PART = pl.ds(0, cut), pl.ds(cut, rows - cut)

    def wait(src, part, sem):
        ref = buf.at[src] if part is None else buf.at[src, part]
        pltpu.make_async_remote_copy(src_ref=ref, dst_ref=ref, send_sem=send.at[0], recv_sem=sem,
                                     device_id=pos.dev(a, q, 1 - c), device_id_type=MESH).wait_recv()

    def unpack(src):
        if outs is None:
            return
        for o_ref, p, o in zip(outs, parts, spots):
            for j in range(4):
                o_ref[pl.ds(pl.multiple_of(src * p, 16), p), 128 * j:128 * j + 128] = \
                    buf[src, o + j * p:o + j * p + p, :]

    for k in range(1, pos.quads):
        started.append(push(me, None, recv.at[me], pos.dev(pos.other_a(k), q, c)))

    def spread(src):
        started.append(push(src, None, recv.at[src], pos.dev(a, pos.qx, c)))
        started.append(push(src, None, recv.at[src], pos.dev(a, pos.qy, c)))

    def sibling(src):
        started.append(push(src, None, recv.at[src], pos.dev(a, q, 1 - c)))

    spread(me)
    sibling(me)
    hot = slot_onehot(sel_ref[...], node_ref.shape[0])
    picked = jnp.dot(hot, node_ref[...], preferred_element_type=F32)
    outg[:, 0:slots, :] = picked[:, 0:D // 2].reshape(peers, slots, D // 2).astype(BF)
    outg[:, slots:, :] = picked[:, D // 2:].reshape(peers, slots, D // 2).astype(BF)

    def exchange(t):
        return pltpu.make_async_remote_copy(src_ref=outg.at[t], dst_ref=inc.at[me], send_sem=a_send.at[t],
                                            recv_sem=a_recv.at[me], device_id=(t // 2, t % 2), device_id_type=MESH)

    @pl.loop(1, pos.devices)
    def _(k):
        exchange((me + k) % pos.devices).start()

    inc[me] = outg[me]
    unpack(me)
    line = [pos.idx(pos.other_a(k), q, c) for k in range(1, pos.quads)]
    for src in line:
        wait(src, None, recv.at[src])
        spread(src)
        sibling(src)
        unpack(src)
    for k in range(pos.quads):
        ak = pos.other_a(k)
        sx, sy = pos.idx(ak, pos.qx, c), pos.idx(ak, pos.qy, c)
        wait(sx, None, recv.at[sx])
        started.append(push(sx, A_PART, half.at[0, ak], pos.dev(a, pos.qy, c)))
        sibling(sx)
        unpack(sx)
        wait(sy, None, recv.at[sy])
        started.append(push(sy, B_PART, half.at[1, ak], pos.dev(a, pos.qx, c)))
        sibling(sy)
        unpack(sy)
    for k in range(pos.quads):
        ak = pos.other_a(k)
        sd = pos.idx(ak, pos.qd, c)
        wait(sd, A_PART, half.at[0, ak])
        wait(sd, B_PART, half.at[1, ak])
        sibling(sd)
        unpack(sd)

    @pl.loop(1, pos.devices)
    def _(k):
        t = (me + k) % pos.devices
        pltpu.make_async_remote_copy(src_ref=outg.at[t], dst_ref=inc.at[t], send_sem=a_send.at[t],
                                     recv_sem=a_recv.at[t], device_id=(t // 2, t % 2), device_id_type=MESH).wait()

    snd_out[:, 0:D // 2] = inc[:, 0:slots, :].astype(F32).reshape(S, D // 2).astype(BF)
    snd_out[:, D // 2:] = inc[:, slots:, :].astype(F32).reshape(S, D // 2).astype(BF)
    for k in range(pos.quads):
        ak = pos.other_a(k)
        for qq in (q, pos.qx, pos.qy, pos.qd):
            src = pos.idx(ak, qq, 1 - c)
            wait(src, None, recv.at[src])
            unpack(src)
    for g in range(D // 128):
        v = buf[g * group, tail:tail + 16, :].astype(F32)
        for s in range(1, group):
            v = v + buf[g * group + s, tail:tail + 16, :].astype(F32)
        vec_out[:, 128 * g:128 * g + 128] = v.astype(BF)
    for cp in started:
        cp.wait_send()


def gather_weights(bands, w1, w2, nw1, nw2, sel, node, *vecs):
    parts = tuple(m.shape[0] for m in (w1, w2, nw1, nw2))
    fast = all(p % 16 == 0 for p in parts)
    _, tail = layout(parts)
    rows = tail + 16
    n = bands * 2
    quads = bands // LINE
    D = node.shape[1]
    slots, peers = sel.shape
    S = peers * slots
    V = pl.BlockSpec(memory_space=pltpu.VMEM)
    sds = jax.ShapeDtypeStruct
    shards = sds((n, rows, 128), BF)
    full = [sds((n * p, D), BF) for p in parts]
    outs = (full if fast else [shards]) + [sds((16, D), BF), sds((S, D), BF)]
    sends = (quads - 1) + 2 * quads + 2 * quads + 4 * quads
    scratch = ([pltpu.VMEM(shards.shape, BF)] if fast else []) + [
        pltpu.VMEM((16, 128), F32),
        pltpu.VMEM((peers, 2 * slots, D // 2), BF), pltpu.VMEM((peers, 2 * slots, D // 2), BF),
        pltpu.SemaphoreType.DMA((n,)), pltpu.SemaphoreType.DMA((2, quads)), pltpu.SemaphoreType.DMA((sends,)),
        pltpu.SemaphoreType.DMA((n,)), pltpu.SemaphoreType.DMA((n,))]
    res = pl.pallas_call(
        functools.partial(gather_kernel, bands, parts, fast),
        out_shape=outs, in_specs=[V] * 12, out_specs=[V] * len(outs), scratch_shapes=scratch,
        compiler_params=pltpu.CompilerParams(collective_id=0, has_side_effects=True, vmem_limit_bytes=60 * 2**20),
        name="gather_weights",
    )(w1, w2, nw1, nw2, sel, node, *vecs)
    if fast:
        return res
    got, vec, snd = res
    spots, _ = layout(parts)
    mats = []
    for p, o in zip(parts, spots):
        cols = [got[:, o + j * up16(p):o + j * up16(p) + p, :].reshape(n * p, 128) for j in range(4)]
        mats.append(jnp.concatenate(cols, axis=1))
    return (*mats, vec, snd)


def reduce_kernel(bands, p_ref, msg_ref, red_ref, arr_ref, own, sib, xa, yb, ya, xb, zin,
                  own_sem, sib_recv, x1, y1, y2, x2, z_recv, send, a_recv, a_send):
    pos = Place(bands)
    me, c, a, q = pos.me, pos.c, pos.a, pos.q
    rows = own.shape[1]
    cut = up16(rows // 2)
    A, B = pl.ds(0, cut), pl.ds(cut, rows - cut)
    count = [0]
    started = []

    def push(src, dst, sem, target):
        cp = pltpu.make_async_remote_copy(src_ref=src, dst_ref=dst, send_sem=send.at[count[0]], recv_sem=sem,
                                          device_id=target, device_id_type=MESH)
        count[0] += 1
        cp.start()
        started.append(cp)

    def wait(dst, sem):
        pltpu.make_async_remote_copy(src_ref=dst, dst_ref=dst, send_sem=send.at[0], recv_sem=sem,
                                     device_id=pos.dev(a, q, 1 - c), device_id_type=MESH).wait_recv()

    order = [pos.other_a(k) for k in range(1, pos.quads)] + [a]
    square = [pl.ds(ak * LINE, LINE) for ak in order]
    mine = []
    for ak, sq in zip(order, square):
        cp = pltpu.make_async_copy(p_ref.at[c, sq], own.at[sq], own_sem.at[ak])
        cp.start()
        mine.append(cp)
    barrier_all(pos)
    for ak, sq in zip(order, square):
        push(p_ref.at[1 - c, sq], sib.at[sq], sib_recv.at[ak], pos.dev(a, q, 1 - c))

    def exchange(t):
        return pltpu.make_async_remote_copy(src_ref=msg_ref.at[t], dst_ref=arr_ref.at[me], send_sem=a_send.at[t],
                                            recv_sem=a_recv.at[me], device_id=(t // 2, t % 2), device_id_type=MESH)

    @pl.loop(1, pos.devices)
    def _(k):
        exchange((me + k) % pos.devices).start()

    arr_ref[me] = msg_ref[me]
    to_x, to_y = pos.dev(a, pos.qx, c), pos.dev(a, pos.qy, c)

    def add(ref, idx, other):
        ref[idx] = (ref[idx].astype(F32) + other.astype(F32)).astype(BF)

    def first(k):
        ak, sq = order[k], square[k]
        at = ak * LINE
        mine[k].wait()
        wait(sib.at[sq], sib_recv.at[ak])
        own[sq] = (own[sq].astype(F32) + sib[sq].astype(F32)).astype(BF)
        push(own.at[at + pos.qx, A], xa.at[ak, 0], x1.at[ak, 0], to_x)
        push(own.at[at + pos.qy, B], yb.at[ak, 0], y1.at[ak, 0], to_y)
        push(own.at[at + pos.qd, A], xa.at[ak, 1], x1.at[ak, 1], to_x)
        push(own.at[at + pos.qd, B], yb.at[ak, 1], y1.at[ak, 1], to_y)

    def second(k):
        ak = order[k]
        at = ak * LINE
        wait(xa.at[ak, 1], x1.at[ak, 1])
        add(own, (at + pos.qy, A), xa[ak, 1])
        push(own.at[at + pos.qy, A], ya.at[ak], y2.at[ak], to_y)
        wait(yb.at[ak, 1], y1.at[ak, 1])
        add(own, (at + pos.qx, B), yb[ak, 1])
        push(own.at[at + pos.qx, B], xb.at[ak], x2.at[ak], to_x)

    def third(k):
        ak = order[k]
        at = ak * LINE
        wait(xa.at[ak, 0], x1.at[ak, 0])
        wait(yb.at[ak, 0], y1.at[ak, 0])
        wait(ya.at[ak], y2.at[ak])
        wait(xb.at[ak], x2.at[ak])
        top = own[at + q, A].astype(F32) + xa[ak, 0].astype(F32) + ya[ak].astype(F32)
        low = own[at + q, B].astype(F32) + yb[ak, 0].astype(F32) + xb[ak].astype(F32)
        if k < pos.quads - 1:
            own[at + q, A] = top.astype(BF)
            own[at + q, B] = low.astype(BF)
            push(own.at[at + q], zin.at[a], z_recv.at[a], pos.dev(ak, q, c))
        else:
            red_ref[A, :] = top
            red_ref[B, :] = low

    n = pos.quads
    first(0)
    if n > 1:
        first(1)
    for k in range(n):
        second(k)
        if k + 2 < n:
            first(k + 2)
        if k >= 1:
            third(k - 1)
    third(n - 1)
    for k in range(n - 1):
        ak = order[k]
        wait(zin.at[ak], z_recv.at[ak])
        red_ref[...] += zin[ak].astype(F32)

    @pl.loop(1, pos.devices)
    def _(k):
        t = (me + k) % pos.devices
        pltpu.make_async_remote_copy(src_ref=msg_ref.at[t], dst_ref=arr_ref.at[t], send_sem=a_send.at[t],
                                     recv_sem=a_recv.at[t], device_id=(t // 2, t % 2), device_id_type=MESH).wait()

    for cp in started:
        cp.wait_send()


def reduce_grads(bands, packed, msgs):
    rows = packed.shape[2]
    n = bands * 2
    quads = bands // LINE
    cut = up16(rows // 2)
    V = pl.BlockSpec(memory_space=pltpu.VMEM)
    sds = jax.ShapeDtypeStruct
    sem = pltpu.SemaphoreType.DMA
    return pl.pallas_call(
        functools.partial(reduce_kernel, bands),
        out_shape=[sds((rows, 128), F32), sds(msgs.shape, BF)],
        in_specs=[pl.BlockSpec(memory_space=pl.ANY), V], out_specs=[V, V],
        scratch_shapes=[
            pltpu.VMEM((bands, rows, 128), BF), pltpu.VMEM((bands, rows, 128), BF),
            pltpu.VMEM((quads, 2, cut, 128), BF), pltpu.VMEM((quads, 2, rows - cut, 128), BF),
            pltpu.VMEM((quads, cut, 128), BF), pltpu.VMEM((quads, rows - cut, 128), BF),
            pltpu.VMEM((quads, rows, 128), BF),
            sem((quads,)), sem((quads,)), sem((quads, 2)), sem((quads, 2)), sem((quads,)), sem((quads,)), sem((quads,)),
            sem((8 * quads,)), sem((n,)), sem((n,))],
        compiler_params=pltpu.CompilerParams(collective_id=1, has_side_effects=True, vmem_limit_bytes=60 * 2**20),
        name="reduce_grads",
    )(packed, msgs)


def finish_kernel(bands, parts, red_ref, arr_ref, sel_ref, part_ref, ngrad_ref, w1_ref, w2_ref, nw1_ref, nw2_ref, *vecs):
    me = lax.axis_index("band") * 2 + lax.axis_index("sub")
    spots, tail = layout(parts)
    for o_ref, p, o in zip((w1_ref, w2_ref, nw1_ref, nw2_ref), parts, spots):
        for j in range(4):
            o_ref[:, 128 * j:128 * j + 128] = red_ref[o + j * up16(p):o + j * up16(p) + p, :]
    width = vecs[0].shape[0]
    group = 128 // width
    slab = red_ref[tail:tail + 8, :]
    got = slab[:, 0:width]
    for g in range(1, group):
        got = jnp.where(me % group == g, slab[:, g * width:(g + 1) * width], got)
    for k, v_ref in enumerate(vecs):
        v_ref[...] = got[k]
    slots, peers = sel_ref.shape
    S = peers * slots
    N, D = part_ref.shape
    hot = slot_onehot(sel_ref[...], N)
    arrived = jnp.concatenate([arr_ref[:, 0:slots, :].astype(F32).reshape(S, D // 2),
                               arr_ref[:, slots:, :].astype(F32).reshape(S, D // 2)], axis=1).astype(BF)
    ngrad_ref[...] = part_ref[...] + lax.dot_general(hot, arrived, (((0,), (0,)), ((), ())), preferred_element_type=F32)


def slot_onehot(ids, nodes):
    slots, peers = ids.shape
    S = peers * slots
    pick = (lax.broadcasted_iota(jnp.int32, (S, peers), 0) // slots
            == lax.broadcasted_iota(jnp.int32, (S, peers), 1)).astype(BF)
    low = dot_t(pick, (ids % 256).astype(BF))
    high = dot_t(pick, (ids // 256).astype(BF))
    mine = lax.broadcasted_iota(jnp.int32, (S, slots), 0) % slots == lax.broadcasted_iota(jnp.int32, (S, slots), 1)
    col = jnp.sum(jnp.where(mine, low + 256.0 * high, 0.0), axis=1, keepdims=True)
    return (col == lax.broadcasted_iota(jnp.int32, (S, nodes), 1).astype(F32)).astype(BF)


def finish(bands, parts, width, red, arrived, sel, part):
    V = pl.BlockSpec(memory_space=pltpu.VMEM)
    sds = jax.ShapeDtypeStruct
    D = part.shape[1]
    outs = [sds(part.shape, F32)] + [sds((p, D), F32) for p in parts] + [sds((width,), F32)] * 6
    return pl.pallas_call(
        functools.partial(finish_kernel, bands, parts),
        out_shape=outs, in_specs=[V] * 4, out_specs=[V] * len(outs),
        compiler_params=pltpu.CompilerParams(vmem_limit_bytes=60 * 2**20),
        name="finish",
    )(red, arrived, sel, part)


EPS = 1e-5


def dot(a, b):
    return jnp.dot(a, b, preferred_element_type=F32)


def dot_t(a, b):
    return lax.dot_general(a, b, (((1,), (1,)), ((), ())), preferred_element_type=F32)


def t_dot(a, b):
    return lax.dot_general(a, b, (((0,), (0,)), ((), ())), preferred_element_type=F32)


def rowmean(v):
    return jnp.sum(v, axis=1, keepdims=True) * (1.0 / v.shape[1])


def onehot_cols(ids, width):
    rows = ids.shape[1]
    wide = jnp.broadcast_to(ids, (128, rows)).T
    off = wide - lax.broadcasted_iota(jnp.int32, (rows, 128), 1)
    return jnp.concatenate([jnp.where(off == 128 * j, 1.0, 0.0).astype(BF) for j in range(width // 128)], axis=1)


def onehot_rows(ids, height):
    return jnp.where(lax.broadcasted_iota(jnp.int32, (height, ids.shape[1]), 0) == ids, 1.0, 0.0).astype(BF)


def fold8(v):
    return jnp.sum(v.reshape(v.shape[0] // 8, 8, v.shape[1]), axis=0)


def core_kernel(nb, R, sub, parts, fast, count_ref, sid_ref, rid_ref, e_ref, cot_ref, snd_ref, node_ref, ncot_ref,
                w1_ref, w2_ref, nw1_ref, nw2_ref, vec_ref,
                nout_ref, eout_ref, ngrad_ref, egrad_ref, msg_ref, *refs):
    outs, refs = (refs[:1], refs[1:]) if fast else (refs[:5], refs[5:])
    wcat, w2h, hid_s, slope_s, nrm_s, scale_s, gath, dg, gacc, g2acc, gain_acc, shift_acc, gvec, msg_s, dpre_s, w1t = refs
    i = pl.program_id(0)
    D = e_ref.shape[1]
    S = snd_ref.shape[0]
    N = node_ref.shape[0]
    count = count_ref[0]
    gain = vec_ref[1:2, :].astype(F32)
    shift = vec_ref[2:3, :].astype(F32)
    spots, tail = layout(parts)
    n = 3 * D // parts[0]

    def emit(m, first, value):
        if not fast:
            outs[m][first:first + value.shape[0], :] = value
            return
        p, o = parts[m], spots[m]
        lo, hi = first, first + value.shape[0]
        for d in range(lo // p, -(-hi // p)):
            a, b = max(lo, d * p), min(hi, (d + 1) * p)
            for j in range(D // 128):
                at = o + j * p + a - d * p
                outs[0][d % 2, d // 2, at:at + b - a, :] = value[a - lo:b - lo, 128 * j:128 * j + 128].astype(BF)

    @pl.when(i == 0)
    def _():
        b1 = vec_ref[0:1, :].astype(F32)
        wcat[0:D, :] = w1_ref[0:D, :] * 0.5
        wcat[D:D + S, :] = (dot(snd_ref[...], w1_ref[D:2 * D, :]) * 0.5).astype(BF)
        wcat[D + S:, :] = ((dot(node_ref[...], w1_ref[2 * D:, :]) + b1) * 0.5).astype(BF)
        w2h[...] = (w2_ref[...].astype(F32) * 0.5).T.astype(BF)
        w1t[...] = w1_ref[0:D, :].astype(F32).T.astype(BF)
        gath[...] = jnp.zeros_like(gath)
        gacc[...] = jnp.zeros_like(gacc)
        g2acc[...] = jnp.zeros_like(g2acc)
        gain_acc[...] = jnp.zeros_like(gain_acc)
        shift_acc[...] = jnp.zeros_like(shift_acc)
        scale_s[...] = jnp.zeros_like(scale_s)

    blk = lax.rem(i, nb)
    live_blk = blk * R < count
    subs = R // sub

    def ids(r):
        at = blk * subs + r
        pos = at * sub + lax.broadcasted_iota(jnp.int32, (1, sub), 1)
        sid = sid_ref[pl.ds(at, 1), :]
        rid = jnp.where(pos < count, rid_ref[pl.ds(at, 1), :], -1)
        return sid, rid

    def live_col(r):
        return (blk * subs + r) * sub + lax.broadcasted_iota(jnp.int32, (sub, 1), 0) < count

    def lane_is(at):
        return lax.broadcasted_iota(jnp.int32, (sub, 128), 1) == at

    @pl.when((i < nb) & live_blk)
    def _():
        here = [slice(r * sub, (r + 1) * sub) for r in range(subs)]
        rows = [pl.ds(pl.multiple_of((blk * subs + r) * sub, sub), sub) for r in range(subs)]
        idx = [ids(r) for r in range(subs)]
        h, proj = [None] * subs, [None] * subs

        def a1(r):
            sid, rid = idx[r]
            x = jnp.concatenate([e_ref[here[r], :], onehot_cols(sid, S), onehot_cols(rid, N)], axis=1)
            h[r] = dot(x, wcat[...])

        def a2(r):
            v = h[r]
            a = 1.0 + jnp.tanh(v)
            hid = v * a
            slope_s[rows[r], :] = (a * (1.0 + 2.0 * v - hid)).astype(BF)
            hid_s[rows[r], :] = hid.astype(BF)

        def b1(r):
            proj[r] = dot(hid_s[rows[r], :], w2_ref[...])

        def b2(r):
            live = live_col(r)
            c = proj[r] - rowmean(proj[r])
            s = lax.rsqrt(rowmean(c * c) + EPS)
            s = jnp.where(live, s, 0.0)
            scale_s[...] = jnp.where(lane_is(blk * subs + r), s, scale_s[...])
            nrm = c * s
            nrm_s[rows[r], :] = nrm.astype(BF)
            msg = nrm * gain + shift
            eout_ref[here[r], :] = (e_ref[here[r], :].astype(F32) + jnp.where(live, msg, 0.0)).astype(BF)
            msg_s[here[r], :] = msg.astype(BF)

        def c1(first, last):
            rid = jnp.concatenate([idx[r][1] for r in range(first, last)], axis=1)
            gath[...] += dot(onehot_rows(rid, N), msg_s[first * sub:last * sub, :])

        for t in range(subs + 2):
            if t < subs:
                a1(t)
            if 2 <= t:
                b2(t - 2)
            if 1 <= t < subs + 1:
                b1(t - 1)
            if t < subs:
                a2(t)
        c1(0, subs)

    @pl.when((i < nb) & jnp.logical_not(live_blk))
    def _():
        eout_ref[...] = e_ref[...]

    @pl.when(i == nb - 1)
    def _():
        nb1 = vec_ref[3:4, :].astype(F32)
        ngain = vec_ref[4:5, :].astype(F32)
        nshift = vec_ref[5:6, :].astype(F32)
        node = node_ref[...]
        g16 = gath[...].astype(BF)
        pre = dot(node, nw1_ref[0:D, :]) + dot(g16, nw1_ref[D:, :]) + nb1
        sig = 0.5 + 0.5 * jnp.tanh(0.5 * pre)
        hid = (pre * sig).astype(BF)
        proj = dot(hid, nw2_ref[...])
        c = proj - rowmean(proj)
        s = lax.rsqrt(rowmean(c * c) + EPS)
        nrm = c * s
        nout_ref[...] = (node.astype(F32) + nrm * ngain + nshift).astype(BF)
        up = ncot_ref[...].astype(F32)
        gvec[4:5, :] = jnp.sum(up * nrm, axis=0, keepdims=True)
        gvec[5:6, :] = jnp.sum(up, axis=0, keepdims=True)
        g = up * ngain
        dproj = (s * (g - rowmean(g) - nrm * rowmean(g * nrm))).astype(BF)
        emit(3, 0, t_dot(hid, dproj))
        dpre = dot_t(dproj, nw2_ref[...]) * (sig * (1.0 + pre * (1.0 - sig)))
        dpre16 = dpre.astype(BF)
        emit(2, 0, t_dot(node, dpre16))
        emit(2, D, t_dot(g16, dpre16))
        gvec[3:4, :] = jnp.sum(dpre16.astype(F32), axis=0, keepdims=True)
        ngrad_ref[...] = up + dot_t(dpre16, nw1_ref[0:D, :])
        dg[...] = dot_t(dpre16, nw1_ref[D:, :]).astype(BF)

    @pl.when((i >= nb) & live_blk)
    def _():
        here = [slice(r * sub, (r + 1) * sub) for r in range(subs)]
        rows = [pl.ds(pl.multiple_of((blk * subs + r) * sub, sub), sub) for r in range(subs)]
        every = pl.ds(pl.multiple_of(blk * R, R), R)
        idx = [ids(r) for r in range(subs)]
        came, dhid, back = [None] * subs, [None] * subs, [None] * subs

        def a1(r):
            came[r] = dot(onehot_cols(idx[r][1], N), dg[...])

        def a2(r):
            dm = jnp.where(live_col(r), cot_ref[here[r], :].astype(F32), 0.0) + came[r]
            nrm = nrm_s[rows[r], :].astype(F32)
            p = dm * nrm
            gain_acc[...] += fold8(p)
            shift_acc[...] += fold8(dm)
            g = dm * gain
            m1 = rowmean(g)
            m2 = rowmean(p * gain)
            s = jnp.sum(jnp.where(lane_is(blk * subs + r), scale_s[...], 0.0), axis=1, keepdims=True)
            msg_s[here[r], :] = (s * (g - m1 - nrm * m2)).astype(BF)

        def b1(r):
            dhid[r] = dot(msg_s[here[r], :], w2h[...])

        def b2(r):
            dpre_s[here[r], :] = (dhid[r] * slope_s[rows[r], :].astype(F32)).astype(BF)

        def c1(r):
            back[r] = dot(dpre_s[here[r], :], w1t[...])

        def c2(r):
            egrad_ref[here[r], :] = cot_ref[here[r], :].astype(F32) + back[r]

        for t in range(subs + 3):
            if t < subs:
                a1(t)
            if t >= 3:
                c2(t - 3)
            if 2 <= t < subs + 2:
                b2(t - 2)
            if 1 <= t < subs + 1:
                b1(t - 1)
            if t < subs:
                a2(t)
            if 2 <= t < subs + 2:
                c1(t - 2)
        g2acc[...] += t_dot(hid_s[every, :], msg_s[...])
        sids = jnp.concatenate([v[0] for v in idx], axis=1)
        rids = jnp.concatenate([v[1] for v in idx], axis=1)
        gacc[0:D, :] += t_dot(e_ref[...], dpre_s[...])
        gacc[D:D + S, :] += dot(onehot_rows(sids, S), dpre_s[...])
        gacc[D + S:, :] += dot(onehot_rows(rids, N), dpre_s[...])

    @pl.when((i >= nb) & jnp.logical_not(live_blk))
    def _():
        egrad_ref[...] = cot_ref[...].astype(F32)

    @pl.when(i == 2 * nb - 1)
    def _():
        us = gacc[D:D + S, :].astype(BF)
        ur = gacc[D + S:, :].astype(BF)
        emit(0, 0, gacc[0:D, :])
        emit(0, D, t_dot(snd_ref[...], us))
        emit(0, 2 * D, t_dot(node_ref[...], ur))
        emit(1, 0, g2acc[...])
        ngrad_ref[...] += dot_t(ur, w1_ref[2 * D:, :])
        sgrad = dot_t(us, w1_ref[D:2 * D, :])
        peers, slots = msg_ref.shape[0], msg_ref.shape[1] // 2
        msg_ref[:, 0:slots, :] = sgrad[:, 0:D // 2].reshape(peers, slots, D // 2).astype(BF)
        msg_ref[:, slots:, :] = sgrad[:, D // 2:].reshape(peers, slots, D // 2).astype(BF)
        gvec[0:1, :] = jnp.sum(gacc[D + S:, :], axis=0, keepdims=True)
        gvec[1:2, :] = jnp.sum(gain_acc[...], axis=0, keepdims=True)
        gvec[2:3, :] = jnp.sum(shift_acc[...], axis=0, keepdims=True)
        gvec[6:8, :] = jnp.zeros((2, D), F32)
        if not fast:
            outs[4][...] = gvec[...]
        else:
            for d in range(n):
                g = d * D // n // 128
                outs[0][d % 2, d // 2, tail:tail + 16, :] = jnp.concatenate(
                    [gvec[:, 128 * g:128 * g + 128]] * 2, axis=0).astype(BF)


def core(bands, parts, count, sid, rid, e, cot, snd, node, ncot, w1, w2, nw1, nw2, vec, sub=128):
    E, D = e.shape
    R = 1024 if snd.shape[0] <= 256 else 512
    nb = E // R
    S, N = snd.shape[0], node.shape[0]
    V = pl.BlockSpec(memory_space=pltpu.VMEM)
    fb = pl.BlockSpec((R, D), lambda i: (jnp.minimum(i, nb - 1), 0))
    bb = pl.BlockSpec((R, D), lambda i: (jnp.maximum(i - nb, 0), 0))
    both = pl.BlockSpec((R, D), lambda i: (lax.rem(i, nb), 0))
    sds = jax.ShapeDtypeStruct
    slots = S // (2 * bands)
    fast = all(p % 16 == 0 for p in parts)
    rows = layout(parts)[1] + 16
    grads = [(3 * D, D), (D, D), (2 * D, D), (D, D), (8, D)]
    outs = [sds((N, D), BF), sds((E, D), BF), sds((N, D), F32), sds((E, D), F32),
            sds((2 * bands, 2 * slots, D // 2), BF)]
    outs += [sds((2, bands, rows, 128), BF)] if fast else [sds(g, F32) for g in grads]
    vm = pltpu.VMEM
    *res, packed = res = pl.pallas_call(
        functools.partial(core_kernel, nb, R, sub, parts, fast),
        grid=(2 * nb,),
        in_specs=[pl.BlockSpec(memory_space=pltpu.SMEM), V, V, both, bb, V, V, V, V, V, V, V, V],
        out_specs=[V, fb, V, bb] + [V] * (len(outs) - 4),
        out_shape=outs,
        scratch_shapes=[
            vm((D + S + N, D), BF), vm((D, D), BF), vm((E, D), BF), vm((E, D), BF), vm((E, D), BF),
            vm((sub, 128), F32), vm((N, D), F32), vm((N, D), BF), vm((D + S + N, D), F32), vm((D, D), F32),
            vm((8, D), F32), vm((8, D), F32), vm((8, D), F32), vm((R, D), BF), vm((R, D), BF), vm((D, D), BF)],
        compiler_params=pltpu.CompilerParams(vmem_limit_bytes=63 * 2**20, dimension_semantics=("arbitrary",)),
        name="edge_node_core",
    )(count, sid.reshape(E // sub, sub), rid.reshape(E // sub, sub), e, cot, snd, node, ncot, w1, w2, nw1, nw2, vec)
    if not fast:
        packed = pack_grads(bands, parts, res[5:])
    return (*res[:4], packed, res[4])


def pack_grads(bands, parts, grads):
    *mats, vec = [g.astype(BF) for g in grads]
    n, D = 2 * bands, vec.shape[1]
    blocks = []
    for m, p in zip(mats, parts):
        for j in range(D // 128):
            block = m[:, 128 * j:128 * j + 128].reshape(n, p, 128)
            blocks.append(jnp.pad(block, ((0, 0), (0, up16(p) - p), (0, 0))))
    slabs = jnp.repeat(vec.reshape(8, D // 128, 128).transpose(1, 0, 2), n // (D // 128), axis=0)
    full = jnp.concatenate(blocks + [slabs, slabs], axis=1)
    return full.reshape(bands, 2, full.shape[1], 128).transpose(1, 0, 2, 3)


def local(bands, node_state, edge_state, send_rows, edge_sender, edge_receiver, edge_count, edge_w1, edge_b1, edge_w2,
          edge_gain, edge_shift, node_w1, node_b1, node_w2, node_gain, node_shift, node_cot, edge_cot):
    parts = tuple(m.shape[0] for m in (edge_w1, edge_w2, node_w1, node_w2))
    width = edge_b1.shape[0]
    vecs = (edge_b1, edge_gain, edge_shift, node_b1, node_gain, node_shift)
    sel = send_rows[0].T
    w1, w2, nw1, nw2, vec, senders = gather_weights(
        bands, edge_w1, edge_w2, node_w1, node_w2, sel, node_state, *vecs)
    node_out, edge_out, node_part, edge_grad, packed, msgs = core(
        bands, parts, edge_count, edge_sender, edge_receiver, edge_state, edge_cot, senders, node_state, node_cot,
        w1, w2, nw1, nw2, vec)
    red, arrived = reduce_grads(bands, packed, msgs)
    node_grad, gw1, gw2, gnw1, gnw2, *gv = finish(bands, parts, width, red, arrived, sel, node_part)
    return (node_out, edge_out, node_grad, edge_grad, gw1, gv[0], gw2, gv[1], gv[2], gnw1, gv[3], gnw2, gv[4], gv[5])


def solution(mesh):
    two, one, three = P(AXES, None), P(AXES), P(AXES, None, None)
    in_specs = (two, two, three, one, one, one, two, one, two, one, one, two, one, two, one, one, two, two)
    out_specs = (two, two, two, two, two, one, two, one, one, two, one, two, one, one)
    return jax.shard_map(functools.partial(local, mesh.shape["band"]), mesh=mesh, in_specs=in_specs,
                         out_specs=out_specs, check_vma=False)
```

```python
import functools
import jax, jax.numpy as jnp
from jax import lax
from jax.experimental import pallas as pl
from jax.experimental.pallas import tpu as pltpu
from jax.sharding import PartitionSpec as P

F32 = jnp.float32
BF = jnp.bfloat16
AXES = ("band", "sub")
MESH = pl.DeviceIdType.MESH
LINE = 4


def up16(n):
    return -(-n // 16) * 16


def layout(parts):
    spots, at = [], 0
    for p in parts:
        spots.append(at)
        at += 4 * up16(p)
    return spots, at


class Place:
    def __init__(self, bands):
        self.bands = bands
        self.quads = bands // LINE
        band, self.c = lax.axis_index("band"), lax.axis_index("sub")
        self.a, self.q = band // LINE, band % LINE
        x, y = self.q % 2, self.q // 2
        self.qx = self.q + 1 - 2 * x
        self.qy = self.q + 2 - 4 * y
        self.qd = 3 - self.q
        self.me = band * 2 + self.c
        self.devices = bands * 2

    def dev(self, a, q, c):
        return (a * LINE + q, c)

    def idx(self, a, q, c):
        return (a * LINE + q) * 2 + c

    def other_a(self, k):
        return (self.a + k) % self.quads


def greet_all(pos):
    sem = pltpu.get_barrier_semaphore()

    @pl.loop(1, pos.devices)
    def _(k):
        t = (pos.me + k) % pos.devices
        pl.semaphore_signal(sem, inc=1, device_id=(t // 2, t % 2), device_id_type=MESH)

    return lambda: pl.semaphore_wait(sem, pos.devices - 1)


def gather_kernel(bands, parts, w1_ref, w2_ref, nw1_ref, nw2_ref, sel_ref, node_ref, *refs):
    vecs, refs = refs[:6], refs[6:]
    buf, inc, mine, node, wide, outg, recv, half, send_z, send_q, send_h, send_s, a_recv, a_send, own_sem = refs
    pos = Place(bands)
    spots, tail = layout(parts)
    rows = mine.shape[0]
    cut = up16(rows // 2)
    me, c, a, q, line = pos.me, pos.c, pos.a, pos.q, pos.quads
    D = node.shape[1]
    slots, peers = sel_ref.shape
    met_all = greet_all(pos)
    node_copy = pltpu.make_async_copy(node_ref, node, own_sem.at[0])
    node_copy.start()
    for m, p, o in zip((w1_ref, w2_ref, nw1_ref, nw2_ref), parts, spots):
        for j in range(4):
            mine[o + j * up16(p):o + j * up16(p) + p, :] = m[:, 128 * j:128 * j + 128]
    width = vecs[0].shape[0]
    group = 128 // width
    lanes = lax.broadcasted_iota(jnp.int32, (1, 128), 1)
    wide[...] = jnp.zeros_like(wide)
    for k in range(6):
        val = jnp.concatenate([vecs[k][...].astype(F32).reshape(1, width)] * group, axis=1)
        wide[k:k + 1, :] = jnp.where(lanes // width == me % group, val, 0.0)
    mine[tail:tail + 16, :] = wide[...].astype(BF)
    own_copy = pltpu.make_async_copy(mine, buf.at[me], own_sem.at[1])
    own_copy.start()
    hot = slot_onehot(sel_ref[...], node.shape[0])
    node_copy.wait()
    picked = jnp.dot(hot, node[...], preferred_element_type=F32)
    outg[:, 0:slots, :] = picked[:, 0:D // 2].reshape(peers, slots, D // 2).astype(BF)
    outg[:, slots:, :] = picked[:, D // 2:].reshape(peers, slots, D // 2).astype(BF)
    msg_copy = pltpu.make_async_copy(outg.at[me], inc.at[me], own_sem.at[2])
    msg_copy.start()
    met_all()

    WHOLE = pl.ds(0, rows)
    FIRST, LAST = pl.ds(0, cut), pl.ds(cut, rows - cut)

    def push(ak, qk, part, sem_send, sem_recv, target, own=False):
        src = pos.idx(ak, qk, c)
        return pltpu.make_async_remote_copy(
            src_ref=mine.at[part] if own else buf.at[src, part], dst_ref=buf.at[src, part],
            send_sem=sem_send, recv_sem=sem_recv, device_id=target, device_id_type=MESH)

    def up(ak, own=False):
        return push(ak, q, WHOLE, send_z.at[0, ak], recv.at[pos.idx(ak, q, c)], pos.dev(a + 1, q, c), own)

    def down(ak, own=False):
        return push(ak, q, WHOLE, send_z.at[1, ak], recv.at[pos.idx(ak, q, c)], pos.dev(a - 1, q, c), own)

    def to_x(ak, own=False):
        return push(ak, q, WHOLE, send_q.at[0, ak], recv.at[pos.idx(ak, q, c)], pos.dev(a, pos.qx, c), own)

    def to_y(ak, own=False):
        return push(ak, q, WHOLE, send_q.at[1, ak], recv.at[pos.idx(ak, q, c)], pos.dev(a, pos.qy, c), own)

    def x_to_y(ak):
        return push(ak, pos.qx, FIRST, send_h.at[0, ak], half.at[0, ak], pos.dev(a, pos.qy, c))

    def y_to_x(ak):
        return push(ak, pos.qy, LAST, send_h.at[1, ak], half.at[1, ak], pos.dev(a, pos.qx, c))

    def sibling(ak, qk, own=False):
        return push(ak, qk, WHOLE, send_s.at[ak * LINE + qk], recv.at[pos.idx(ak, qk, c)], pos.dev(a, q, 1 - c), own)

    def arrive(ak, qk, ck=None):
        src = pos.idx(ak, qk, c if ck is None else ck)
        pltpu.make_async_remote_copy(src_ref=buf.at[src], dst_ref=buf.at[src], send_sem=send_s.at[0],
                                     recv_sem=recv.at[src], device_id=pos.dev(a, q, 1 - c),
                                     device_id_type=MESH).wait_recv()

    def exchange(t):
        return pltpu.make_async_remote_copy(src_ref=outg.at[t], dst_ref=inc.at[me], send_sem=a_send.at[t],
                                            recv_sem=a_recv.at[me], device_id=(t // 2, t % 2), device_id_type=MESH)

    pl.when(a + 1 < line)(lambda: up(a, True).start())
    pl.when(a > 0)(lambda: down(a, True).start())
    to_x(a, True).start()
    to_y(a, True).start()
    sibling(a, q, True).start()

    def along(ak, below):
        arrive(ak, q)
        if below:
            pl.when(a + 1 < line)(lambda: up(ak).start())
        else:
            pl.when(a > 0)(lambda: down(ak).start())
        to_x(ak).start()
        to_y(ak).start()
        sibling(ak, q).start()

    def square(ak):
        arrive(ak, pos.qx)
        x_to_y(ak).start()
        sibling(ak, pos.qx).start()
        arrive(ak, pos.qy)
        y_to_x(ak).start()
        sibling(ak, pos.qy).start()

    def both(k, what):
        pl.when(a - k >= 0)(lambda: what(a - k, True))
        pl.when(a + k < line)(lambda: what(a + k, False))

    for k in range(1, line):
        both(k, along)
        if k == 1:
            square(a)
        else:
            both(k - 1, lambda ak, below: square(ak))
    both(line - 1, lambda ak, below: square(ak))

    @pl.loop(1, pos.devices)
    def _(k):
        exchange((me + k) % pos.devices).start()

    for k in range(line):
        ak = pos.other_a(k)
        for part, at in ((FIRST, 0), (LAST, 1)):
            ref = buf.at[pos.idx(ak, pos.qd, c), part]
            pltpu.make_async_remote_copy(src_ref=ref, dst_ref=ref, send_sem=send_s.at[0], recv_sem=half.at[at, ak],
                                         device_id=pos.dev(a, q, 1 - c), device_id_type=MESH).wait_recv()
        sibling(ak, pos.qd).start()

    @pl.loop(1, pos.devices)
    def _(k):
        t = (me + k) % pos.devices
        pltpu.make_async_remote_copy(src_ref=outg.at[t], dst_ref=inc.at[t], send_sem=a_send.at[t],
                                     recv_sem=a_recv.at[t], device_id=(t // 2, t % 2), device_id_type=MESH).wait()

    own_copy.wait()
    msg_copy.wait()
    for k in range(line):
        ak = pos.other_a(k)
        pl.when((a + 1 < line) & (ak <= a))(lambda: up(ak).wait_send())
        pl.when((a > 0) & (ak >= a))(lambda: down(ak).wait_send())
        for cp in (to_x(ak), to_y(ak), x_to_y(ak), y_to_x(ak)):
            cp.wait_send()
        for qk in (q, pos.qx, pos.qy, pos.qd):
            sibling(ak, qk).wait_send()
            arrive(ak, qk, 1 - c)


def gather_weights(bands, w1, w2, nw1, nw2, sel, node, *vecs):
    parts = tuple(m.shape[0] for m in (w1, w2, nw1, nw2))
    rows = layout(parts)[1] + 16
    n, line = bands * 2, bands // LINE
    D = node.shape[1]
    slots, peers = sel.shape
    V, H = pl.BlockSpec(memory_space=pltpu.VMEM), pl.BlockSpec(memory_space=pl.ANY)
    sds, sem, vm = jax.ShapeDtypeStruct, pltpu.SemaphoreType.DMA, pltpu.VMEM
    msgs = (peers, 2 * slots, D // 2)
    return pl.pallas_call(
        functools.partial(gather_kernel, bands, parts),
        out_shape=[sds((n, rows, 128), BF), sds(msgs, BF)],
        in_specs=[V] * 5 + [H] + [V] * 6, out_specs=[H, H],
        scratch_shapes=[
            vm((rows, 128), BF), vm(node.shape, BF), vm((16, 128), F32), vm(msgs, BF),
            sem((n,)), sem((2, line)), sem((2, line)), sem((2, line)), sem((2, line)), sem((bands,)),
            sem((n,)), sem((n,)), sem((3,))],
        compiler_params=pltpu.CompilerParams(collective_id=0, has_side_effects=True, vmem_limit_bytes=63 * 2**20),
        name="gather_weights",
    )(w1, w2, nw1, nw2, sel, node, *vecs)


def reduce_kernel(bands, p_ref, msg_ref, red_ref, arr_ref, own, sib, xa, yb, ya, xb, zin,
                  own_sem, sib_recv, x1, y1, y2, x2, z_recv, send, a_recv, a_send):
    pos = Place(bands)
    me, c, a, q = pos.me, pos.c, pos.a, pos.q
    rows = own.shape[1]
    cut = up16(rows // 2)
    A, B = pl.ds(0, cut), pl.ds(cut, rows - cut)
    count = [0]
    started = []

    def push(src, dst, sem, target):
        cp = pltpu.make_async_remote_copy(src_ref=src, dst_ref=dst, send_sem=send.at[count[0]], recv_sem=sem,
                                          device_id=target, device_id_type=MESH)
        count[0] += 1
        cp.start()
        started.append(cp)

    def wait(dst, sem):
        pltpu.make_async_remote_copy(src_ref=dst, dst_ref=dst, send_sem=send.at[0], recv_sem=sem,
                                     device_id=pos.dev(a, q, 1 - c), device_id_type=MESH).wait_recv()

    order = [pos.other_a(k) for k in range(1, pos.quads)] + [a]
    square = [pl.ds(ak * LINE, LINE) for ak in order]
    mine = []
    for ak, sq in zip(order, square):
        cp = pltpu.make_async_copy(p_ref.at[c, sq], own.at[sq], own_sem.at[ak])
        cp.start()
        mine.append(cp)
    greet_all(pos)()
    for ak, sq in zip(order, square):
        push(p_ref.at[1 - c, sq], sib.at[sq], sib_recv.at[ak], pos.dev(a, q, 1 - c))

    def exchange(t):
        return pltpu.make_async_remote_copy(src_ref=msg_ref.at[t], dst_ref=arr_ref.at[me], send_sem=a_send.at[t],
                                            recv_sem=a_recv.at[me], device_id=(t // 2, t % 2), device_id_type=MESH)

    @pl.loop(1, pos.devices)
    def _(k):
        exchange((me + k) % pos.devices).start()

    arr_ref[me] = msg_ref[me]
    to_x, to_y = pos.dev(a, pos.qx, c), pos.dev(a, pos.qy, c)

    def add(ref, idx, other):
        ref[idx] = (ref[idx].astype(F32) + other.astype(F32)).astype(BF)

    def first(k):
        ak, sq = order[k], square[k]
        at = ak * LINE
        mine[k].wait()
        wait(sib.at[sq], sib_recv.at[ak])
        own[sq] = (own[sq].astype(F32) + sib[sq].astype(F32)).astype(BF)
        push(own.at[at + pos.qx, A], xa.at[ak, 0], x1.at[ak, 0], to_x)
        push(own.at[at + pos.qy, B], yb.at[ak, 0], y1.at[ak, 0], to_y)
        push(own.at[at + pos.qd, A], xa.at[ak, 1], x1.at[ak, 1], to_x)
        push(own.at[at + pos.qd, B], yb.at[ak, 1], y1.at[ak, 1], to_y)

    def second(k):
        ak = order[k]
        at = ak * LINE
        wait(xa.at[ak, 1], x1.at[ak, 1])
        add(own, (at + pos.qy, A), xa[ak, 1])
        push(own.at[at + pos.qy, A], ya.at[ak], y2.at[ak], to_y)
        wait(yb.at[ak, 1], y1.at[ak, 1])
        add(own, (at + pos.qx, B), yb[ak, 1])
        push(own.at[at + pos.qx, B], xb.at[ak], x2.at[ak], to_x)

    def third(k):
        ak = order[k]
        at = ak * LINE
        wait(xa.at[ak, 0], x1.at[ak, 0])
        wait(yb.at[ak, 0], y1.at[ak, 0])
        wait(ya.at[ak], y2.at[ak])
        wait(xb.at[ak], x2.at[ak])
        top = own[at + q, A].astype(F32) + xa[ak, 0].astype(F32) + ya[ak].astype(F32)
        low = own[at + q, B].astype(F32) + yb[ak, 0].astype(F32) + xb[ak].astype(F32)
        if k < pos.quads - 1:
            own[at + q, A] = top.astype(BF)
            own[at + q, B] = low.astype(BF)
            push(own.at[at + q], zin.at[a], z_recv.at[a], pos.dev(ak, q, c))
        else:
            red_ref[A, :] = top
            red_ref[B, :] = low

    n = pos.quads
    first(0)
    if n > 1:
        first(1)
    for k in range(n):
        second(k)
        if k + 2 < n:
            first(k + 2)
        if k >= 1:
            third(k - 1)
    third(n - 1)
    for k in range(n - 1):
        ak = order[k]
        wait(zin.at[ak], z_recv.at[ak])
        red_ref[...] += zin[ak].astype(F32)

    @pl.loop(1, pos.devices)
    def _(k):
        t = (me + k) % pos.devices
        pltpu.make_async_remote_copy(src_ref=msg_ref.at[t], dst_ref=arr_ref.at[t], send_sem=a_send.at[t],
                                     recv_sem=a_recv.at[t], device_id=(t // 2, t % 2), device_id_type=MESH).wait()

    for cp in started:
        cp.wait_send()


def reduce_grads(bands, packed, msgs):
    rows = packed.shape[2]
    n = bands * 2
    quads = bands // LINE
    cut = up16(rows // 2)
    V = pl.BlockSpec(memory_space=pltpu.VMEM)
    sds = jax.ShapeDtypeStruct
    sem = pltpu.SemaphoreType.DMA
    return pl.pallas_call(
        functools.partial(reduce_kernel, bands),
        out_shape=[sds((rows, 128), F32), sds(msgs.shape, BF)],
        in_specs=[pl.BlockSpec(memory_space=pl.ANY), V], out_specs=[V, V],
        scratch_shapes=[
            pltpu.VMEM((bands, rows, 128), BF), pltpu.VMEM((bands, rows, 128), BF),
            pltpu.VMEM((quads, 2, cut, 128), BF), pltpu.VMEM((quads, 2, rows - cut, 128), BF),
            pltpu.VMEM((quads, cut, 128), BF), pltpu.VMEM((quads, rows - cut, 128), BF),
            pltpu.VMEM((quads, rows, 128), BF),
            sem((quads,)), sem((quads,)), sem((quads, 2)), sem((quads, 2)), sem((quads,)), sem((quads,)), sem((quads,)),
            sem((8 * quads,)), sem((n,)), sem((n,))],
        compiler_params=pltpu.CompilerParams(collective_id=1, has_side_effects=True, vmem_limit_bytes=63 * 2**20),
        name="reduce_grads",
    )(packed, msgs)


def finish_kernel(bands, parts, red_ref, arr_ref, sel_ref, part_ref, ngrad_ref, w1_ref, w2_ref, nw1_ref, nw2_ref, *vecs):
    me = lax.axis_index("band") * 2 + lax.axis_index("sub")
    spots, tail = layout(parts)
    for o_ref, p, o in zip((w1_ref, w2_ref, nw1_ref, nw2_ref), parts, spots):
        for j in range(4):
            o_ref[:, 128 * j:128 * j + 128] = red_ref[o + j * up16(p):o + j * up16(p) + p, :]
    width = vecs[0].shape[0]
    group = 128 // width
    slab = red_ref[tail:tail + 8, :]
    got = slab[:, 0:width]
    for g in range(1, group):
        got = jnp.where(me % group == g, slab[:, g * width:(g + 1) * width], got)
    for k, v_ref in enumerate(vecs):
        v_ref[...] = got[k]
    slots, peers = sel_ref.shape
    S = peers * slots
    N, D = part_ref.shape
    hot = slot_onehot(sel_ref[...], N)
    arrived = jnp.concatenate([arr_ref[:, 0:slots, :].astype(F32).reshape(S, D // 2),
                               arr_ref[:, slots:, :].astype(F32).reshape(S, D // 2)], axis=1).astype(BF)
    ngrad_ref[...] = part_ref[...] + lax.dot_general(hot, arrived, (((0,), (0,)), ((), ())), preferred_element_type=F32)


def slot_onehot(ids, nodes):
    slots, peers = ids.shape
    S = peers * slots
    pick = (lax.broadcasted_iota(jnp.int32, (S, peers), 0) // slots
            == lax.broadcasted_iota(jnp.int32, (S, peers), 1)).astype(BF)
    low = dot_t(pick, (ids % 256).astype(BF))
    high = dot_t(pick, (ids // 256).astype(BF))
    mine = lax.broadcasted_iota(jnp.int32, (S, slots), 0) % slots == lax.broadcasted_iota(jnp.int32, (S, slots), 1)
    col = jnp.sum(jnp.where(mine, low + 256.0 * high, 0.0), axis=1, keepdims=True)
    return (col == lax.broadcasted_iota(jnp.int32, (S, nodes), 1).astype(F32)).astype(BF)


def finish(bands, parts, width, red, arrived, sel, part):
    V = pl.BlockSpec(memory_space=pltpu.VMEM)
    sds = jax.ShapeDtypeStruct
    D = part.shape[1]
    outs = [sds(part.shape, F32)] + [sds((p, D), F32) for p in parts] + [sds((width,), F32)] * 6
    return pl.pallas_call(
        functools.partial(finish_kernel, bands, parts),
        out_shape=outs, in_specs=[V] * 4, out_specs=[V] * len(outs),
        compiler_params=pltpu.CompilerParams(vmem_limit_bytes=63 * 2**20),
        name="finish",
    )(red, arrived, sel, part)


EPS = 1e-5


def dot(a, b):
    return jnp.dot(a, b, preferred_element_type=F32)


def dot_t(a, b):
    return lax.dot_general(a, b, (((1,), (1,)), ((), ())), preferred_element_type=F32)


def t_dot(a, b):
    return lax.dot_general(a, b, (((0,), (0,)), ((), ())), preferred_element_type=F32)


def rowmean(v):
    return jnp.sum(v, axis=1, keepdims=True) * (1.0 / v.shape[1])


def onehot_cols(ids, width):
    rows = ids.shape[1]
    wide = jnp.broadcast_to(ids, (128, rows)).T
    off = wide - lax.broadcasted_iota(jnp.int32, (rows, 128), 1)
    return jnp.concatenate([jnp.where(off == 128 * j, 1.0, 0.0).astype(BF) for j in range(width // 128)], axis=1)


def onehot_rows(ids, height):
    return jnp.where(lax.broadcasted_iota(jnp.int32, (height, ids.shape[1]), 0) == ids, 1.0, 0.0).astype(BF)


def fold8(v):
    return jnp.sum(v.reshape(v.shape[0] // 8, 8, v.shape[1]), axis=0)


def core_kernel(nb, R, sub, parts, fast, count_ref, sid_ref, rid_ref, e_ref, cot_ref, node_ref, ncot_ref, *refs):
    (got_ref, inc_ref), refs = (refs[:2], refs[2:]) if fast else ((None, None), refs)
    weights, refs = ((), refs) if fast else (refs[:6], refs[6:])
    nout_ref, eout_ref, ngrad_ref, egrad_ref, msg_ref, *refs = refs
    outs, refs = (refs[:1], refs[1:]) if fast else (refs[:5], refs[5:])
    weights, refs = (refs[:6], refs[6:]) if fast else (weights, refs)
    w1_ref, w2_ref, nw1_ref, nw2_ref, vec_ref, snd_ref = weights
    wcat, w2h, hid_s, slope_s, nrm_s, scale_s, gath, dg, gacc, g2acc, gain_acc, shift_acc, gvec, msg_s, dpre_s, w1t, sem = refs
    i = pl.program_id(0)
    D = e_ref.shape[1]
    S = snd_ref.shape[0]
    N = node_ref.shape[0]
    count = count_ref[0]
    spots, tail = layout(parts)
    n = 3 * D // parts[0]

    def emit(m, first, value):
        if not fast:
            outs[m][first:first + value.shape[0], :] = value
            return
        p, o = parts[m], spots[m]
        lo, hi = first, first + value.shape[0]
        for d in range(lo // p, -(-hi // p)):
            a, b = max(lo, d * p), min(hi, (d + 1) * p)
            for j in range(D // 128):
                at = o + j * p + a - d * p
                outs[0][d % 2, d // 2, at:at + b - a, :] = value[a - lo:b - lo, 128 * j:128 * j + 128].astype(BF)

    def unpack():
        stage = outs[0]
        cp = pltpu.make_async_copy(got_ref, stage, sem)
        cp.start()
        cp.wait()

        @pl.loop(0, n)
        def _(d):
            for w_ref, p, o in zip((w1_ref, w2_ref, nw1_ref, nw2_ref), parts, spots):
                for j in range(D // 128):
                    w_ref[pl.ds(pl.multiple_of(d * p, p), p), 128 * j:128 * j + 128] = \
                        stage[d // (n // 2), d % (n // 2), o + j * p:o + j * p + p, :]

        group = n // (D // 128)
        for g in range(D // 128):
            tiles = [stage[d // (n // 2), d % (n // 2), tail:tail + 16, :].astype(F32)
                     for d in range(g * group, (g + 1) * group)]
            vec_ref[:, 128 * g:128 * g + 128] = functools.reduce(jnp.add, tiles).astype(BF)
        slots = inc_ref.shape[1] // 2
        snd_ref[:, 0:D // 2] = inc_ref[:, 0:slots, :].astype(F32).reshape(S, D // 2).astype(BF)
        snd_ref[:, D // 2:] = inc_ref[:, slots:, :].astype(F32).reshape(S, D // 2).astype(BF)

    @pl.when(i == 0)
    def _():
        if fast:
            unpack()
        b1 = vec_ref[0:1, :].astype(F32)
        wcat[0:D, :] = w1_ref[0:D, :] * 0.5
        wcat[D:D + S, :] = (dot(snd_ref[...], w1_ref[D:2 * D, :]) * 0.5).astype(BF)
        wcat[D + S:, :] = ((dot(node_ref[...], w1_ref[2 * D:, :]) + b1) * 0.5).astype(BF)
        w2h[...] = (w2_ref[...].astype(F32) * 0.5).T.astype(BF)
        w1t[...] = w1_ref[0:D, :].astype(F32).T.astype(BF)
        gath[...] = jnp.zeros_like(gath)
        gacc[...] = jnp.zeros_like(gacc)
        g2acc[...] = jnp.zeros_like(g2acc)
        gain_acc[...] = jnp.zeros_like(gain_acc)
        shift_acc[...] = jnp.zeros_like(shift_acc)
        scale_s[...] = jnp.zeros_like(scale_s)

    gain = vec_ref[1:2, :].astype(F32)
    shift = vec_ref[2:3, :].astype(F32)
    blk = lax.rem(i, nb)
    live_blk = blk * R < count
    subs = R // sub

    def ids(r):
        at = blk * subs + r
        pos = at * sub + lax.broadcasted_iota(jnp.int32, (1, sub), 1)
        sid = sid_ref[pl.ds(at, 1), :]
        rid = jnp.where(pos < count, rid_ref[pl.ds(at, 1), :], -1)
        return sid, rid

    def live_col(r):
        return (blk * subs + r) * sub + lax.broadcasted_iota(jnp.int32, (sub, 1), 0) < count

    def lane_is(at):
        return lax.broadcasted_iota(jnp.int32, (sub, 128), 1) == at

    @pl.when((i < nb) & live_blk)
    def _():
        here = [slice(r * sub, (r + 1) * sub) for r in range(subs)]
        rows = [pl.ds(pl.multiple_of((blk * subs + r) * sub, sub), sub) for r in range(subs)]
        idx = [ids(r) for r in range(subs)]
        h, proj = [None] * subs, [None] * subs

        def a1(r):
            sid, rid = idx[r]
            x = jnp.concatenate([e_ref[here[r], :], onehot_cols(sid, S), onehot_cols(rid, N)], axis=1)
            h[r] = dot(x, wcat[...])

        def a2(r):
            v = h[r]
            a = 1.0 + jnp.tanh(v)
            hid = v * a
            slope_s[rows[r], :] = (a + hid * (2.0 - a)).astype(BF)
            hid_s[rows[r], :] = hid.astype(BF)

        def b1(r):
            proj[r] = dot(hid_s[rows[r], :], w2_ref[...])

        def b2(r):
            live = live_col(r)
            c = proj[r] - rowmean(proj[r])
            s = lax.rsqrt(rowmean(c * c) + EPS)
            s = jnp.where(live, s, 0.0)
            scale_s[...] = jnp.where(lane_is(blk * subs + r), s, scale_s[...])
            nrm = c * s
            nrm_s[rows[r], :] = nrm.astype(BF)
            msg = nrm * gain + shift
            eout_ref[here[r], :] = (e_ref[here[r], :].astype(F32) + jnp.where(live, msg, 0.0)).astype(BF)
            msg_s[here[r], :] = msg.astype(BF)

        def c1(first, last):
            rid = jnp.concatenate([idx[r][1] for r in range(first, last)], axis=1)
            gath[...] += dot(onehot_rows(rid, N), msg_s[first * sub:last * sub, :])

        for t in range(subs + 2):
            if t < subs:
                a1(t)
            if 2 <= t:
                b2(t - 2)
            if 1 <= t < subs + 1:
                b1(t - 1)
            if t < subs:
                a2(t)
        c1(0, subs)

    @pl.when((i < nb) & jnp.logical_not(live_blk))
    def _():
        eout_ref[...] = e_ref[...]

    @pl.when(i == nb - 1)
    def _():
        nb1 = vec_ref[3:4, :].astype(F32)
        ngain = vec_ref[4:5, :].astype(F32)
        nshift = vec_ref[5:6, :].astype(F32)
        node = node_ref[...]
        g16 = gath[...].astype(BF)
        pre = dot(node, nw1_ref[0:D, :]) + dot(g16, nw1_ref[D:, :]) + nb1
        sig = 0.5 + 0.5 * jnp.tanh(0.5 * pre)
        hid = (pre * sig).astype(BF)
        proj = dot(hid, nw2_ref[...])
        c = proj - rowmean(proj)
        s = lax.rsqrt(rowmean(c * c) + EPS)
        nrm = c * s
        nout_ref[...] = (node.astype(F32) + nrm * ngain + nshift).astype(BF)
        up = ncot_ref[...].astype(F32)
        gvec[4:5, :] = jnp.sum(up * nrm, axis=0, keepdims=True)
        gvec[5:6, :] = jnp.sum(up, axis=0, keepdims=True)
        g = up * ngain
        dproj = (s * (g - rowmean(g) - nrm * rowmean(g * nrm))).astype(BF)
        emit(3, 0, t_dot(hid, dproj))
        dpre = dot_t(dproj, nw2_ref[...]) * (sig * (1.0 + pre * (1.0 - sig)))
        dpre16 = dpre.astype(BF)
        emit(2, 0, t_dot(node, dpre16))
        emit(2, D, t_dot(g16, dpre16))
        gvec[3:4, :] = jnp.sum(dpre16.astype(F32), axis=0, keepdims=True)
        ngrad_ref[...] = up + dot_t(dpre16, nw1_ref[0:D, :])
        dg[...] = dot_t(dpre16, nw1_ref[D:, :]).astype(BF)

    @pl.when((i >= nb) & live_blk)
    def _():
        here = [slice(r * sub, (r + 1) * sub) for r in range(subs)]
        rows = [pl.ds(pl.multiple_of((blk * subs + r) * sub, sub), sub) for r in range(subs)]
        every = pl.ds(pl.multiple_of(blk * R, R), R)
        idx = [ids(r) for r in range(subs)]
        came, dhid, back = [None] * subs, [None] * subs, [None] * subs

        def a1(r):
            came[r] = dot(onehot_cols(idx[r][1], N), dg[...])

        def a2(r):
            dm = jnp.where(live_col(r), cot_ref[here[r], :].astype(F32), 0.0) + came[r]
            nrm = nrm_s[rows[r], :].astype(F32)
            p = dm * nrm
            gain_acc[...] += fold8(p)
            shift_acc[...] += fold8(dm)
            g = dm * gain
            m1 = rowmean(g)
            m2 = rowmean(p * gain)
            s = jnp.sum(jnp.where(lane_is(blk * subs + r), scale_s[...], 0.0), axis=1, keepdims=True)
            msg_s[here[r], :] = (s * (g - m1 - nrm * m2)).astype(BF)

        def b1(r):
            dhid[r] = dot(msg_s[here[r], :], w2h[...])

        def b2(r):
            dpre_s[here[r], :] = (dhid[r] * slope_s[rows[r], :].astype(F32)).astype(BF)

        def c1(r):
            back[r] = dot(dpre_s[here[r], :], w1t[...])

        def c2(r):
            egrad_ref[here[r], :] = cot_ref[here[r], :].astype(F32) + back[r]

        for t in range(subs + 3):
            if t < subs:
                a1(t)
            if t >= 3:
                c2(t - 3)
            if 2 <= t < subs + 2:
                b2(t - 2)
            if 1 <= t < subs + 1:
                b1(t - 1)
            if t < subs:
                a2(t)
            if 2 <= t < subs + 2:
                c1(t - 2)
        g2acc[...] += t_dot(hid_s[every, :], msg_s[...])
        sids = jnp.concatenate([v[0] for v in idx], axis=1)
        rids = jnp.concatenate([v[1] for v in idx], axis=1)
        gacc[0:D, :] += t_dot(e_ref[...], dpre_s[...])
        gacc[D:D + S, :] += dot(onehot_rows(sids, S), dpre_s[...])
        gacc[D + S:, :] += dot(onehot_rows(rids, N), dpre_s[...])

    @pl.when((i >= nb) & jnp.logical_not(live_blk))
    def _():
        egrad_ref[...] = cot_ref[...].astype(F32)

    @pl.when(i == 2 * nb - 1)
    def _():
        us = gacc[D:D + S, :].astype(BF)
        ur = gacc[D + S:, :].astype(BF)
        emit(0, 0, gacc[0:D, :])
        emit(0, D, t_dot(snd_ref[...], us))
        emit(0, 2 * D, t_dot(node_ref[...], ur))
        emit(1, 0, g2acc[...])
        ngrad_ref[...] += dot_t(ur, w1_ref[2 * D:, :])
        sgrad = dot_t(us, w1_ref[D:2 * D, :])
        peers, slots = msg_ref.shape[0], msg_ref.shape[1] // 2
        msg_ref[:, 0:slots, :] = sgrad[:, 0:D // 2].reshape(peers, slots, D // 2).astype(BF)
        msg_ref[:, slots:, :] = sgrad[:, D // 2:].reshape(peers, slots, D // 2).astype(BF)
        gvec[0:1, :] = jnp.sum(gacc[D + S:, :], axis=0, keepdims=True)
        gvec[1:2, :] = jnp.sum(gain_acc[...], axis=0, keepdims=True)
        gvec[2:3, :] = jnp.sum(shift_acc[...], axis=0, keepdims=True)
        gvec[6:8, :] = jnp.zeros((2, D), F32)
        if not fast:
            outs[4][...] = gvec[...]
        else:
            for d in range(n):
                g = d * D // n // 128
                outs[0][d % 2, d // 2, tail:tail + 16, :] = jnp.concatenate(
                    [gvec[:, 128 * g:128 * g + 128]] * 2, axis=0).astype(BF)


def core(bands, parts, count, sid, rid, e, cot, node, ncot, got, inc, sub=128):
    E, D = e.shape
    S, N = inc.shape[0] * inc.shape[1] // 2, node.shape[0]
    R = 1024 if S <= 256 else 512
    nb = E // R
    V, H = pl.BlockSpec(memory_space=pltpu.VMEM), pl.BlockSpec(memory_space=pl.ANY)
    fb = pl.BlockSpec((R, D), lambda i: (jnp.minimum(i, nb - 1), 0))
    bb = pl.BlockSpec((R, D), lambda i: (jnp.maximum(i - nb, 0), 0))
    both = pl.BlockSpec((R, D), lambda i: (lax.rem(i, nb), 0))
    sds, vm = jax.ShapeDtypeStruct, pltpu.VMEM
    fast = all(p % 16 == 0 for p in parts)
    rows = layout(parts)[1] + 16
    if fast:
        weights, specs = (got.reshape(2, bands, rows, 128), inc), [H, V]
    else:
        weights, specs = unpack_weights(bands, parts, got, inc), [V] * 6
    grads = [(3 * D, D), (D, D), (2 * D, D), (D, D), (8, D)]
    outs = [sds((N, D), BF), sds((E, D), BF), sds((N, D), F32), sds((E, D), F32), sds(inc.shape, BF)]
    outs += [sds((2, bands, rows, 128), BF)] if fast else [sds(g, F32) for g in grads]
    *res, packed = res = pl.pallas_call(
        functools.partial(core_kernel, nb, R, sub, parts, fast),
        grid=(2 * nb,),
        in_specs=[pl.BlockSpec(memory_space=pltpu.SMEM), V, V, both, bb, V, V] + specs,
        out_specs=[V, fb, V, bb] + [V] * (len(outs) - 4),
        out_shape=outs,
        scratch_shapes=([vm(g, BF) for g in grads[:4]] + [vm((16, D), BF), vm((S, D), BF)] if fast else []) + [
            vm((D + S + N, D), BF), vm((D, D), BF), vm((E, D), BF), vm((E, D), BF), vm((E, D), BF),
            vm((sub, 128), F32), vm((N, D), F32), vm((N, D), BF), vm((D + S + N, D), F32), vm((D, D), F32),
            vm((8, D), F32), vm((8, D), F32), vm((8, D), F32), vm((R, D), BF), vm((R, D), BF), vm((D, D), BF),
            pltpu.SemaphoreType.DMA],
        compiler_params=pltpu.CompilerParams(vmem_limit_bytes=63 * 2**20, dimension_semantics=("arbitrary",)),
        name="edge_node_core",
    )(count, sid.reshape(E // sub, sub), rid.reshape(E // sub, sub), e, cot, node, ncot, *weights)
    if not fast:
        packed = pack_grads(bands, parts, res[5:])
    return (*res[:4], packed, res[4])


def unpack_weights(bands, parts, got, inc):
    spots, tail = layout(parts)
    n, slots, D = 2 * bands, inc.shape[1] // 2, 2 * inc.shape[2]
    mats = []
    for p, o in zip(parts, spots):
        cols = [got[:, o + j * up16(p):o + j * up16(p) + p, :].reshape(n * p, 128) for j in range(D // 128)]
        mats.append(jnp.concatenate(cols, axis=1))
    slabs = got[:, tail:tail + 16, :].reshape(D // 128, -1, 16, 128).sum(axis=1)
    vec = slabs.transpose(1, 0, 2).reshape(16, D)
    snd = jnp.concatenate([inc[:, :slots].reshape(n * slots, D // 2), inc[:, slots:].reshape(n * slots, D // 2)], axis=1)
    return (*mats, vec, snd)


def pack_grads(bands, parts, grads):
    *mats, vec = [g.astype(BF) for g in grads]
    n, D = 2 * bands, vec.shape[1]
    blocks = []
    for m, p in zip(mats, parts):
        for j in range(D // 128):
            block = m[:, 128 * j:128 * j + 128].reshape(n, p, 128)
            blocks.append(jnp.pad(block, ((0, 0), (0, up16(p) - p), (0, 0))))
    slabs = jnp.repeat(vec.reshape(8, D // 128, 128).transpose(1, 0, 2), n // (D // 128), axis=0)
    full = jnp.concatenate(blocks + [slabs, slabs], axis=1)
    return full.reshape(bands, 2, full.shape[1], 128).transpose(1, 0, 2, 3)


def local(bands, node_state, edge_state, send_rows, edge_sender, edge_receiver, edge_count, edge_w1, edge_b1, edge_w2,
          edge_gain, edge_shift, node_w1, node_b1, node_w2, node_gain, node_shift, node_cot, edge_cot):
    parts = tuple(m.shape[0] for m in (edge_w1, edge_w2, node_w1, node_w2))
    width = edge_b1.shape[0]
    vecs = (edge_b1, edge_gain, edge_shift, node_b1, node_gain, node_shift)
    sel = send_rows[0].T
    got, inc = gather_weights(bands, edge_w1, edge_w2, node_w1, node_w2, sel, node_state, *vecs)
    node_out, edge_out, node_part, edge_grad, packed, msgs = core(
        bands, parts, edge_count, edge_sender, edge_receiver, edge_state, edge_cot, node_state, node_cot, got, inc)
    red, arrived = reduce_grads(bands, packed, msgs)
    node_grad, gw1, gw2, gnw1, gnw2, *gv = finish(bands, parts, width, red, arrived, sel, node_part)
    return (node_out, edge_out, node_grad, edge_grad, gw1, gv[0], gw2, gv[1], gv[2], gnw1, gv[3], gnw2, gv[4], gv[5])


def solution(mesh):
    two, one, three = P(AXES, None), P(AXES), P(AXES, None, None)
    in_specs = (two, two, three, one, one, one, two, one, two, one, one, two, one, two, one, one, two, two)
    out_specs = (two, two, two, two, two, one, two, one, one, two, one, two, one, one)
    return jax.shard_map(functools.partial(local, mesh.shape["band"]), mesh=mesh, in_specs=in_specs,
                         out_specs=out_specs, check_vma=False)
```

```python
import functools
import jax, jax.numpy as jnp
from jax import lax
from jax.experimental import pallas as pl
from jax.experimental.pallas import tpu as pltpu
from jax.sharding import PartitionSpec as P

F32 = jnp.float32
BF = jnp.bfloat16
AXES = ("band", "sub")
MESH = pl.DeviceIdType.MESH
LINE = 4


def up16(n):
    return -(-n // 16) * 16


def layout(parts):
    spots, at = [], 0
    for p in parts:
        spots.append(at)
        at += 4 * up16(p)
    return spots, at


class Place:
    def __init__(self, bands):
        self.bands = bands
        self.quads = bands // LINE
        band, self.c = lax.axis_index("band"), lax.axis_index("sub")
        self.a, self.q = band // LINE, band % LINE
        x, y = self.q % 2, self.q // 2
        self.qx = self.q + 1 - 2 * x
        self.qy = self.q + 2 - 4 * y
        self.qd = 3 - self.q
        self.me = band * 2 + self.c
        self.devices = bands * 2

    def dev(self, a, q, c):
        return (a * LINE + q, c)

    def idx(self, a, q, c):
        return (a * LINE + q) * 2 + c

    def other_a(self, k):
        return (self.a + k) % self.quads


def greet_all(pos):
    sem = pltpu.get_barrier_semaphore()

    @pl.loop(1, pos.devices)
    def _(k):
        t = (pos.me + k) % pos.devices
        pl.semaphore_signal(sem, inc=1, device_id=(t // 2, t % 2), device_id_type=MESH)

    return lambda: pl.semaphore_wait(sem, pos.devices - 1)


def gather_kernel(bands, parts, *refs):
    inputs, refs = refs[:12], refs[12:]
    buf, inc, mine, node, wide, outg, recv, half, send_z, send_q, send_h, send_s, a_recv, a_send, own_sem, in_sem, *held = refs
    pos = Place(bands)
    spots, tail = layout(parts)
    rows = mine.shape[0]
    cut = up16(rows // 2)
    me, c, a, q, line = pos.me, pos.c, pos.a, pos.q, pos.quads
    w1_ref, w2_ref, nw1_ref, nw2_ref, sel_ref = held[:5]
    vecs = held[5:]
    D = node.shape[1]
    slots, peers = sel_ref.shape
    met_all = greet_all(pos)
    fetched = [pltpu.make_async_copy(h, v, in_sem.at[k]) for k, (h, v) in enumerate(zip(inputs, held))]
    node_copy = pltpu.make_async_copy(inputs[11], node, own_sem.at[0])
    for cp in fetched:
        cp.start()
    node_copy.start()
    for cp in fetched:
        cp.wait()
    for m, p, o in zip((w1_ref, w2_ref, nw1_ref, nw2_ref), parts, spots):
        for j in range(4):
            mine[o + j * up16(p):o + j * up16(p) + p, :] = m[:, 128 * j:128 * j + 128]
    width = vecs[0].shape[0]
    group = 128 // width
    lanes = lax.broadcasted_iota(jnp.int32, (1, 128), 1)
    wide[...] = jnp.zeros_like(wide)
    for k in range(6):
        val = jnp.concatenate([vecs[k][...].astype(F32).reshape(1, width)] * group, axis=1)
        wide[k:k + 1, :] = jnp.where(lanes // width == me % group, val, 0.0)
    mine[tail:tail + 16, :] = wide[...].astype(BF)
    own_copy = pltpu.make_async_copy(mine, buf.at[me], own_sem.at[1])
    own_copy.start()
    met_all()

    WHOLE = pl.ds(0, rows)
    FIRST, LAST = pl.ds(0, cut), pl.ds(cut, rows - cut)

    def push(ak, qk, part, sem_send, sem_recv, target, own=False):
        src = pos.idx(ak, qk, c)
        return pltpu.make_async_remote_copy(
            src_ref=mine.at[part] if own else buf.at[src, part], dst_ref=buf.at[src, part],
            send_sem=sem_send, recv_sem=sem_recv, device_id=target, device_id_type=MESH)

    def up(ak, own=False):
        return push(ak, q, WHOLE, send_z.at[0, ak], recv.at[pos.idx(ak, q, c)], pos.dev(a + 1, q, c), own)

    def down(ak, own=False):
        return push(ak, q, WHOLE, send_z.at[1, ak], recv.at[pos.idx(ak, q, c)], pos.dev(a - 1, q, c), own)

    def to_x(ak, own=False):
        return push(ak, q, WHOLE, send_q.at[0, ak], recv.at[pos.idx(ak, q, c)], pos.dev(a, pos.qx, c), own)

    def to_y(ak, own=False):
        return push(ak, q, WHOLE, send_q.at[1, ak], recv.at[pos.idx(ak, q, c)], pos.dev(a, pos.qy, c), own)

    def x_to_y(ak):
        return push(ak, pos.qx, FIRST, send_h.at[0, ak], half.at[0, ak], pos.dev(a, pos.qy, c))

    def y_to_x(ak):
        return push(ak, pos.qy, LAST, send_h.at[1, ak], half.at[1, ak], pos.dev(a, pos.qx, c))

    def sibling(ak, qk, own=False):
        return push(ak, qk, WHOLE, send_s.at[ak * LINE + qk], recv.at[pos.idx(ak, qk, c)], pos.dev(a, q, 1 - c), own)

    def arrive(ak, qk, ck=None):
        src = pos.idx(ak, qk, c if ck is None else ck)
        pltpu.make_async_remote_copy(src_ref=buf.at[src], dst_ref=buf.at[src], send_sem=send_s.at[0],
                                     recv_sem=recv.at[src], device_id=pos.dev(a, q, 1 - c),
                                     device_id_type=MESH).wait_recv()

    def exchange(t):
        return pltpu.make_async_remote_copy(src_ref=outg.at[t], dst_ref=inc.at[me], send_sem=a_send.at[t],
                                            recv_sem=a_recv.at[me], device_id=(t // 2, t % 2), device_id_type=MESH)

    pl.when(a + 1 < line)(lambda: up(a, True).start())
    pl.when(a > 0)(lambda: down(a, True).start())
    to_x(a, True).start()
    to_y(a, True).start()
    sibling(a, q, True).start()

    hot = slot_onehot(sel_ref[...], node.shape[0])
    node_copy.wait()
    picked = jnp.dot(hot, node[...], preferred_element_type=F32)
    outg[:, 0:slots, :] = picked[:, 0:D // 2].reshape(peers, slots, D // 2).astype(BF)
    outg[:, slots:, :] = picked[:, D // 2:].reshape(peers, slots, D // 2).astype(BF)
    msg_copy = pltpu.make_async_copy(outg.at[me], inc.at[me], own_sem.at[2])
    msg_copy.start()

    def along(ak, below):
        arrive(ak, q)
        if below:
            pl.when(a + 1 < line)(lambda: up(ak).start())
        else:
            pl.when(a > 0)(lambda: down(ak).start())
        to_x(ak).start()
        to_y(ak).start()
        sibling(ak, q).start()

    def square(ak):
        arrive(ak, pos.qx)
        x_to_y(ak).start()
        sibling(ak, pos.qx).start()
        arrive(ak, pos.qy)
        y_to_x(ak).start()
        sibling(ak, pos.qy).start()

    def both(k, what):
        pl.when(a - k >= 0)(lambda: what(a - k, True))
        pl.when(a + k < line)(lambda: what(a + k, False))

    for k in range(1, line):
        both(k, along)
        if k == 1:
            square(a)
        else:
            both(k - 1, lambda ak, below: square(ak))
    both(line - 1, lambda ak, below: square(ak))

    @pl.loop(1, pos.devices)
    def _(k):
        exchange((me + k) % pos.devices).start()

    for k in range(line):
        ak = pos.other_a(k)
        for part, at in ((FIRST, 0), (LAST, 1)):
            ref = buf.at[pos.idx(ak, pos.qd, c), part]
            pltpu.make_async_remote_copy(src_ref=ref, dst_ref=ref, send_sem=send_s.at[0], recv_sem=half.at[at, ak],
                                         device_id=pos.dev(a, q, 1 - c), device_id_type=MESH).wait_recv()
        sibling(ak, pos.qd).start()

    @pl.loop(1, pos.devices)
    def _(k):
        t = (me + k) % pos.devices
        pltpu.make_async_remote_copy(src_ref=outg.at[t], dst_ref=inc.at[t], send_sem=a_send.at[t],
                                     recv_sem=a_recv.at[t], device_id=(t // 2, t % 2), device_id_type=MESH).wait()

    own_copy.wait()
    msg_copy.wait()
    for k in range(line):
        ak = pos.other_a(k)
        pl.when((a + 1 < line) & (ak <= a))(lambda: up(ak).wait_send())
        pl.when((a > 0) & (ak >= a))(lambda: down(ak).wait_send())
        for cp in (to_x(ak), to_y(ak), x_to_y(ak), y_to_x(ak)):
            cp.wait_send()
        for qk in (q, pos.qx, pos.qy, pos.qd):
            sibling(ak, qk).wait_send()
            arrive(ak, qk, 1 - c)


def gather_weights(bands, w1, w2, nw1, nw2, sel, node, *vecs):
    parts = tuple(m.shape[0] for m in (w1, w2, nw1, nw2))
    rows = layout(parts)[1] + 16
    n, line = bands * 2, bands // LINE
    D = node.shape[1]
    slots, peers = sel.shape
    H = pl.BlockSpec(memory_space=pl.ANY)
    inputs = (w1, w2, nw1, nw2, sel, *vecs)
    sds, sem, vm = jax.ShapeDtypeStruct, pltpu.SemaphoreType.DMA, pltpu.VMEM
    msgs = (peers, 2 * slots, D // 2)
    return pl.pallas_call(
        functools.partial(gather_kernel, bands, parts),
        out_shape=[sds((n, rows, 128), BF), sds(msgs, BF)],
        in_specs=[H] * 12, out_specs=[H, H],
        scratch_shapes=[
            vm((rows, 128), BF), vm(node.shape, BF), vm((16, 128), F32), vm(msgs, BF),
            sem((n,)), sem((2, line)), sem((2, line)), sem((2, line)), sem((2, line)), sem((bands,)),
            sem((n,)), sem((n,)), sem((3,)), sem((11,)), *[vm(m.shape, m.dtype) for m in inputs]],
        compiler_params=pltpu.CompilerParams(collective_id=0, has_side_effects=True, vmem_limit_bytes=63 * 2**20),
        name="gather_weights",
    )(*inputs, node)


def reduce_kernel(bands, p_ref, msg_ref, red_ref, arr_ref, own, sib, xa, yb, ya, xb, zin,
                  own_sem, sib_recv, x1, y1, y2, x2, z_recv, send, a_recv, a_send, kept_sem):
    pos = Place(bands)
    me, c, a, q = pos.me, pos.c, pos.a, pos.q
    rows = own.shape[1]
    cut = up16(rows // 2)
    A, B = pl.ds(0, cut), pl.ds(cut, rows - cut)
    count = [0]
    started = []

    def push(src, dst, sem, target):
        cp = pltpu.make_async_remote_copy(src_ref=src, dst_ref=dst, send_sem=send.at[count[0]], recv_sem=sem,
                                          device_id=target, device_id_type=MESH)
        count[0] += 1
        cp.start()
        started.append(cp)

    def wait(dst, sem):
        pltpu.make_async_remote_copy(src_ref=dst, dst_ref=dst, send_sem=send.at[0], recv_sem=sem,
                                     device_id=pos.dev(a, q, 1 - c), device_id_type=MESH).wait_recv()

    order = [pos.other_a(k) for k in range(1, pos.quads)] + [a]
    square = [pl.ds(ak * LINE, LINE) for ak in order]
    met_all = greet_all(pos)
    kept = pltpu.make_async_copy(msg_ref.at[me], arr_ref.at[me], kept_sem)
    mine = []
    for ak, sq in zip(order, square):
        cp = pltpu.make_async_copy(p_ref.at[c, sq], own.at[sq], own_sem.at[ak])
        cp.start()
        mine.append(cp)
    kept.start()
    met_all()
    for ak, sq in zip(order, square):
        push(p_ref.at[1 - c, sq], sib.at[sq], sib_recv.at[ak], pos.dev(a, q, 1 - c))

    def exchange(t):
        return pltpu.make_async_remote_copy(src_ref=msg_ref.at[t], dst_ref=arr_ref.at[me], send_sem=a_send.at[t],
                                            recv_sem=a_recv.at[me], device_id=(t // 2, t % 2), device_id_type=MESH)

    @pl.loop(1, pos.devices)
    def _(k):
        exchange((me + k) % pos.devices).start()

    to_x, to_y = pos.dev(a, pos.qx, c), pos.dev(a, pos.qy, c)

    def add(ref, idx, other):
        ref[idx] = (ref[idx].astype(F32) + other.astype(F32)).astype(BF)

    def first(k):
        ak, sq = order[k], square[k]
        at = ak * LINE
        mine[k].wait()
        wait(sib.at[sq], sib_recv.at[ak])
        own[sq] = (own[sq].astype(F32) + sib[sq].astype(F32)).astype(BF)
        push(own.at[at + pos.qx, A], xa.at[ak, 0], x1.at[ak, 0], to_x)
        push(own.at[at + pos.qy, B], yb.at[ak, 0], y1.at[ak, 0], to_y)
        push(own.at[at + pos.qd, A], xa.at[ak, 1], x1.at[ak, 1], to_x)
        push(own.at[at + pos.qd, B], yb.at[ak, 1], y1.at[ak, 1], to_y)

    def second(k):
        ak = order[k]
        at = ak * LINE
        wait(xa.at[ak, 1], x1.at[ak, 1])
        add(own, (at + pos.qy, A), xa[ak, 1])
        push(own.at[at + pos.qy, A], ya.at[ak], y2.at[ak], to_y)
        wait(yb.at[ak, 1], y1.at[ak, 1])
        add(own, (at + pos.qx, B), yb[ak, 1])
        push(own.at[at + pos.qx, B], xb.at[ak], x2.at[ak], to_x)

    def third(k):
        ak = order[k]
        at = ak * LINE
        wait(xa.at[ak, 0], x1.at[ak, 0])
        wait(yb.at[ak, 0], y1.at[ak, 0])
        wait(ya.at[ak], y2.at[ak])
        wait(xb.at[ak], x2.at[ak])
        top = own[at + q, A].astype(F32) + xa[ak, 0].astype(F32) + ya[ak].astype(F32)
        low = own[at + q, B].astype(F32) + yb[ak, 0].astype(F32) + xb[ak].astype(F32)
        if k < pos.quads - 1:
            own[at + q, A] = top.astype(BF)
            own[at + q, B] = low.astype(BF)
            push(own.at[at + q], zin.at[a], z_recv.at[a], pos.dev(ak, q, c))
        else:
            red_ref[A, :] = top
            red_ref[B, :] = low

    n = pos.quads
    first(0)
    if n > 1:
        first(1)
    for k in range(n):
        second(k)
        if k + 2 < n:
            first(k + 2)
        if k >= 1:
            third(k - 1)
    third(n - 1)
    for k in range(n - 1):
        ak = order[k]
        wait(zin.at[ak], z_recv.at[ak])
        red_ref[...] += zin[ak].astype(F32)

    @pl.loop(1, pos.devices)
    def _(k):
        t = (me + k) % pos.devices
        pltpu.make_async_remote_copy(src_ref=msg_ref.at[t], dst_ref=arr_ref.at[t], send_sem=a_send.at[t],
                                     recv_sem=a_recv.at[t], device_id=(t // 2, t % 2), device_id_type=MESH).wait()

    kept.wait()
    for cp in started:
        cp.wait_send()


def reduce_grads(bands, packed, msgs):
    rows = packed.shape[2]
    n = bands * 2
    quads = bands // LINE
    cut = up16(rows // 2)
    V = pl.BlockSpec(memory_space=pltpu.VMEM)
    sds = jax.ShapeDtypeStruct
    sem = pltpu.SemaphoreType.DMA
    return pl.pallas_call(
        functools.partial(reduce_kernel, bands),
        out_shape=[sds((rows, 128), F32), sds(msgs.shape, BF)],
        in_specs=[pl.BlockSpec(memory_space=pl.ANY)] * 2, out_specs=[V, V],
        scratch_shapes=[
            pltpu.VMEM((bands, rows, 128), BF), pltpu.VMEM((bands, rows, 128), BF),
            pltpu.VMEM((quads, 2, cut, 128), BF), pltpu.VMEM((quads, 2, rows - cut, 128), BF),
            pltpu.VMEM((quads, cut, 128), BF), pltpu.VMEM((quads, rows - cut, 128), BF),
            pltpu.VMEM((quads, rows, 128), BF),
            sem((quads,)), sem((quads,)), sem((quads, 2)), sem((quads, 2)), sem((quads,)), sem((quads,)), sem((quads,)),
            sem((8 * quads,)), sem((n,)), sem((n,)), sem],
        compiler_params=pltpu.CompilerParams(collective_id=1, has_side_effects=True, vmem_limit_bytes=63 * 2**20),
        name="reduce_grads",
    )(packed, msgs)


def finish_kernel(bands, parts, red_ref, arr_ref, sel_ref, part_ref, ngrad_ref, w1_ref, w2_ref, nw1_ref, nw2_ref, *vecs):
    me = lax.axis_index("band") * 2 + lax.axis_index("sub")
    spots, tail = layout(parts)
    for o_ref, p, o in zip((w1_ref, w2_ref, nw1_ref, nw2_ref), parts, spots):
        for j in range(4):
            o_ref[:, 128 * j:128 * j + 128] = red_ref[o + j * up16(p):o + j * up16(p) + p, :]
    width = vecs[0].shape[0]
    group = 128 // width
    slab = red_ref[tail:tail + 8, :]
    got = slab[:, 0:width]
    for g in range(1, group):
        got = jnp.where(me % group == g, slab[:, g * width:(g + 1) * width], got)
    for k, v_ref in enumerate(vecs):
        v_ref[...] = got[k]
    slots, peers = sel_ref.shape
    S = peers * slots
    N, D = part_ref.shape
    hot = slot_onehot(sel_ref[...], N)
    arrived = jnp.concatenate([arr_ref[:, 0:slots, :].astype(F32).reshape(S, D // 2),
                               arr_ref[:, slots:, :].astype(F32).reshape(S, D // 2)], axis=1).astype(BF)
    ngrad_ref[...] = part_ref[...] + lax.dot_general(hot, arrived, (((0,), (0,)), ((), ())), preferred_element_type=F32)


def slot_onehot(ids, nodes):
    slots, peers = ids.shape
    S = peers * slots
    pick = (lax.broadcasted_iota(jnp.int32, (S, peers), 0) // slots
            == lax.broadcasted_iota(jnp.int32, (S, peers), 1)).astype(BF)
    low = dot_t(pick, (ids % 256).astype(BF))
    high = dot_t(pick, (ids // 256).astype(BF))
    mine = lax.broadcasted_iota(jnp.int32, (S, slots), 0) % slots == lax.broadcasted_iota(jnp.int32, (S, slots), 1)
    col = jnp.sum(jnp.where(mine, low + 256.0 * high, 0.0), axis=1, keepdims=True)
    return (col == lax.broadcasted_iota(jnp.int32, (S, nodes), 1).astype(F32)).astype(BF)


def finish(bands, parts, width, red, arrived, sel, part):
    V = pl.BlockSpec(memory_space=pltpu.VMEM)
    sds = jax.ShapeDtypeStruct
    D = part.shape[1]
    outs = [sds(part.shape, F32)] + [sds((p, D), F32) for p in parts] + [sds((width,), F32)] * 6
    return pl.pallas_call(
        functools.partial(finish_kernel, bands, parts),
        out_shape=outs, in_specs=[V] * 4, out_specs=[V] * len(outs),
        compiler_params=pltpu.CompilerParams(vmem_limit_bytes=63 * 2**20),
        name="finish",
    )(red, arrived, sel, part)


EPS = 1e-5


def dot(a, b):
    return jnp.dot(a, b, preferred_element_type=F32)


def dot_t(a, b):
    return lax.dot_general(a, b, (((1,), (1,)), ((), ())), preferred_element_type=F32)


def t_dot(a, b):
    return lax.dot_general(a, b, (((0,), (0,)), ((), ())), preferred_element_type=F32)


def rowmean(v):
    return jnp.sum(v, axis=1, keepdims=True) * (1.0 / v.shape[1])


def onehot_cols(ids, width):
    rows = ids.shape[1]
    wide = jnp.broadcast_to(ids, (128, rows)).T
    off = wide - lax.broadcasted_iota(jnp.int32, (rows, 128), 1)
    return jnp.concatenate([jnp.where(off == 128 * j, 1.0, 0.0).astype(BF) for j in range(width // 128)], axis=1)


def onehot_rows(ids, height):
    return jnp.where(lax.broadcasted_iota(jnp.int32, (height, ids.shape[1]), 0) == ids, 1.0, 0.0).astype(BF)


def fold8(v):
    return jnp.sum(v.reshape(v.shape[0] // 8, 8, v.shape[1]), axis=0)


def core_kernel(nb, R, sub, parts, fast, count_ref, sid_ref, rid_ref, e_ref, cot_ref, node_ref, ncot_ref, *refs):
    (got_ref, inc_ref), refs = (refs[:2], refs[2:]) if fast else ((None, None), refs)
    weights, refs = ((), refs) if fast else (refs[:6], refs[6:])
    nout_ref, eout_ref, ngrad_ref, egrad_ref, msg_ref, *refs = refs
    outs, refs = (refs[:1], refs[1:]) if fast else (refs[:5], refs[5:])
    if fast:
        pack_ref, stage, refs = outs[0], refs[0], refs[1:]
        outs = [stage]
    weights, refs = (refs[:6], refs[6:]) if fast else (weights, refs)
    w1_ref, w2_ref, nw1_ref, nw2_ref, vec_ref, snd_ref = weights
    wcat, w2h, hid_s, slope_s, nrm_s, scale_s, gath, dg, gacc, g2acc, gain_acc, shift_acc, gvec, msg_s, dpre_s, w1t, sem = refs
    i = pl.program_id(0)
    D = e_ref.shape[1]
    S = snd_ref.shape[0]
    N = node_ref.shape[0]
    count = count_ref[0]
    spots, tail = layout(parts)
    n = 3 * D // parts[0]

    def emit(m, first, value):
        if not fast:
            outs[m][first:first + value.shape[0], :] = value
            return
        p, o = parts[m], spots[m]
        lo, hi = first, first + value.shape[0]
        for d in range(lo // p, -(-hi // p)):
            a, b = max(lo, d * p), min(hi, (d + 1) * p)
            for j in range(D // 128):
                at = o + j * p + a - d * p
                outs[0][d % 2, d // 2, at:at + b - a, :] = value[a - lo:b - lo, 128 * j:128 * j + 128].astype(BF)

    RANGES = (pl.ds(0, spots[2]), pl.ds(spots[2], tail - spots[2]), pl.ds(tail, 16))

    def fetch(k):
        return pltpu.make_async_copy(got_ref.at[:, :, RANGES[k]], stage.at[:, :, RANGES[k]], sem.at[k])

    def deliver(k):
        return pltpu.make_async_copy(stage.at[:, :, RANGES[k]], pack_ref.at[:, :, RANGES[k]], sem.at[k])

    def unpack(mats):
        @pl.loop(0, n)
        def _(d):
            for w_ref, p, o in mats:
                for j in range(D // 128):
                    w_ref[pl.ds(pl.multiple_of(d * p, p), p), 128 * j:128 * j + 128] = \
                        stage[d // (n // 2), d % (n // 2), o + j * p:o + j * p + p, :]

    def unpack_vectors():
        group = n // (D // 128)
        for g in range(D // 128):
            tiles = [stage[d // (n // 2), d % (n // 2), tail:tail + 16, :].astype(F32)
                     for d in range(g * group, (g + 1) * group)]
            vec_ref[:, 128 * g:128 * g + 128] = functools.reduce(jnp.add, tiles).astype(BF)
        slots = inc_ref.shape[1] // 2
        snd_ref[:, 0:D // 2] = inc_ref[:, 0:slots, :].astype(F32).reshape(S, D // 2).astype(BF)
        snd_ref[:, D // 2:] = inc_ref[:, slots:, :].astype(F32).reshape(S, D // 2).astype(BF)

    @pl.when(i == 0)
    def _():
        if fast:
            for k in range(3):
                fetch(k).start()
            fetch(0).wait()
            unpack(list(zip((w1_ref, w2_ref), parts, spots))[:2])
            fetch(2).wait()
            unpack_vectors()
        b1 = vec_ref[0:1, :].astype(F32)
        wcat[0:D, :] = w1_ref[0:D, :] * 0.5
        wcat[D:D + S, :] = (dot(snd_ref[...], w1_ref[D:2 * D, :]) * 0.5).astype(BF)
        wcat[D + S:, :] = ((dot(node_ref[...], w1_ref[2 * D:, :]) + b1) * 0.5).astype(BF)
        w2h[...] = (w2_ref[...].astype(F32) * 0.5).T.astype(BF)
        w1t[...] = w1_ref[0:D, :].astype(F32).T.astype(BF)
        gath[...] = jnp.zeros_like(gath)
        gacc[...] = jnp.zeros_like(gacc)
        g2acc[...] = jnp.zeros_like(g2acc)
        gain_acc[...] = jnp.zeros_like(gain_acc)
        shift_acc[...] = jnp.zeros_like(shift_acc)
        scale_s[...] = jnp.zeros_like(scale_s)

    gain = vec_ref[1:2, :].astype(F32)
    shift = vec_ref[2:3, :].astype(F32)
    blk = lax.rem(i, nb)
    live_blk = blk * R < count
    subs = R // sub

    def ids(r):
        at = blk * subs + r
        pos = at * sub + lax.broadcasted_iota(jnp.int32, (1, sub), 1)
        sid = sid_ref[pl.ds(at, 1), :]
        rid = jnp.where(pos < count, rid_ref[pl.ds(at, 1), :], -1)
        return sid, rid

    def live_col(r):
        return (blk * subs + r) * sub + lax.broadcasted_iota(jnp.int32, (sub, 1), 0) < count

    def lane_is(at):
        return lax.broadcasted_iota(jnp.int32, (sub, 128), 1) == at

    @pl.when((i < nb) & live_blk)
    def _():
        here = [slice(r * sub, (r + 1) * sub) for r in range(subs)]
        rows = [pl.ds(pl.multiple_of((blk * subs + r) * sub, sub), sub) for r in range(subs)]
        idx = [ids(r) for r in range(subs)]
        h, proj = [None] * subs, [None] * subs

        def a1(r):
            sid, rid = idx[r]
            x = jnp.concatenate([e_ref[here[r], :], onehot_cols(sid, S), onehot_cols(rid, N)], axis=1)
            h[r] = dot(x, wcat[...])

        def a2(r):
            v = h[r]
            a = 1.0 + jnp.tanh(v)
            hid = v * a
            slope_s[rows[r], :] = (a + hid * (2.0 - a)).astype(BF)
            hid_s[rows[r], :] = hid.astype(BF)

        def b1(r):
            proj[r] = dot(hid_s[rows[r], :], w2_ref[...])

        def b2(r):
            live = live_col(r)
            c = proj[r] - rowmean(proj[r])
            s = lax.rsqrt(rowmean(c * c) + EPS)
            s = jnp.where(live, s, 0.0)
            scale_s[...] = jnp.where(lane_is(blk * subs + r), s, scale_s[...])
            nrm = c * s
            nrm_s[rows[r], :] = nrm.astype(BF)
            msg = nrm * gain + shift
            eout_ref[here[r], :] = (e_ref[here[r], :].astype(F32) + msg).astype(BF)
            msg_s[here[r], :] = msg.astype(BF)

        def c1(first, last):
            rid = jnp.concatenate([idx[r][1] for r in range(first, last)], axis=1)
            gath[...] += dot(onehot_rows(rid, N), msg_s[first * sub:last * sub, :])

        for t in range(subs + 2):
            if t < subs:
                a1(t)
            if 2 <= t:
                b2(t - 2)
            if 1 <= t < subs + 1:
                b1(t - 1)
            if t < subs:
                a2(t)
        c1(0, subs)

    @pl.when((i < nb) & live_blk & ((blk + 1) * R > count))
    def _():
        live = blk * R + lax.broadcasted_iota(jnp.int32, (R, 1), 0) < count
        eout_ref[...] = jnp.where(live, eout_ref[...].astype(F32), e_ref[...].astype(F32)).astype(BF)

    @pl.when((i < nb) & jnp.logical_not(live_blk))
    def _():
        eout_ref[...] = e_ref[...]

    @pl.when(i == nb - 1)
    def _():
        if fast:
            fetch(1).wait()
            unpack(list(zip((nw1_ref, nw2_ref), parts[2:], spots[2:])))
        nb1 = vec_ref[3:4, :].astype(F32)
        ngain = vec_ref[4:5, :].astype(F32)
        nshift = vec_ref[5:6, :].astype(F32)
        node = node_ref[...]
        g16 = gath[...].astype(BF)
        pre = dot(node, nw1_ref[0:D, :]) + dot(g16, nw1_ref[D:, :]) + nb1
        sig = 0.5 + 0.5 * jnp.tanh(0.5 * pre)
        hid = (pre * sig).astype(BF)
        proj = dot(hid, nw2_ref[...])
        c = proj - rowmean(proj)
        s = lax.rsqrt(rowmean(c * c) + EPS)
        nrm = c * s
        nout_ref[...] = (node.astype(F32) + nrm * ngain + nshift).astype(BF)
        up = ncot_ref[...].astype(F32)
        gvec[4:5, :] = jnp.sum(up * nrm, axis=0, keepdims=True)
        gvec[5:6, :] = jnp.sum(up, axis=0, keepdims=True)
        g = up * ngain
        dproj = (s * (g - rowmean(g) - nrm * rowmean(g * nrm))).astype(BF)
        emit(3, 0, t_dot(hid, dproj))
        dpre = dot_t(dproj, nw2_ref[...]) * (sig * (1.0 + pre * (1.0 - sig)))
        dpre16 = dpre.astype(BF)
        emit(2, 0, t_dot(node, dpre16))
        emit(2, D, t_dot(g16, dpre16))
        gvec[3:4, :] = jnp.sum(dpre16.astype(F32), axis=0, keepdims=True)
        ngrad_ref[...] = up + dot_t(dpre16, nw1_ref[0:D, :])
        dg[...] = dot_t(dpre16, nw1_ref[D:, :]).astype(BF)
        if fast:
            deliver(1).start()

    @pl.when((i >= nb) & live_blk)
    def _():
        here = [slice(r * sub, (r + 1) * sub) for r in range(subs)]
        rows = [pl.ds(pl.multiple_of((blk * subs + r) * sub, sub), sub) for r in range(subs)]
        every = pl.ds(pl.multiple_of(blk * R, R), R)
        idx = [ids(r) for r in range(subs)]
        came, dhid, back = [None] * subs, [None] * subs, [None] * subs

        def a1(r):
            came[r] = dot(onehot_cols(idx[r][1], N), dg[...])

        def a2(r):
            dm = jnp.where(live_col(r), cot_ref[here[r], :].astype(F32), 0.0) + came[r]
            nrm = nrm_s[rows[r], :].astype(F32)
            p = dm * nrm
            gain_acc[...] += fold8(p)
            shift_acc[...] += fold8(dm)
            g = dm * gain
            m1 = rowmean(g)
            m2 = rowmean(p * gain)
            s = jnp.sum(jnp.where(lane_is(blk * subs + r), scale_s[...], 0.0), axis=1, keepdims=True)
            msg_s[here[r], :] = (s * (g - m1 - nrm * m2)).astype(BF)

        def b1(r):
            dhid[r] = dot(msg_s[here[r], :], w2h[...])

        def b2(r):
            dpre_s[here[r], :] = (dhid[r] * slope_s[rows[r], :].astype(F32)).astype(BF)

        def c1(r):
            back[r] = dot(dpre_s[here[r], :], w1t[...])

        def c2(r):
            egrad_ref[here[r], :] = cot_ref[here[r], :].astype(F32) + back[r]

        for t in range(subs + 3):
            if t < subs:
                a1(t)
            if t >= 3:
                c2(t - 3)
            if 2 <= t < subs + 2:
                b2(t - 2)
            if 1 <= t < subs + 1:
                b1(t - 1)
            if t < subs:
                a2(t)
            if 2 <= t < subs + 2:
                c1(t - 2)
        g2acc[...] += t_dot(hid_s[every, :], msg_s[...])
        sids = jnp.concatenate([v[0] for v in idx], axis=1)
        rids = jnp.concatenate([v[1] for v in idx], axis=1)
        gacc[0:D, :] += t_dot(e_ref[...], dpre_s[...])
        gacc[D:D + S, :] += dot(onehot_rows(sids, S), dpre_s[...])
        gacc[D + S:, :] += dot(onehot_rows(rids, N), dpre_s[...])

    @pl.when((i >= nb) & jnp.logical_not(live_blk))
    def _():
        egrad_ref[...] = cot_ref[...].astype(F32)

    @pl.when(i == 2 * nb - 1)
    def _():
        us = gacc[D:D + S, :].astype(BF)
        ur = gacc[D + S:, :].astype(BF)
        emit(0, 0, gacc[0:D, :])
        emit(0, D, t_dot(snd_ref[...], us))
        emit(0, 2 * D, t_dot(node_ref[...], ur))
        emit(1, 0, g2acc[...])
        ngrad_ref[...] += dot_t(ur, w1_ref[2 * D:, :])
        sgrad = dot_t(us, w1_ref[D:2 * D, :])
        peers, slots = msg_ref.shape[0], msg_ref.shape[1] // 2
        msg_ref[:, 0:slots, :] = sgrad[:, 0:D // 2].reshape(peers, slots, D // 2).astype(BF)
        msg_ref[:, slots:, :] = sgrad[:, D // 2:].reshape(peers, slots, D // 2).astype(BF)
        gvec[0:1, :] = jnp.sum(gacc[D + S:, :], axis=0, keepdims=True)
        gvec[1:2, :] = jnp.sum(gain_acc[...], axis=0, keepdims=True)
        gvec[2:3, :] = jnp.sum(shift_acc[...], axis=0, keepdims=True)
        gvec[6:8, :] = jnp.zeros((2, D), F32)
        if not fast:
            outs[4][...] = gvec[...]
        else:
            for d in range(n):
                g = d * D // n // 128
                stage[d % 2, d // 2, tail:tail + 16, :] = jnp.concatenate(
                    [gvec[:, 128 * g:128 * g + 128]] * 2, axis=0).astype(BF)
            deliver(0).start()
            deliver(2).start()
            for k in range(3):
                deliver(k).wait()


def core(bands, parts, count, sid, rid, e, cot, node, ncot, got, inc, sub=128):
    E, D = e.shape
    S, N = inc.shape[0] * inc.shape[1] // 2, node.shape[0]
    R = 1024 if S <= 256 else 512
    nb = E // R
    V, H = pl.BlockSpec(memory_space=pltpu.VMEM), pl.BlockSpec(memory_space=pl.ANY)
    fb = pl.BlockSpec((R, D), lambda i: (jnp.minimum(i, nb - 1), 0))
    bb = pl.BlockSpec((R, D), lambda i: (jnp.maximum(i - nb, 0), 0))
    both = pl.BlockSpec((R, D), lambda i: (lax.rem(i, nb), 0))
    sds, vm = jax.ShapeDtypeStruct, pltpu.VMEM
    fast = all(p % 16 == 0 for p in parts)
    rows = layout(parts)[1] + 16
    if fast:
        weights, specs = (got.reshape(2, bands, rows, 128), inc), [H, V]
    else:
        weights, specs = unpack_weights(bands, parts, got, inc), [V] * 6
    grads = [(3 * D, D), (D, D), (2 * D, D), (D, D), (8, D)]
    outs = [sds((N, D), BF), sds((E, D), BF), sds((N, D), F32), sds((E, D), F32), sds(inc.shape, BF)]
    outs += [sds((2, bands, rows, 128), BF)] if fast else [sds(g, F32) for g in grads]
    *res, packed = res = pl.pallas_call(
        functools.partial(core_kernel, nb, R, sub, parts, fast),
        grid=(2 * nb,),
        in_specs=[pl.BlockSpec(memory_space=pltpu.SMEM), V, V, both, bb, V, V] + specs,
        out_specs=[V, fb, V, bb, V] + ([H] if fast else [V] * 5),
        out_shape=outs,
        scratch_shapes=([vm((2, bands, rows, 128), BF)] + [vm(g, BF) for g in grads[:4]] + [vm((16, D), BF), vm((S, D), BF)] if fast else []) + [
            vm((D + S + N, D), BF), vm((D, D), BF), vm((E, D), BF), vm((E, D), BF), vm((E, D), BF),
            vm((sub, 128), F32), vm((N, D), F32), vm((N, D), BF), vm((D + S + N, D), F32), vm((D, D), F32),
            vm((8, D), F32), vm((8, D), F32), vm((8, D), F32), vm((R, D), BF), vm((R, D), BF), vm((D, D), BF),
            pltpu.SemaphoreType.DMA((3,))],
        compiler_params=pltpu.CompilerParams(vmem_limit_bytes=63 * 2**20, dimension_semantics=("arbitrary",)),
        name="edge_node_core",
    )(count, sid.reshape(E // sub, sub), rid.reshape(E // sub, sub), e, cot, node, ncot, *weights)
    if not fast:
        packed = pack_grads(bands, parts, res[5:])
    return (*res[:4], packed, res[4])


def unpack_weights(bands, parts, got, inc):
    spots, tail = layout(parts)
    n, slots, D = 2 * bands, inc.shape[1] // 2, 2 * inc.shape[2]
    mats = []
    for p, o in zip(parts, spots):
        cols = [got[:, o + j * up16(p):o + j * up16(p) + p, :].reshape(n * p, 128) for j in range(D // 128)]
        mats.append(jnp.concatenate(cols, axis=1))
    slabs = got[:, tail:tail + 16, :].reshape(D // 128, -1, 16, 128).sum(axis=1)
    vec = slabs.transpose(1, 0, 2).reshape(16, D)
    snd = jnp.concatenate([inc[:, :slots].reshape(n * slots, D // 2), inc[:, slots:].reshape(n * slots, D // 2)], axis=1)
    return (*mats, vec, snd)


def pack_grads(bands, parts, grads):
    *mats, vec = [g.astype(BF) for g in grads]
    n, D = 2 * bands, vec.shape[1]
    blocks = []
    for m, p in zip(mats, parts):
        for j in range(D // 128):
            block = m[:, 128 * j:128 * j + 128].reshape(n, p, 128)
            blocks.append(jnp.pad(block, ((0, 0), (0, up16(p) - p), (0, 0))))
    slabs = jnp.repeat(vec.reshape(8, D // 128, 128).transpose(1, 0, 2), n // (D // 128), axis=0)
    full = jnp.concatenate(blocks + [slabs, slabs], axis=1)
    return full.reshape(bands, 2, full.shape[1], 128).transpose(1, 0, 2, 3)


def local(bands, node_state, edge_state, send_rows, edge_sender, edge_receiver, edge_count, edge_w1, edge_b1, edge_w2,
          edge_gain, edge_shift, node_w1, node_b1, node_w2, node_gain, node_shift, node_cot, edge_cot):
    parts = tuple(m.shape[0] for m in (edge_w1, edge_w2, node_w1, node_w2))
    width = edge_b1.shape[0]
    vecs = (edge_b1, edge_gain, edge_shift, node_b1, node_gain, node_shift)
    sel = send_rows[0].T
    got, inc = gather_weights(bands, edge_w1, edge_w2, node_w1, node_w2, sel, node_state, *vecs)
    node_out, edge_out, node_part, edge_grad, packed, msgs = core(
        bands, parts, edge_count, edge_sender, edge_receiver, edge_state, edge_cot, node_state, node_cot, got, inc)
    red, arrived = reduce_grads(bands, packed, msgs)
    node_grad, gw1, gw2, gnw1, gnw2, *gv = finish(bands, parts, width, red, arrived, sel, node_part)
    return (node_out, edge_out, node_grad, edge_grad, gw1, gv[0], gw2, gv[1], gv[2], gnw1, gv[3], gnw2, gv[4], gv[5])


def solution(mesh):
    two, one, three = P(AXES, None), P(AXES), P(AXES, None, None)
    in_specs = (two, two, three, one, one, one, two, one, two, one, one, two, one, two, one, one, two, two)
    out_specs = (two, two, two, two, two, one, two, one, one, two, one, two, one, one)
    return jax.shard_map(functools.partial(local, mesh.shape["band"]), mesh=mesh, in_specs=in_specs,
                         out_specs=out_specs, check_vma=False)
```

```python
import functools
import jax, jax.numpy as jnp
from jax import lax
from jax.experimental import pallas as pl
from jax.experimental.pallas import tpu as pltpu
from jax.sharding import PartitionSpec as P

F32 = jnp.float32
BF = jnp.bfloat16
AXES = ("band", "sub")
MESH = pl.DeviceIdType.MESH
LINE = 4


def up16(n):
    return -(-n // 16) * 16


def layout(parts):
    spots, at = [], 0
    for p in parts:
        spots.append(at)
        at += 4 * up16(p)
    return spots, at


class Place:
    def __init__(self, bands):
        self.bands = bands
        self.quads = bands // LINE
        band, self.c = lax.axis_index("band"), lax.axis_index("sub")
        self.a, self.q = band // LINE, band % LINE
        x, y = self.q % 2, self.q // 2
        self.qx = self.q + 1 - 2 * x
        self.qy = self.q + 2 - 4 * y
        self.qd = 3 - self.q
        self.me = band * 2 + self.c
        self.devices = bands * 2

    def dev(self, a, q, c):
        return (a * LINE + q, c)

    def idx(self, a, q, c):
        return (a * LINE + q) * 2 + c

    def other_a(self, k):
        return (self.a + k) % self.quads


def greet_all(pos):
    sem = pltpu.get_barrier_semaphore()

    @pl.loop(1, pos.devices)
    def _(k):
        t = (pos.me + k) % pos.devices
        pl.semaphore_signal(sem, inc=1, device_id=(t // 2, t % 2), device_id_type=MESH)

    return lambda: pl.semaphore_wait(sem, pos.devices - 1)


def gather_kernel(bands, parts, *refs):
    inputs, refs = refs[:12], refs[12:]
    buf, inc, mine, node, wide, outg, recv, half, send_z, send_q, send_h, send_s, a_recv, a_send, own_sem, in_sem, *held = refs
    pos = Place(bands)
    spots, tail = layout(parts)
    rows = mine.shape[0]
    cut = up16(rows // 2)
    me, c, a, q, line = pos.me, pos.c, pos.a, pos.q, pos.quads
    w1_ref, w2_ref, nw1_ref, nw2_ref, sel_ref = held[:5]
    vecs = held[5:]
    D = node.shape[1]
    slots, peers = sel_ref.shape
    met_all = greet_all(pos)
    fetched = [pltpu.make_async_copy(h, v, in_sem.at[k]) for k, (h, v) in enumerate(zip(inputs, held))]
    node_copy = pltpu.make_async_copy(inputs[11], node, own_sem.at[0])
    for cp in fetched:
        cp.start()
    node_copy.start()
    for cp in fetched:
        cp.wait()
    for m, p, o in zip((w1_ref, w2_ref, nw1_ref, nw2_ref), parts, spots):
        for j in range(4):
            mine[o + j * up16(p):o + j * up16(p) + p, :] = m[:, 128 * j:128 * j + 128]
    width = vecs[0].shape[0]
    group = 128 // width
    lanes = lax.broadcasted_iota(jnp.int32, (1, 128), 1)
    wide[...] = jnp.zeros_like(wide)
    for k in range(6):
        val = jnp.concatenate([vecs[k][...].astype(F32).reshape(1, width)] * group, axis=1)
        wide[k:k + 1, :] = jnp.where(lanes // width == me % group, val, 0.0)
    mine[tail:tail + 16, :] = wide[...].astype(BF)
    own_copy = pltpu.make_async_copy(mine, buf.at[me], own_sem.at[1])
    own_copy.start()
    met_all()

    WHOLE = pl.ds(0, rows)
    FIRST, LAST = pl.ds(0, cut), pl.ds(cut, rows - cut)

    def push(ak, qk, part, sem_send, sem_recv, target, own=False):
        src = pos.idx(ak, qk, c)
        return pltpu.make_async_remote_copy(
            src_ref=mine.at[part] if own else buf.at[src, part], dst_ref=buf.at[src, part],
            send_sem=sem_send, recv_sem=sem_recv, device_id=target, device_id_type=MESH)

    def up(ak, own=False):
        return push(ak, q, WHOLE, send_z.at[0, ak], recv.at[pos.idx(ak, q, c)], pos.dev(a + 1, q, c), own)

    def down(ak, own=False):
        return push(ak, q, WHOLE, send_z.at[1, ak], recv.at[pos.idx(ak, q, c)], pos.dev(a - 1, q, c), own)

    def to_x(ak, own=False):
        return push(ak, q, WHOLE, send_q.at[0, ak], recv.at[pos.idx(ak, q, c)], pos.dev(a, pos.qx, c), own)

    def to_y(ak, own=False):
        return push(ak, q, WHOLE, send_q.at[1, ak], recv.at[pos.idx(ak, q, c)], pos.dev(a, pos.qy, c), own)

    def x_to_y(ak):
        return push(ak, pos.qx, FIRST, send_h.at[0, ak], half.at[0, ak], pos.dev(a, pos.qy, c))

    def y_to_x(ak):
        return push(ak, pos.qy, LAST, send_h.at[1, ak], half.at[1, ak], pos.dev(a, pos.qx, c))

    def sibling(ak, qk, own=False):
        return push(ak, qk, WHOLE, send_s.at[ak * LINE + qk], recv.at[pos.idx(ak, qk, c)], pos.dev(a, q, 1 - c), own)

    def arrive(ak, qk, ck=None):
        src = pos.idx(ak, qk, c if ck is None else ck)
        pltpu.make_async_remote_copy(src_ref=buf.at[src], dst_ref=buf.at[src], send_sem=send_s.at[0],
                                     recv_sem=recv.at[src], device_id=pos.dev(a, q, 1 - c),
                                     device_id_type=MESH).wait_recv()

    def exchange(t):
        return pltpu.make_async_remote_copy(src_ref=outg.at[t], dst_ref=inc.at[me], send_sem=a_send.at[t],
                                            recv_sem=a_recv.at[me], device_id=(t // 2, t % 2), device_id_type=MESH)

    pl.when(a + 1 < line)(lambda: up(a, True).start())
    pl.when(a > 0)(lambda: down(a, True).start())
    to_x(a, True).start()
    to_y(a, True).start()
    sibling(a, q, True).start()

    hot = slot_onehot(sel_ref[...], node.shape[0])
    node_copy.wait()
    picked = jnp.dot(hot, node[...], preferred_element_type=F32)
    outg[:, 0:slots, :] = picked[:, 0:D // 2].reshape(peers, slots, D // 2).astype(BF)
    outg[:, slots:, :] = picked[:, D // 2:].reshape(peers, slots, D // 2).astype(BF)
    msg_copy = pltpu.make_async_copy(outg.at[me], inc.at[me], own_sem.at[2])
    msg_copy.start()

    def along(ak, below):
        arrive(ak, q)
        if below:
            pl.when(a + 1 < line)(lambda: up(ak).start())
        else:
            pl.when(a > 0)(lambda: down(ak).start())
        to_x(ak).start()
        to_y(ak).start()
        sibling(ak, q).start()

    def square(ak):
        arrive(ak, pos.qx)
        x_to_y(ak).start()
        sibling(ak, pos.qx).start()
        arrive(ak, pos.qy)
        y_to_x(ak).start()
        sibling(ak, pos.qy).start()

    def both(k, what):
        pl.when(a - k >= 0)(lambda: what(a - k, True))
        pl.when(a + k < line)(lambda: what(a + k, False))

    for k in range(1, line):
        both(k, along)
        if k == 1:
            square(a)
        else:
            both(k - 1, lambda ak, below: square(ak))
    both(line - 1, lambda ak, below: square(ak))

    @pl.loop(1, pos.devices)
    def _(k):
        exchange((me + k) % pos.devices).start()

    for k in range(line):
        ak = pos.other_a(k)
        for part, at in ((FIRST, 0), (LAST, 1)):
            ref = buf.at[pos.idx(ak, pos.qd, c), part]
            pltpu.make_async_remote_copy(src_ref=ref, dst_ref=ref, send_sem=send_s.at[0], recv_sem=half.at[at, ak],
                                         device_id=pos.dev(a, q, 1 - c), device_id_type=MESH).wait_recv()
        sibling(ak, pos.qd).start()

    @pl.loop(1, pos.devices)
    def _(k):
        t = (me + k) % pos.devices
        pltpu.make_async_remote_copy(src_ref=outg.at[t], dst_ref=inc.at[t], send_sem=a_send.at[t],
                                     recv_sem=a_recv.at[t], device_id=(t // 2, t % 2), device_id_type=MESH).wait()

    own_copy.wait()
    msg_copy.wait()
    for k in range(line):
        ak = pos.other_a(k)
        pl.when((a + 1 < line) & (ak <= a))(lambda: up(ak).wait_send())
        pl.when((a > 0) & (ak >= a))(lambda: down(ak).wait_send())
        for cp in (to_x(ak), to_y(ak), x_to_y(ak), y_to_x(ak)):
            cp.wait_send()
        for qk in (q, pos.qx, pos.qy, pos.qd):
            sibling(ak, qk).wait_send()
            arrive(ak, qk, 1 - c)


def gather_weights(bands, w1, w2, nw1, nw2, sel, node, *vecs):
    parts = tuple(m.shape[0] for m in (w1, w2, nw1, nw2))
    rows = layout(parts)[1] + 16
    n, line = bands * 2, bands // LINE
    D = node.shape[1]
    slots, peers = sel.shape
    H = pl.BlockSpec(memory_space=pl.ANY)
    inputs = (w1, w2, nw1, nw2, sel, *vecs)
    sds, sem, vm = jax.ShapeDtypeStruct, pltpu.SemaphoreType.DMA, pltpu.VMEM
    msgs = (peers, 2 * slots, D // 2)
    return pl.pallas_call(
        functools.partial(gather_kernel, bands, parts),
        out_shape=[sds((n, rows, 128), BF), sds(msgs, BF)],
        in_specs=[H] * 12, out_specs=[H, H],
        scratch_shapes=[
            vm((rows, 128), BF), vm(node.shape, BF), vm((16, 128), F32), vm(msgs, BF),
            sem((n,)), sem((2, line)), sem((2, line)), sem((2, line)), sem((2, line)), sem((bands,)),
            sem((n,)), sem((n,)), sem((3,)), sem((11,)), *[vm(m.shape, m.dtype) for m in inputs]],
        compiler_params=pltpu.CompilerParams(collective_id=0, has_side_effects=True, vmem_limit_bytes=63 * 2**20),
        name="gather_weights",
    )(*inputs, node)


def reduce_kernel(bands, p_ref, msg_ref, red_ref, arr_ref, own, sib, xa, yb, ya, xb, zin,
                  own_sem, sib_recv, x1, y1, y2, x2, z_recv, send, a_recv, a_send, kept_sem):
    pos = Place(bands)
    me, c, a, q = pos.me, pos.c, pos.a, pos.q
    rows = own.shape[1]
    cut = up16(rows // 2)
    A, B = pl.ds(0, cut), pl.ds(cut, rows - cut)
    count = [0]
    started = []

    def push(src, dst, sem, target):
        cp = pltpu.make_async_remote_copy(src_ref=src, dst_ref=dst, send_sem=send.at[count[0]], recv_sem=sem,
                                          device_id=target, device_id_type=MESH)
        count[0] += 1
        cp.start()
        started.append(cp)

    def wait(dst, sem):
        pltpu.make_async_remote_copy(src_ref=dst, dst_ref=dst, send_sem=send.at[0], recv_sem=sem,
                                     device_id=pos.dev(a, q, 1 - c), device_id_type=MESH).wait_recv()

    order = [pos.other_a(k) for k in range(1, pos.quads)] + [a]
    square = [pl.ds(ak * LINE, LINE) for ak in order]
    met_all = greet_all(pos)
    kept = pltpu.make_async_copy(msg_ref.at[me], arr_ref.at[me], kept_sem)
    mine = []
    for ak, sq in zip(order, square):
        cp = pltpu.make_async_copy(p_ref.at[c, sq], own.at[sq], own_sem.at[ak])
        cp.start()
        mine.append(cp)
    kept.start()
    met_all()
    for ak, sq in zip(order, square):
        push(p_ref.at[1 - c, sq], sib.at[sq], sib_recv.at[ak], pos.dev(a, q, 1 - c))

    def exchange(t):
        return pltpu.make_async_remote_copy(src_ref=msg_ref.at[t], dst_ref=arr_ref.at[me], send_sem=a_send.at[t],
                                            recv_sem=a_recv.at[me], device_id=(t // 2, t % 2), device_id_type=MESH)

    @pl.loop(1, pos.devices)
    def _(k):
        exchange((me + k) % pos.devices).start()

    to_x, to_y = pos.dev(a, pos.qx, c), pos.dev(a, pos.qy, c)

    def add(ref, idx, other):
        ref[idx] = (ref[idx].astype(F32) + other.astype(F32)).astype(BF)

    def first(k):
        ak, sq = order[k], square[k]
        at = ak * LINE
        mine[k].wait()
        wait(sib.at[sq], sib_recv.at[ak])
        own[sq] = (own[sq].astype(F32) + sib[sq].astype(F32)).astype(BF)
        push(own.at[at + pos.qx, A], xa.at[ak, 0], x1.at[ak, 0], to_x)
        push(own.at[at + pos.qy, B], yb.at[ak, 0], y1.at[ak, 0], to_y)
        push(own.at[at + pos.qd, A], xa.at[ak, 1], x1.at[ak, 1], to_x)
        push(own.at[at + pos.qd, B], yb.at[ak, 1], y1.at[ak, 1], to_y)

    def second(k):
        ak = order[k]
        at = ak * LINE
        wait(xa.at[ak, 1], x1.at[ak, 1])
        add(own, (at + pos.qy, A), xa[ak, 1])
        push(own.at[at + pos.qy, A], ya.at[ak], y2.at[ak], to_y)
        wait(yb.at[ak, 1], y1.at[ak, 1])
        add(own, (at + pos.qx, B), yb[ak, 1])
        push(own.at[at + pos.qx, B], xb.at[ak], x2.at[ak], to_x)

    def third(k):
        ak = order[k]
        at = ak * LINE
        wait(xa.at[ak, 0], x1.at[ak, 0])
        wait(yb.at[ak, 0], y1.at[ak, 0])
        wait(ya.at[ak], y2.at[ak])
        wait(xb.at[ak], x2.at[ak])
        top = own[at + q, A].astype(F32) + xa[ak, 0].astype(F32) + ya[ak].astype(F32)
        low = own[at + q, B].astype(F32) + yb[ak, 0].astype(F32) + xb[ak].astype(F32)
        if k < pos.quads - 1:
            own[at + q, A] = top.astype(BF)
            own[at + q, B] = low.astype(BF)
            push(own.at[at + q], zin.at[a], z_recv.at[a], pos.dev(ak, q, c))
        else:
            red_ref[A, :] = top
            red_ref[B, :] = low

    n = pos.quads
    first(0)
    if n > 1:
        first(1)
    for k in range(n):
        second(k)
        if k + 2 < n:
            first(k + 2)
        if k >= 1:
            third(k - 1)
    third(n - 1)
    for k in range(n - 1):
        ak = order[k]
        wait(zin.at[ak], z_recv.at[ak])
        red_ref[...] += zin[ak].astype(F32)

    @pl.loop(1, pos.devices)
    def _(k):
        t = (me + k) % pos.devices
        pltpu.make_async_remote_copy(src_ref=msg_ref.at[t], dst_ref=arr_ref.at[t], send_sem=a_send.at[t],
                                     recv_sem=a_recv.at[t], device_id=(t // 2, t % 2), device_id_type=MESH).wait()

    kept.wait()
    for cp in started:
        cp.wait_send()


def reduce_grads(bands, packed, msgs):
    rows = packed.shape[2]
    n = bands * 2
    quads = bands // LINE
    cut = up16(rows // 2)
    V = pl.BlockSpec(memory_space=pltpu.VMEM)
    sds = jax.ShapeDtypeStruct
    sem = pltpu.SemaphoreType.DMA
    return pl.pallas_call(
        functools.partial(reduce_kernel, bands),
        out_shape=[sds((rows, 128), F32), sds(msgs.shape, BF)],
        in_specs=[pl.BlockSpec(memory_space=pl.ANY)] * 2, out_specs=[V, V],
        scratch_shapes=[
            pltpu.VMEM((bands, rows, 128), BF), pltpu.VMEM((bands, rows, 128), BF),
            pltpu.VMEM((quads, 2, cut, 128), BF), pltpu.VMEM((quads, 2, rows - cut, 128), BF),
            pltpu.VMEM((quads, cut, 128), BF), pltpu.VMEM((quads, rows - cut, 128), BF),
            pltpu.VMEM((quads, rows, 128), BF),
            sem((quads,)), sem((quads,)), sem((quads, 2)), sem((quads, 2)), sem((quads,)), sem((quads,)), sem((quads,)),
            sem((8 * quads,)), sem((n,)), sem((n,)), sem],
        compiler_params=pltpu.CompilerParams(collective_id=1, has_side_effects=True, vmem_limit_bytes=63 * 2**20),
        name="reduce_grads",
    )(packed, msgs)


def finish_kernel(bands, parts, red_ref, arr_ref, sel_ref, part_ref, ngrad_ref, w1_ref, w2_ref, nw1_ref, nw2_ref, *vecs):
    me = lax.axis_index("band") * 2 + lax.axis_index("sub")
    spots, tail = layout(parts)
    for o_ref, p, o in zip((w1_ref, w2_ref, nw1_ref, nw2_ref), parts, spots):
        for j in range(4):
            o_ref[:, 128 * j:128 * j + 128] = red_ref[o + j * up16(p):o + j * up16(p) + p, :]
    width = vecs[0].shape[0]
    group = 128 // width
    slab = red_ref[tail:tail + 8, :]
    got = slab[:, 0:width]
    for g in range(1, group):
        got = jnp.where(me % group == g, slab[:, g * width:(g + 1) * width], got)
    for k, v_ref in enumerate(vecs):
        v_ref[...] = got[k]
    slots, peers = sel_ref.shape
    S = peers * slots
    N, D = part_ref.shape
    hot = slot_onehot(sel_ref[...], N)
    arrived = jnp.concatenate([arr_ref[:, 0:slots, :].astype(F32).reshape(S, D // 2),
                               arr_ref[:, slots:, :].astype(F32).reshape(S, D // 2)], axis=1).astype(BF)
    ngrad_ref[...] = part_ref[...] + lax.dot_general(hot, arrived, (((0,), (0,)), ((), ())), preferred_element_type=F32)


def slot_onehot(ids, nodes):
    slots, peers = ids.shape
    S = peers * slots
    pick = (lax.broadcasted_iota(jnp.int32, (S, peers), 0) // slots
            == lax.broadcasted_iota(jnp.int32, (S, peers), 1)).astype(BF)
    low = dot_t(pick, (ids % 256).astype(BF))
    high = dot_t(pick, (ids // 256).astype(BF))
    mine = lax.broadcasted_iota(jnp.int32, (S, slots), 0) % slots == lax.broadcasted_iota(jnp.int32, (S, slots), 1)
    col = jnp.sum(jnp.where(mine, low + 256.0 * high, 0.0), axis=1, keepdims=True)
    return (col == lax.broadcasted_iota(jnp.int32, (S, nodes), 1).astype(F32)).astype(BF)


def finish(bands, parts, width, red, arrived, sel, part):
    V = pl.BlockSpec(memory_space=pltpu.VMEM)
    sds = jax.ShapeDtypeStruct
    D = part.shape[1]
    outs = [sds(part.shape, F32)] + [sds((p, D), F32) for p in parts] + [sds((width,), F32)] * 6
    return pl.pallas_call(
        functools.partial(finish_kernel, bands, parts),
        out_shape=outs, in_specs=[V] * 4, out_specs=[V] * len(outs),
        compiler_params=pltpu.CompilerParams(vmem_limit_bytes=63 * 2**20),
        name="finish",
    )(red, arrived, sel, part)


EPS = 1e-5


def dot(a, b):
    return jnp.dot(a, b, preferred_element_type=F32)


def dot_t(a, b):
    return lax.dot_general(a, b, (((1,), (1,)), ((), ())), preferred_element_type=F32)


def t_dot(a, b):
    return lax.dot_general(a, b, (((0,), (0,)), ((), ())), preferred_element_type=F32)


def rowmean(v):
    return jnp.sum(v, axis=1, keepdims=True) * (1.0 / v.shape[1])


def onehot_cols(ids, width):
    rows = ids.shape[1]
    wide = jnp.broadcast_to(ids, (128, rows)).T
    off = wide - lax.broadcasted_iota(jnp.int32, (rows, 128), 1)
    return jnp.concatenate([jnp.where(off == 128 * j, 1.0, 0.0).astype(BF) for j in range(width // 128)], axis=1)


def onehot_rows(ids, height):
    return jnp.where(lax.broadcasted_iota(jnp.int32, (height, ids.shape[1]), 0) == ids, 1.0, 0.0).astype(BF)


def fold8(v):
    return jnp.sum(v.reshape(v.shape[0] // 8, 8, v.shape[1]), axis=0)


def core_kernel(nb, R, sub, parts, fast, count_ref, sid_ref, rid_ref, e_ref, cot_ref, node_ref, ncot_ref, *refs):
    (got_ref, inc_ref), refs = (refs[:2], refs[2:]) if fast else ((None, None), refs)
    weights, refs = ((), refs) if fast else (refs[:6], refs[6:])
    nout_ref, eout_ref, ngrad_ref, egrad_ref, msg_ref, *refs = refs
    outs, refs = (refs[:1], refs[1:]) if fast else (refs[:5], refs[5:])
    if fast:
        pack_ref, stage, refs = outs[0], refs[0], refs[1:]
        outs = [stage]
    weights, refs = (refs[:6], refs[6:]) if fast else (weights, refs)
    w1_ref, w2_ref, nw1_ref, nw2_ref, vec_ref, snd_ref = weights
    wcat, w2h, hid_s, slope_s, nrm_s, scale_s, gath, dg, gacc, g2acc, gain_acc, shift_acc, gvec, msg_s, dpre_s, w1t, sem = refs
    i = pl.program_id(0)
    D = e_ref.shape[1]
    S = snd_ref.shape[0]
    N = node_ref.shape[0]
    count = count_ref[0]
    spots, tail = layout(parts)
    n = 3 * D // parts[0]

    def emit(m, first, value):
        if not fast:
            outs[m][first:first + value.shape[0], :] = value
            return
        p, o = parts[m], spots[m]
        lo, hi = first, first + value.shape[0]
        for d in range(lo // p, -(-hi // p)):
            a, b = max(lo, d * p), min(hi, (d + 1) * p)
            for j in range(D // 128):
                at = o + j * p + a - d * p
                outs[0][d % 2, d // 2, at:at + b - a, :] = value[a - lo:b - lo, 128 * j:128 * j + 128].astype(BF)

    RANGES = (pl.ds(0, spots[2]), pl.ds(spots[2], tail - spots[2]), pl.ds(tail, 16))

    def fetch(k):
        return pltpu.make_async_copy(got_ref.at[:, :, RANGES[k]], stage.at[:, :, RANGES[k]], sem.at[k])

    def deliver(k):
        return pltpu.make_async_copy(stage.at[:, :, RANGES[k]], pack_ref.at[:, :, RANGES[k]], sem.at[k])

    def unpack(mats):
        @pl.loop(0, n)
        def _(d):
            for w_ref, p, o in mats:
                for j in range(D // 128):
                    w_ref[pl.ds(pl.multiple_of(d * p, p), p), 128 * j:128 * j + 128] = \
                        stage[d // (n // 2), d % (n // 2), o + j * p:o + j * p + p, :]

    def unpack_vectors():
        group = n // (D // 128)
        for g in range(D // 128):
            tiles = [stage[d // (n // 2), d % (n // 2), tail:tail + 16, :].astype(F32)
                     for d in range(g * group, (g + 1) * group)]
            vec_ref[:, 128 * g:128 * g + 128] = functools.reduce(jnp.add, tiles).astype(BF)
        slots = inc_ref.shape[1] // 2
        snd_ref[:, 0:D // 2] = inc_ref[:, 0:slots, :].astype(F32).reshape(S, D // 2).astype(BF)
        snd_ref[:, D // 2:] = inc_ref[:, slots:, :].astype(F32).reshape(S, D // 2).astype(BF)

    @pl.when(i == 0)
    def _():
        if fast:
            for k in range(3):
                fetch(k).start()
            fetch(0).wait()
            unpack(list(zip((w1_ref, w2_ref), parts, spots))[:2])
            fetch(2).wait()
            unpack_vectors()
        b1 = vec_ref[0:1, :].astype(F32)
        wcat[0:D, :] = w1_ref[0:D, :] * 0.5
        wcat[D:D + S, :] = (dot(snd_ref[...], w1_ref[D:2 * D, :]) * 0.5).astype(BF)
        wcat[D + S:, :] = ((dot(node_ref[...], w1_ref[2 * D:, :]) + b1) * 0.5).astype(BF)
        w2h[...] = (w2_ref[...].astype(F32) * 0.5).T.astype(BF)
        w1t[...] = w1_ref[0:D, :].astype(F32).T.astype(BF)
        gath[...] = jnp.zeros_like(gath)
        gacc[...] = jnp.zeros_like(gacc)
        g2acc[...] = jnp.zeros_like(g2acc)
        gain_acc[...] = jnp.zeros_like(gain_acc)
        shift_acc[...] = jnp.zeros_like(shift_acc)
        scale_s[...] = jnp.zeros_like(scale_s)

    gain = vec_ref[1:2, :].astype(F32)
    shift = vec_ref[2:3, :].astype(F32)
    blk = lax.rem(i, nb)
    live_blk = blk * R < count
    subs = R // sub

    def ids(r):
        at = blk * subs + r
        pos = at * sub + lax.broadcasted_iota(jnp.int32, (1, sub), 1)
        sid = sid_ref[pl.ds(at, 1), :]
        rid = jnp.where(pos < count, rid_ref[pl.ds(at, 1), :], -1)
        return sid, rid

    def live_col(r):
        return (blk * subs + r) * sub + lax.broadcasted_iota(jnp.int32, (sub, 1), 0) < count

    def lane_is(at):
        return lax.broadcasted_iota(jnp.int32, (sub, 128), 1) == at

    @pl.when((i < nb) & live_blk)
    def _():
        here = [slice(r * sub, (r + 1) * sub) for r in range(subs)]
        rows = [pl.ds(pl.multiple_of((blk * subs + r) * sub, sub), sub) for r in range(subs)]
        idx = [ids(r) for r in range(subs)]
        h, proj = [None] * subs, [None] * subs

        def a1(r):
            sid, rid = idx[r]
            x = jnp.concatenate([e_ref[here[r], :], onehot_cols(sid, S), onehot_cols(rid, N)], axis=1)
            h[r] = dot(x, wcat[...])

        def a2(r):
            v = h[r]
            a = 1.0 + jnp.tanh(v)
            hid = v * a
            slope_s[rows[r], :] = (a + hid * (2.0 - a)).astype(BF)
            hid_s[rows[r], :] = hid.astype(BF)

        def b1(r):
            proj[r] = dot(hid_s[rows[r], :], w2_ref[...])

        def b2(r):
            live = live_col(r)
            c = proj[r] - rowmean(proj[r])
            s = lax.rsqrt(rowmean(c * c) + EPS)
            s = jnp.where(live, s, 0.0)
            scale_s[...] = jnp.where(lane_is(blk * subs + r), s, scale_s[...])
            nrm = c * s
            nrm_s[rows[r], :] = nrm.astype(BF)
            msg = nrm * gain + shift
            eout_ref[here[r], :] = (e_ref[here[r], :].astype(F32) + msg).astype(BF)
            msg_s[here[r], :] = msg.astype(BF)

        def c1(first, last):
            rid = jnp.concatenate([idx[r][1] for r in range(first, last)], axis=1)
            gath[...] += dot(onehot_rows(rid, N), msg_s[first * sub:last * sub, :])

        for t in range(subs + 2):
            if t < subs:
                a1(t)
            if 2 <= t:
                b2(t - 2)
            if 1 <= t < subs + 1:
                b1(t - 1)
            if t < subs:
                a2(t)
        c1(0, subs)

    @pl.when((i < nb) & live_blk & ((blk + 1) * R > count))
    def _():
        live = blk * R + lax.broadcasted_iota(jnp.int32, (R, 1), 0) < count
        eout_ref[...] = jnp.where(live, eout_ref[...].astype(F32), e_ref[...].astype(F32)).astype(BF)

    @pl.when((i < nb) & jnp.logical_not(live_blk))
    def _():
        eout_ref[...] = e_ref[...]

    @pl.when(i == nb - 1)
    def _():
        if fast:
            fetch(1).wait()
            unpack(list(zip((nw1_ref, nw2_ref), parts[2:], spots[2:])))
        nb1 = vec_ref[3:4, :].astype(F32)
        ngain = vec_ref[4:5, :].astype(F32)
        nshift = vec_ref[5:6, :].astype(F32)
        node = node_ref[...]
        g16 = gath[...].astype(BF)
        pre = dot(node, nw1_ref[0:D, :]) + dot(g16, nw1_ref[D:, :]) + nb1
        sig = 0.5 + 0.5 * jnp.tanh(0.5 * pre)
        hid = (pre * sig).astype(BF)
        proj = dot(hid, nw2_ref[...])
        c = proj - rowmean(proj)
        s = lax.rsqrt(rowmean(c * c) + EPS)
        nrm = c * s
        nout_ref[...] = (node.astype(F32) + nrm * ngain + nshift).astype(BF)
        up = ncot_ref[...].astype(F32)
        gvec[4:5, :] = jnp.sum(up * nrm, axis=0, keepdims=True)
        gvec[5:6, :] = jnp.sum(up, axis=0, keepdims=True)
        g = up * ngain
        dproj = (s * (g - rowmean(g) - nrm * rowmean(g * nrm))).astype(BF)
        emit(3, 0, t_dot(hid, dproj))
        dpre = dot_t(dproj, nw2_ref[...]) * (sig * (1.0 + pre * (1.0 - sig)))
        dpre16 = dpre.astype(BF)
        emit(2, 0, t_dot(node, dpre16))
        emit(2, D, t_dot(g16, dpre16))
        gvec[3:4, :] = jnp.sum(dpre16.astype(F32), axis=0, keepdims=True)
        ngrad_ref[...] = up + dot_t(dpre16, nw1_ref[0:D, :])
        dg[...] = dot_t(dpre16, nw1_ref[D:, :]).astype(BF)
        if fast:
            deliver(1).start()

    @pl.when((i >= nb) & live_blk)
    def _():
        here = [slice(r * sub, (r + 1) * sub) for r in range(subs)]
        rows = [pl.ds(pl.multiple_of((blk * subs + r) * sub, sub), sub) for r in range(subs)]
        every = pl.ds(pl.multiple_of(blk * R, R), R)
        idx = [ids(r) for r in range(subs)]
        came, dhid, back = [None] * subs, [None] * subs, [None] * subs

        def a1(r):
            came[r] = dot(onehot_cols(idx[r][1], N), dg[...])

        def a2(r):
            dm = jnp.where(live_col(r), cot_ref[here[r], :].astype(F32), 0.0) + came[r]
            nrm = nrm_s[rows[r], :].astype(F32)
            p = dm * nrm
            gain_acc[...] += fold8(p)
            shift_acc[...] += fold8(dm)
            g = dm * gain
            m1 = rowmean(g)
            m2 = rowmean(p * gain)
            s = jnp.sum(jnp.where(lane_is(blk * subs + r), scale_s[...], 0.0), axis=1, keepdims=True)
            msg_s[here[r], :] = (s * (g - m1 - nrm * m2)).astype(BF)

        def b1(r):
            dhid[r] = dot(msg_s[here[r], :], w2h[...])

        def b2(r):
            dpre_s[here[r], :] = (dhid[r] * slope_s[rows[r], :].astype(F32)).astype(BF)

        def c1(r):
            back[r] = dot(dpre_s[here[r], :], w1t[...])

        def c2(r):
            egrad_ref[here[r], :] = cot_ref[here[r], :].astype(F32) + back[r]

        for t in range(subs + 3):
            if t < subs:
                a1(t)
            if t >= 3:
                c2(t - 3)
            if 2 <= t < subs + 2:
                b2(t - 2)
            if 1 <= t < subs + 1:
                b1(t - 1)
            if t < subs:
                a2(t)
            if 2 <= t < subs + 2:
                c1(t - 2)
            if t == subs:
                g2acc[...] += t_dot(hid_s[every, :], msg_s[...])
        sids = jnp.concatenate([v[0] for v in idx], axis=1)
        rids = jnp.concatenate([v[1] for v in idx], axis=1)
        gacc[0:D, :] += t_dot(e_ref[...], dpre_s[...])
        gacc[D:D + S, :] += dot(onehot_rows(sids, S), dpre_s[...])
        gacc[D + S:, :] += dot(onehot_rows(rids, N), dpre_s[...])

    @pl.when((i >= nb) & jnp.logical_not(live_blk))
    def _():
        egrad_ref[...] = cot_ref[...].astype(F32)

    @pl.when(i == 2 * nb - 1)
    def _():
        us = gacc[D:D + S, :].astype(BF)
        ur = gacc[D + S:, :].astype(BF)
        emit(0, 0, gacc[0:D, :])
        emit(0, D, t_dot(snd_ref[...], us))
        emit(0, 2 * D, t_dot(node_ref[...], ur))
        emit(1, 0, g2acc[...])
        ngrad_ref[...] += dot_t(ur, w1_ref[2 * D:, :])
        sgrad = dot_t(us, w1_ref[D:2 * D, :])
        peers, slots = msg_ref.shape[0], msg_ref.shape[1] // 2
        msg_ref[:, 0:slots, :] = sgrad[:, 0:D // 2].reshape(peers, slots, D // 2).astype(BF)
        msg_ref[:, slots:, :] = sgrad[:, D // 2:].reshape(peers, slots, D // 2).astype(BF)
        gvec[0:1, :] = jnp.sum(gacc[D + S:, :], axis=0, keepdims=True)
        gvec[1:2, :] = jnp.sum(gain_acc[...], axis=0, keepdims=True)
        gvec[2:3, :] = jnp.sum(shift_acc[...], axis=0, keepdims=True)
        gvec[6:8, :] = jnp.zeros((2, D), F32)
        if not fast:
            outs[4][...] = gvec[...]
        else:
            for d in range(n):
                g = d * D // n // 128
                stage[d % 2, d // 2, tail:tail + 16, :] = jnp.concatenate(
                    [gvec[:, 128 * g:128 * g + 128]] * 2, axis=0).astype(BF)
            deliver(0).start()
            deliver(2).start()
            for k in range(3):
                deliver(k).wait()


def core(bands, parts, count, sid, rid, e, cot, node, ncot, got, inc, sub=128):
    E, D = e.shape
    S, N = inc.shape[0] * inc.shape[1] // 2, node.shape[0]
    R = 1024 if S <= 256 else 512
    nb = E // R
    V, H = pl.BlockSpec(memory_space=pltpu.VMEM), pl.BlockSpec(memory_space=pl.ANY)
    fb = pl.BlockSpec((R, D), lambda i: (jnp.minimum(i, nb - 1), 0))
    bb = pl.BlockSpec((R, D), lambda i: (jnp.maximum(i - nb, 0), 0))
    both = pl.BlockSpec((R, D), lambda i: (lax.rem(i, nb), 0))
    sds, vm = jax.ShapeDtypeStruct, pltpu.VMEM
    fast = all(p % 16 == 0 for p in parts)
    rows = layout(parts)[1] + 16
    if fast:
        weights, specs = (got.reshape(2, bands, rows, 128), inc), [H, V]
    else:
        weights, specs = unpack_weights(bands, parts, got, inc), [V] * 6
    grads = [(3 * D, D), (D, D), (2 * D, D), (D, D), (8, D)]
    outs = [sds((N, D), BF), sds((E, D), BF), sds((N, D), F32), sds((E, D), F32), sds(inc.shape, BF)]
    outs += [sds((2, bands, rows, 128), BF)] if fast else [sds(g, F32) for g in grads]
    *res, packed = res = pl.pallas_call(
        functools.partial(core_kernel, nb, R, sub, parts, fast),
        grid=(2 * nb,),
        in_specs=[pl.BlockSpec(memory_space=pltpu.SMEM), V, V, both, bb, V, V] + specs,
        out_specs=[V, fb, V, bb, V] + ([H] if fast else [V] * 5),
        out_shape=outs,
        scratch_shapes=([vm((2, bands, rows, 128), BF)] + [vm(g, BF) for g in grads[:4]] + [vm((16, D), BF), vm((S, D), BF)] if fast else []) + [
            vm((D + S + N, D), BF), vm((D, D), BF), vm((E, D), BF), vm((E, D), BF), vm((E, D), BF),
            vm((sub, 128), F32), vm((N, D), F32), vm((N, D), BF), vm((D + S + N, D), F32), vm((D, D), F32),
            vm((8, D), F32), vm((8, D), F32), vm((8, D), F32), vm((R, D), BF), vm((R, D), BF), vm((D, D), BF),
            pltpu.SemaphoreType.DMA((3,))],
        compiler_params=pltpu.CompilerParams(vmem_limit_bytes=63 * 2**20, dimension_semantics=("arbitrary",)),
        name="edge_node_core",
    )(count, sid.reshape(E // sub, sub), rid.reshape(E // sub, sub), e, cot, node, ncot, *weights)
    if not fast:
        packed = pack_grads(bands, parts, res[5:])
    return (*res[:4], packed, res[4])


def unpack_weights(bands, parts, got, inc):
    spots, tail = layout(parts)
    n, slots, D = 2 * bands, inc.shape[1] // 2, 2 * inc.shape[2]
    mats = []
    for p, o in zip(parts, spots):
        cols = [got[:, o + j * up16(p):o + j * up16(p) + p, :].reshape(n * p, 128) for j in range(D // 128)]
        mats.append(jnp.concatenate(cols, axis=1))
    slabs = got[:, tail:tail + 16, :].reshape(D // 128, -1, 16, 128).sum(axis=1)
    vec = slabs.transpose(1, 0, 2).reshape(16, D)
    snd = jnp.concatenate([inc[:, :slots].reshape(n * slots, D // 2), inc[:, slots:].reshape(n * slots, D // 2)], axis=1)
    return (*mats, vec, snd)


def pack_grads(bands, parts, grads):
    *mats, vec = [g.astype(BF) for g in grads]
    n, D = 2 * bands, vec.shape[1]
    blocks = []
    for m, p in zip(mats, parts):
        for j in range(D // 128):
            block = m[:, 128 * j:128 * j + 128].reshape(n, p, 128)
            blocks.append(jnp.pad(block, ((0, 0), (0, up16(p) - p), (0, 0))))
    slabs = jnp.repeat(vec.reshape(8, D // 128, 128).transpose(1, 0, 2), n // (D // 128), axis=0)
    full = jnp.concatenate(blocks + [slabs, slabs], axis=1)
    return full.reshape(bands, 2, full.shape[1], 128).transpose(1, 0, 2, 3)


def local(bands, node_state, edge_state, send_rows, edge_sender, edge_receiver, edge_count, edge_w1, edge_b1, edge_w2,
          edge_gain, edge_shift, node_w1, node_b1, node_w2, node_gain, node_shift, node_cot, edge_cot):
    parts = tuple(m.shape[0] for m in (edge_w1, edge_w2, node_w1, node_w2))
    width = edge_b1.shape[0]
    vecs = (edge_b1, edge_gain, edge_shift, node_b1, node_gain, node_shift)
    sel = send_rows[0].T
    got, inc = gather_weights(bands, edge_w1, edge_w2, node_w1, node_w2, sel, node_state, *vecs)
    node_out, edge_out, node_part, edge_grad, packed, msgs = core(
        bands, parts, edge_count, edge_sender, edge_receiver, edge_state, edge_cot, node_state, node_cot, got, inc)
    red, arrived = reduce_grads(bands, packed, msgs)
    node_grad, gw1, gw2, gnw1, gnw2, *gv = finish(bands, parts, width, red, arrived, sel, node_part)
    return (node_out, edge_out, node_grad, edge_grad, gw1, gv[0], gw2, gv[1], gv[2], gnw1, gv[3], gnw2, gv[4], gv[5])


def solution(mesh):
    two, one, three = P(AXES, None), P(AXES), P(AXES, None, None)
    in_specs = (two, two, three, one, one, one, two, one, two, one, one, two, one, two, one, one, two, two)
    out_specs = (two, two, two, two, two, one, two, one, one, two, one, two, one, one)
    return jax.shard_map(functools.partial(local, mesh.shape["band"]), mesh=mesh, in_specs=in_specs,
                         out_specs=out_specs, check_vma=False)
```
